32 devices in a mesh: dam: 16 (over z, y, x), sec: 2 (over core).
Axes of the slice: x: 2, y: 2, z: 4, core: 2. Of those that a mesh axis runs over, the one named last changes fastest.
Arguments:
- segment_load: float32 [16, 2, 16, 1024], P('dam', 'sec')
- segment_mask: int32 [16, 2, 16, 16], P('dam', 'sec'), may hold values 0 or 1
- stiffness: float32 [16, 2, 16, 64, 448], P('dam', 'sec'), may hold values from -2 to 3, as said below
- block_cols: int32 [16, 2, 16, 7], P('dam', 'sec'), may hold values from 0 to 15, as said below
- capillary: float32 [16, 2, 16, 64], P('dam', 'sec'), may hold values from 0.25 to 2
- dirichlet_blocks: float32 [16, 2, 16, 64, 64], P('dam', 'sec'), may hold values from -1 to 1, as said below
- face_map: int32 [16, 2, 4, 8], P('dam', 'sec'), may hold values from 0 to 15, as said below
- face_weight: float32 [16, 2, 4, 512], P('dam', 'sec'), may hold values from 0 to 2, as said below
- corner_map: int32 [16, 2, 4], P('dam', 'sec'), may hold values from 0 to 15, as said below
- coarse_inverse: float32 [16, 512, 512], P('dam', 'sec'), may hold values from -1 to 1, as said below
Outputs:
- solution: float32 [16, 2, 16, 1024], P('dam', 'sec')
- residual: float32 [16, 2, 16, 1024], P('dam', 'sec')
The draws below stay inside these ranges and needn't reach their ends.
Inputs may be any that keep to these rules, and one draw needn't show every extreme that they name: `block_cols`: in each subdomain block b stores blocks b, b + o1, b - o1, b + o2, b - o2, b + o3, b - o3 (mod 16), for 3 distinct offsets o1, o2, o3 from 1 to 7 drawn per subdomain, in that order. The stiffness is symmetric, its off-diagonal entries of a row sum in magnitude to under 1.5, and its diagonal entries are 2 to 3. `dirichlet_blocks`: each block is symmetric and positive definite. `coarse_inverse`: each cross-section's matrix is symmetric and positive definite. `face_map`: the 8 blocks of a face are distinct; position p of a face meets position p of the neighbour's opposite face. `face_weight`: equal on the two sides of an interface, zero on faces with no neighbour. `corner_map`: distinct within a subdomain.
All inputs are finite; a program needn't handle non-finite values. No bound on the sum of `segment_mask` on one device may be relied on, other than what follows from the above.
Results may differ from the reference program's by a relative error of at most 0.00075.
Values sent between devices are 32-bit elements; how exact they have to be, the bound alone decides.
No kernel may reach another device: no remote copies, remote signals or barrier semaphores. Data moves between devices by JAX's collectives and lax.ppermute only.
A program may use at most 64 MiB of HBM per device.

```python
import math
import jax
import jax.numpy as jnp
from jax import lax

NB = 16
BD = 64
RHS = 16
KB = 7
NC = 4
ITERS = 2
FB = 8
SD = 16
SS = 2
CO = 512


def draw_segment_load(key, part):
    first = jax.random.fold_in(key, 0)
    shape = (SD, SS, NB, BD * RHS)
    scale = (3.0 ** (jnp.arange(SD).astype(jnp.float32) / (SD - 1))).reshape(SD, 1, 1, 1)
    return jax.random.normal(first, shape, jnp.float32) * scale


def stiff_offsets(key):
    keys = jax.random.split(jax.random.fold_in(key, 17), SD * SS)
    half = (KB - 1) // 2

    def single(subkey):
        return (1 + jax.random.permutation(subkey, NB // 2 - 1)[:half]).astype(jnp.int32)
    return jax.vmap(single)(keys).reshape(SD, SS, half)


def draw_block_cols(key, part):
    offsets = stiff_offsets(key)
    half = (KB - 1) // 2
    base = jnp.arange(NB).astype(jnp.int32)
    plus = (base[None, None, :, None] + offsets[:, :, None, :]) % NB
    minus = (base[None, None, :, None] - offsets[:, :, None, :] + NB) % NB
    paired = jnp.stack([plus, minus], axis=-1).reshape(SD, SS, NB, 2 * half)
    own = jnp.broadcast_to(base[None, None, :, None], (SD, SS, NB, 1))
    return jnp.concatenate([own, paired], axis=-1).astype(jnp.int32)


def draw_stiffness(key, part):
    offsets = stiff_offsets(key)
    half = (KB - 1) // 2
    amp = 1.5 / (KB * BD)
    keys = jax.random.split(jax.random.fold_in(key, 29), 3)
    side = jax.random.uniform(keys[0], (SD, SS, half, NB, BD, BD), jnp.float32, -amp, amp)
    inner_part = jax.random.uniform(keys[1], (SD, SS, NB, BD, BD), jnp.float32, -amp, amp)
    inner_part = 0.5 * (inner_part + jnp.swapaxes(inner_part, -1, -2))
    diag_vals = 2.0 + jax.random.uniform(keys[2], (SD, SS, NB, BD), jnp.float32)
    ident = jnp.arange(BD)[:, None] == jnp.arange(BD)[None, :]
    blocks = [jnp.where(ident, diag_vals[..., None], inner_part)]
    base = jnp.arange(NB).astype(jnp.int32)
    for which in range(half):
        upper = side[:, :, which]
        index = (base[None, None, :] - offsets[:, :, which][:, :, None] + NB) % NB
        lower = jnp.take_along_axis(upper, index[..., None, None], axis=2)
        blocks.append(upper)
        blocks.append(jnp.swapaxes(lower, -1, -2))
    stacked = jnp.stack(blocks, axis=4)
    return stacked.reshape(SD, SS, NB, BD, KB * BD)


def draw_dirichlet_blocks(key, part):
    first, second = jax.random.split(jax.random.fold_in(key, 61))
    off = jax.random.uniform(first, (SD, SS, NB, BD, BD), jnp.float32, -0.25 / BD, 0.25 / BD)
    off = 0.5 * (off + jnp.swapaxes(off, -1, -2))
    diag_vals = jax.random.uniform(second, (SD, SS, NB, BD), jnp.float32, 0.3, 0.6)
    ident = jnp.arange(BD)[:, None] == jnp.arange(BD)[None, :]
    return jnp.where(ident, diag_vals[..., None], off)


def draw_coarse_inverse(key, part):
    first, second = jax.random.split(jax.random.fold_in(key, 67))
    off = jax.random.uniform(first, (SD, CO, CO), jnp.float32, -0.4 / CO, 0.4 / CO)
    off = 0.5 * (off + jnp.swapaxes(off, -1, -2))
    diag_vals = jax.random.uniform(second, (SD, CO), jnp.float32, 0.5, 1.0)
    ident = jnp.arange(CO)[:, None] == jnp.arange(CO)[None, :]
    return jnp.where(ident, diag_vals[..., None], off)


def draw_face_map(key, part):
    keys = jax.random.split(jax.random.fold_in(key, 41), SD * SS * 4)

    def single(subkey):
        return jax.random.permutation(subkey, NB)[:FB].astype(jnp.int32)
    return jax.vmap(single)(keys).reshape(SD, SS, 4, FB)


def draw_corner_map(key, part):
    keys = jax.random.split(jax.random.fold_in(key, 43), SD * SS)

    def single(subkey):
        return jax.random.permutation(subkey, NB)[:NC].astype(jnp.int32)
    return jax.vmap(single)(keys).reshape(SD, SS, NC)


def draw_face_weight(key, part):
    first, second = jax.random.split(jax.random.fold_in(key, 53))
    low = math.log(0.5)
    high = math.log(2.0)
    along_dam = jnp.exp(jax.random.uniform(first, (SD - 1, SS, FB * BD), jnp.float32, low, high))
    along_sec = jnp.exp(jax.random.uniform(second, (SD, SS - 1, FB * BD), jnp.float32, low, high))
    zero_dam = jnp.zeros((1, SS, FB * BD), jnp.float32)
    zero_sec = jnp.zeros((SD, 1, FB * BD), jnp.float32)
    dam_low = jnp.concatenate([zero_dam, along_dam], axis=0)
    dam_up = jnp.concatenate([along_dam, zero_dam], axis=0)
    sec_low = jnp.concatenate([zero_sec, along_sec], axis=1)
    sec_up = jnp.concatenate([along_sec, zero_sec], axis=1)
    return jnp.stack([dam_low, dam_up, sec_low, sec_up], axis=2)


def place_ends(array, stream_key, low, largest):
    shape = array.shape
    index_at = [jax.random.randint(jax.random.fold_in(stream_key, axis), (), 0, shape[axis]) for axis in range(len(shape))]
    array = array.at[tuple(index_at)].set(low)
    longest = shape.index(max(shape))
    index_at[longest] = (index_at[longest] + 1) % shape[longest]
    return array.at[tuple(index_at)].set(largest)


def block_scale(rng, extent, pieces, low, high):
    gain = 1.0
    for dim, parts in pieces:
        draws = jax.random.uniform(jax.random.fold_in(jax.random.fold_in(rng, 6), dim), (parts,), jnp.float32, low / len(pieces), high / len(pieces))
        gain = gain * jnp.repeat(jnp.exp(draws), extent[dim] // parts).reshape((-1,) + (1,) * (len(extent) - 1 - dim))
    return gain


def setup_inputs(seed: int = 0) -> dict:
    arg_keys = jax.random.split(jax.random.key(seed), 11)
    segment_load = draw_segment_load(jax.random.fold_in(arg_keys[10], 71), 0)
    segment_mask = place_ends((jax.random.randint(arg_keys[1], (SD, SS, NB, RHS), 0, 4) < 3).astype(jnp.int32), jax.random.fold_in(arg_keys[1], 1), 0, 1)
    stiffness = draw_stiffness(jax.random.fold_in(arg_keys[10], 71), 0)
    block_cols = draw_block_cols(jax.random.fold_in(arg_keys[10], 71), 0)
    capillary = jnp.clip(jnp.exp(math.log(2.0) - 2.0794415 * jax.random.uniform(arg_keys[4], (SD, SS, NB, BD), jnp.float32) ** block_scale(arg_keys[4], (SD, SS, NB, BD), ((0, 16), (1, 2)), -0.2, 0.2)), 0.25, 2.0)
    dirichlet_blocks = draw_dirichlet_blocks(jax.random.fold_in(arg_keys[10], 71), 0)
    face_map = draw_face_map(jax.random.fold_in(arg_keys[10], 71), 0)
    face_weight = draw_face_weight(jax.random.fold_in(arg_keys[10], 71), 0)
    corner_map = draw_corner_map(jax.random.fold_in(arg_keys[10], 71), 0)
    coarse_inverse = draw_coarse_inverse(jax.random.fold_in(arg_keys[10], 71), 0)
    return dict(segment_load=segment_load, segment_mask=segment_mask, stiffness=stiffness, block_cols=block_cols, capillary=capillary, dirichlet_blocks=dirichlet_blocks, face_map=face_map, face_weight=face_weight, corner_map=corner_map, coarse_inverse=coarse_inverse)


HIGH = lax.Precision.HIGHEST


def local_product(stiff, cols, tang, field):
    nblk, bdof = tang.shape
    ncol = field.shape[1] // bdof
    gathered = field[cols].reshape(nblk, cols.shape[1] * bdof, ncol)
    prod = jnp.einsum("bde,bes->bds", stiff, gathered, precision=HIGH)
    prod = prod + tang[:, :, None] * field.reshape(nblk, bdof, ncol)
    return prod.reshape(nblk, bdof * ncol)


def take_rows(field, index):
    return field[index]


def add_rows(field, index, values):
    return field.at[index].add(values)


def operate(field, stiffness, block_cols, capillary, face_map, face_weight):
    local = jax.vmap(jax.vmap(local_product))(stiffness, block_cols, capillary, field)
    faces = jax.vmap(jax.vmap(take_rows))(field, face_map)
    zero_dam = jnp.zeros_like(faces[:1, :, 0])
    zero_sec = jnp.zeros_like(faces[:, :1, 2])
    below = jnp.concatenate([zero_dam, faces[:-1, :, 1]], axis=0)
    above = jnp.concatenate([faces[1:, :, 0], zero_dam], axis=0)
    left_sec = jnp.concatenate([zero_sec, faces[:, :-1, 3]], axis=1)
    right_sec = jnp.concatenate([faces[:, 1:, 2], zero_sec], axis=1)
    beside = jnp.stack([below, above, left_sec, right_sec], axis=2)
    weights = face_weight.reshape(SD, SS, 4, FB, BD, 1)
    term = (weights * (faces - beside).reshape(SD, SS, 4, FB, BD, RHS)).reshape(SD, SS, 4 * FB, BD * RHS)
    return jax.vmap(jax.vmap(add_rows))(local, face_map.reshape(SD, SS, 4 * FB), term)


def precondition(resid, dirichlet_blocks, corner_map, coarse_inverse):
    shaped = resid.reshape(SD, SS, NB, BD, RHS)
    outz = jnp.einsum("ijbde,ijbes->ijbds", dirichlet_blocks, shaped, precision=HIGH).reshape(SD, SS, NB, BD * RHS)
    corners = jax.vmap(jax.vmap(take_rows))(resid, corner_map)
    stacked = corners.reshape(SD, SS * NC * BD, RHS)
    correct = jnp.einsum("iqp,ips->iqs", coarse_inverse, stacked, precision=HIGH).reshape(SD, SS, NC, BD * RHS)
    return jax.vmap(jax.vmap(add_rows))(outz, corner_map, correct)


def inner(first, second):
    return (first * second).reshape(SD, SS, NB, BD, RHS).sum(axis=(0, 1, 2, 3))


def spread(coef):
    return jnp.tile(coef, BD)


def reference(segment_load, segment_mask, stiffness, block_cols, capillary, dirichlet_blocks, face_map, face_weight, corner_map, coarse_inverse):
    masked = segment_load.reshape(SD, SS, NB, BD, RHS) * segment_mask.astype(jnp.float32)[:, :, :, None, :]
    resid = masked.reshape(SD, SS, NB, BD * RHS)
    solution = jnp.zeros_like(resid)
    zvec = precondition(resid, dirichlet_blocks, corner_map, coarse_inverse)
    direction = zvec
    gamma = inner(resid, zvec)
    for step in range(ITERS):
        image = operate(direction, stiffness, block_cols, capillary, face_map, face_weight)
        delta = inner(direction, image)
        alpha = spread(gamma / delta)
        solution = solution + alpha * direction
        resid = resid - alpha * image
        if step + 1 < ITERS:
            zvec = precondition(resid, dirichlet_blocks, corner_map, coarse_inverse)
            gnew = inner(resid, zvec)
            direction = zvec + spread(gnew / gamma) * direction
            gamma = gnew
    return (solution, resid)
```

```python
import jax
import jax.numpy as jnp
from jax import lax
from jax.sharding import PartitionSpec as P

HIGH = lax.Precision.HIGHEST


def swap_gather(values, axis):
    size = lax.axis_size(axis)
    if size & (size - 1):
        return lax.all_gather(values, axis, axis=0, tiled=True)
    hop = 1
    while hop < size:
        pairs = [[i, i + hop] for i in range(size) if not i & hop]
        values = lax.all_gather(
            values, axis, axis=0, tiled=True, axis_index_groups=pairs
        )
        hop *= 2
    return values


def with_halo(array, sides, width):
    for axis, dim in sides:
        peers, length = (lax.axis_size(axis), array.shape[dim])
        up = [(i, (i + 1) % peers) for i in range(peers - 1)]
        down = [(j, i) for i, j in up]
        last = lax.slice_in_dim(array, length - width, length, axis=dim)
        first = lax.slice_in_dim(array, 0, width, axis=dim)
        before = lax.ppermute(last, axis, up)
        after = lax.ppermute(first, axis, down)
        array = jnp.concatenate([before, array, after], axis=dim)
    return array


def local_product(stiff, cols, tang, field):
    nblk, bdof = tang.shape
    ncol = field.shape[1] // bdof
    gathered = field[cols].reshape(nblk, cols.shape[1] * bdof, ncol)
    prod = jnp.einsum("bde,bes->bds", stiff, gathered, precision=HIGH)
    prod = prod + tang[:, :, None] * field.reshape(nblk, bdof, ncol)
    return prod.reshape(nblk, bdof * ncol)


def shards(
    segment_load,
    segment_mask,
    stiffness,
    block_cols,
    capillary,
    dirichlet_blocks,
    face_map,
    face_weight,
    corner_map,
    coarse_inverse,
):
    stiff = stiffness[0, 0]
    cols = block_cols[0, 0]
    tang = capillary[0, 0]
    blocks_pre = dirichlet_blocks[0, 0]
    fmap = face_map[0, 0]
    cmap = corner_map[0, 0]
    own_rows = coarse_inverse[0]
    nblk, bdof = tang.shape
    width = segment_load.shape[-1]
    ncol = width // bdof
    nface = fmap.shape[1]
    ncorner = cmap.shape[0]
    weights = face_weight[0, 0].reshape(4, nface, bdof, 1)
    flat_faces = fmap.reshape(4 * nface)
    masked = (
        segment_load[0, 0].reshape(nblk, bdof, ncol)
        * segment_mask[0, 0].astype(jnp.float32)[:, None, :]
    )
    resid = masked.reshape(nblk, width)

    def precondition(field):
        outz = jnp.einsum(
            "bde,bes->bds", blocks_pre, field.reshape(nblk, bdof, ncol), precision=HIGH
        ).reshape(nblk, width)
        corners = field[cmap]
        piece = lax.all_gather(corners, "sec", axis=0, tiled=True)
        correct = jnp.dot(
            own_rows, piece.reshape(piece.shape[0] * bdof, ncol), precision=HIGH
        ).reshape(ncorner, width)
        return outz.at[cmap].add(correct)

    def operate(field):
        local = local_product(stiff, cols, tang, field)
        faces = field[fmap]
        dam_side = with_halo(faces[0:2], (("dam", 0),), 1)
        sec_side = with_halo(faces[2:4], (("sec", 0),), 1)
        beside = jnp.stack([dam_side[0], dam_side[3], sec_side[0], sec_side[3]])
        term = (weights * (faces - beside).reshape(4, nface, bdof, ncol)).reshape(4 * nface, width)
        return local.at[flat_faces].add(term)

    def inner(first, second):
        return (first * second).reshape(nblk, bdof, ncol).sum(axis=(0, 1))

    def spread(coef):
        return jnp.tile(coef, bdof)

    zvec = precondition(resid)
    image = operate(zvec)
    mvec = precondition(image)
    nvec = operate(mvec)
    parts = jnp.concatenate(
        [inner(resid, zvec), inner(zvec, image), inner(image, mvec), inner(mvec, nvec)]
    )
    stacked = swap_gather(swap_gather(parts[None], "sec"), "dam")
    sums = stacked.sum(axis=0).reshape(4, ncol)
    gamma, delta, mu, nu = sums[0], sums[1], sums[2], sums[3]
    alpha = gamma / delta
    gnew = gamma - 2.0 * alpha * delta + alpha * alpha * mu
    grow = 1.0 + gnew / gamma
    dnew = grow * grow * delta - 2.0 * alpha * grow * mu + alpha * alpha * nu
    anew = gnew / dnew
    both = spread(alpha + anew * grow)
    second = spread(anew * alpha)
    return (
        (both * zvec - second * mvec)[None, None],
        (resid - both * image + second * nvec)[None, None],
    )


def solution(mesh):
    placed = (
        P("dam", "sec", None, None),
        P("dam", "sec", None, None),
        P("dam", "sec", None, None, None),
        P("dam", "sec", None, None),
        P("dam", "sec", None, None),
        P("dam", "sec", None, None, None),
        P("dam", "sec", None, None),
        P("dam", "sec", None, None),
        P("dam", "sec", None),
        P("dam", "sec", None),
    )
    return jax.shard_map(
        shards,
        mesh=mesh,
        in_specs=placed,
        out_specs=(P("dam", "sec", None, None), P("dam", "sec", None, None)),
        check_vma=False,
    )
```

```python
import jax
import jax.numpy as jnp
from jax import lax
from jax.sharding import PartitionSpec as P

HIGH = lax.Precision.HIGHEST


def everywhere(values):
    total = lax.axis_size("dam") * lax.axis_size("sec")
    copies = jnp.broadcast_to(values[None], (total,) + values.shape)
    return lax.all_to_all(copies, ("dam", "sec"), split_axis=0, concat_axis=0)


def from_sides(lower, upper, axis):
    size = lax.axis_size(axis)
    if size & 1:
        up = [(i, i + 1) for i in range(size - 1)]
        down = [(j, i) for i, j in up]
        return lax.ppermute(upper, axis, up), lax.ppermute(lower, axis, down)
    even = lax.axis_index(axis) % 2 == 0
    if size == 2:
        both = lax.all_gather(jnp.where(even, upper, lower), axis)
        other = jnp.where(even, both[1], both[0])
        zero = jnp.zeros_like(other)
        return jnp.where(even, zero, other), jnp.where(even, other, zero)
    first = [(i, i ^ 1) for i in range(size)]
    second = [(i, i + 1) for i in range(1, size - 1, 2)]
    second = second + [(j, i) for i, j in second]
    near = lax.ppermute(jnp.where(even, upper, lower), axis, first)
    far = lax.ppermute(jnp.where(even, lower, upper), axis, second)
    return jnp.where(even, far, near), jnp.where(even, near, far)


def local_product(stiff, cols, tang, field):
    nblk, bdof = tang.shape
    ncol = field.shape[1] // bdof
    gathered = field[cols].reshape(nblk, cols.shape[1] * bdof, ncol)
    prod = jnp.einsum("bde,bes->bds", stiff, gathered, precision=HIGH)
    prod = prod + tang[:, :, None] * field.reshape(nblk, bdof, ncol)
    return prod.reshape(nblk, bdof * ncol)


def shards(
    segment_load,
    segment_mask,
    stiffness,
    block_cols,
    capillary,
    dirichlet_blocks,
    face_map,
    face_weight,
    corner_map,
    coarse_inverse,
):
    stiff = stiffness[0, 0]
    cols = block_cols[0, 0]
    tang = capillary[0, 0]
    blocks_pre = dirichlet_blocks[0, 0]
    fmap = face_map[0, 0]
    cmap = corner_map[0, 0]
    own_rows = coarse_inverse[0]
    nblk, bdof = tang.shape
    width = segment_load.shape[-1]
    ncol = width // bdof
    nface = fmap.shape[1]
    ncorner = cmap.shape[0]
    weights = face_weight[0, 0].reshape(4, nface, bdof, 1)
    flat_faces = fmap.reshape(4 * nface)
    masked = (
        segment_load[0, 0].reshape(nblk, bdof, ncol)
        * segment_mask[0, 0].astype(jnp.float32)[:, None, :]
    )
    resid = masked.reshape(nblk, width)

    def precondition(field):
        outz = jnp.einsum(
            "bde,bes->bds", blocks_pre, field.reshape(nblk, bdof, ncol), precision=HIGH
        ).reshape(nblk, width)
        corners = field[cmap]
        piece = lax.all_gather(corners, "sec", axis=0, tiled=True)
        correct = jnp.dot(
            own_rows, piece.reshape(piece.shape[0] * bdof, ncol), precision=HIGH
        ).reshape(ncorner, width)
        return outz.at[cmap].add(correct)

    def operate(field):
        local = local_product(stiff, cols, tang, field)
        faces = field[fmap]
        sec_side = from_sides(faces[2], faces[3], "sec")
        dam_side = from_sides(faces[0], faces[1], "dam")
        beside = jnp.stack(dam_side + sec_side)
        term = (weights * (faces - beside).reshape(4, nface, bdof, ncol)).reshape(4 * nface, width)
        return local.at[flat_faces].add(term)

    def inner(first, second):
        return (first * second).reshape(nblk, bdof, ncol).sum(axis=(0, 1))

    def spread(coef):
        return jnp.tile(coef, bdof)

    zvec = precondition(resid)
    image = operate(zvec)
    mvec = precondition(image)
    nvec = operate(mvec)
    parts = jnp.concatenate(
        [inner(resid, zvec), inner(zvec, image), inner(image, mvec), inner(mvec, nvec)]
    )
    sums = everywhere(parts).sum(axis=0).reshape(4, ncol)
    gamma, delta, mu, nu = sums[0], sums[1], sums[2], sums[3]
    alpha = gamma / delta
    gnew = gamma - 2.0 * alpha * delta + alpha * alpha * mu
    grow = 1.0 + gnew / gamma
    dnew = grow * grow * delta - 2.0 * alpha * grow * mu + alpha * alpha * nu
    anew = gnew / dnew
    both = spread(alpha + anew * grow)
    second = spread(anew * alpha)
    return (
        (both * zvec - second * mvec)[None, None],
        (resid - both * image + second * nvec)[None, None],
    )


def solution(mesh):
    placed = (
        P("dam", "sec", None, None),
        P("dam", "sec", None, None),
        P("dam", "sec", None, None, None),
        P("dam", "sec", None, None),
        P("dam", "sec", None, None),
        P("dam", "sec", None, None, None),
        P("dam", "sec", None, None),
        P("dam", "sec", None, None),
        P("dam", "sec", None),
        P("dam", "sec", None),
    )
    return jax.shard_map(
        shards,
        mesh=mesh,
        in_specs=placed,
        out_specs=(P("dam", "sec", None, None), P("dam", "sec", None, None)),
        check_vma=False,
    )
```

```python
import functools

import jax
import jax.numpy as jnp
from jax import lax
from jax.experimental import pallas as pl
from jax.experimental.pallas import tpu as pltpu
from jax.sharding import PartitionSpec as P

F32 = jnp.float32
BF16 = jnp.bfloat16
VMEM_LIMIT = 24 * 1024 * 1024


def halves(x):
    high = x.astype(BF16)
    return high, (x - high.astype(F32)).astype(BF16)


def dot_t(a, b):
    return lax.dot_general(a, b, (((1,), (1,)), ((), ())), preferred_element_type=F32)


def dot(a, b):
    return lax.dot_general(a, b, (((1,), (0,)), ((), ())), preferred_element_type=F32)


def three_pass(mul, left, high, low):
    rows = left.shape[0] // 2
    first = mul(left, high)
    return first[:rows] + first[rows:] + mul(left[:rows], low)


def corner_kernel(cmap, field, out):
    bdof = field.shape[2]
    for n in range(out.shape[1] // bdof):
        out[:, n * bdof : (n + 1) * bdof] = field[cmap[n]]


def pack_faces(ints, where, ids_at, field, outs):
    bdof = field.shape[2]
    nface = outs[0].shape[1] // bdof
    for i, out in enumerate(outs):
        face = ints[ids_at + i] * nface + where
        for p in range(nface):
            out[:, p * bdof : (p + 1) * bdof] = field[ints[face + p]]


def precondition_kernel(ncorner, nface, ints, field, blocks, rows, corners, zout, *rest):
    *faces, tiles_high, tiles_low, left = rest
    nblk, ncol, bdof = field.shape
    group = tiles_high.shape[1] // bdof
    tiles_high[...] = jnp.zeros_like(tiles_high)
    tiles_low[...] = jnp.zeros_like(tiles_low)
    for b in range(nblk):
        t, j = divmod(b, group)
        high, low = halves(blocks[b])
        here = slice(j * bdof, (j + 1) * bdof)
        tiles_high[t, here, here] = high
        tiles_low[t, here, here] = low
        high, low = halves(field[b])
        left[t, :ncol, here] = high
        left[t, ncol:, here] = low
    for t in range(nblk // group):
        out = three_pass(dot, left[t], tiles_high[t], tiles_low[t])
        for j in range(group):
            zout[t * group + j] = out[:, j * bdof : (j + 1) * bdof]
    wide = ncorner * bdof
    correct = None
    for s in range(corners.shape[0]):
        high, low = halves(rows[:, s * wide : (s + 1) * wide])
        chigh, clow = halves(corners[s])
        term = three_pass(dot_t, jnp.concatenate([chigh, clow], axis=0), high, low)
        correct = term if correct is None else correct + term
    for n in range(ncorner):
        b = ints[n]
        zout[b] = zout[b] + correct[:, n * bdof : (n + 1) * bdof]
    pack_faces(ints, ncorner, ncorner + 4 * nface, zout, faces)


def stack_left(field, left):
    nblk, ncol, bdof = field.shape
    for b in range(nblk):
        high, low = halves(field[b])
        left[:ncol, b * bdof : (b + 1) * bdof] = high
        left[ncol:, b * bdof : (b + 1) * bdof] = low


def build_kernel(nface, ints, cols, field, stiff, capillary, weights, out, high, low, left, diag):
    nblk, ncol, bdof = field.shape
    kept = stiff.shape[2] // bdof
    ncorner = ints.shape[0] - 4 * nface - 8
    for b in range(nblk):
        diag[b] = capillary[b : b + 1, :]
    for f in range(4):
        for p in range(nface):
            b = ints[ncorner + f * nface + p]
            diag[b] = diag[b] + weights[f : f + 1, p * bdof : (p + 1) * bdof]
    eye = lax.broadcasted_iota(jnp.int32, (bdof, bdof), 0) == lax.broadcasted_iota(
        jnp.int32, (bdof, bdof), 1
    )
    high[...] = jnp.zeros_like(high)
    low[...] = jnp.zeros_like(low)
    for b in range(nblk):
        for k in range(kept):
            back = 0 if k == 0 else k + 1 if k % 2 else k - 1
            c = cols[b * kept + k]
            part = stiff[c, :, back * bdof : (back + 1) * bdof]
            if k == 0:
                part = part + jnp.where(eye, diag[b], 0.0)
            phigh, plow = halves(part)
            start = pl.multiple_of(c * bdof, bdof)
            high[pl.ds(start, bdof), b * bdof : (b + 1) * bdof] = phigh
            low[pl.ds(start, bdof), b * bdof : (b + 1) * bdof] = plow
    stack_left(field, left)
    out[...] = three_pass(dot, left[...], high[...], low[...])


def local_kernel(field, high, low, out, left):
    stack_left(field, left)
    out[...] = three_pass(dot, left[...], high[...], low[...])


def couple(ints, ids_at, where, nface, weights, local, besides, field):
    nblk, ncol, bdof = field.shape
    for b in range(nblk):
        field[b] = local[:, b * bdof : (b + 1) * bdof]
    for i, beside in enumerate(besides):
        face = ints[ids_at + i]
        term = weights[pl.ds(face, 1), :] * beside[...]
        for p in range(nface):
            b = ints[where + face * nface + p]
            field[b] = field[b] - term[:, p * bdof : (p + 1) * bdof]


def lanes(first, second):
    return jnp.sum(first[...] * second[...], axis=0)


def image_kernel(ncorner, nface, ints, weights, local, rvec, zvec, *rest):
    *besides, wout, corners, sums = rest
    couple(ints, ncorner + 4 * nface, ncorner, nface, weights, local, besides, wout)
    bdof = zvec.shape[2]
    for n in range(ncorner):
        corners[:, n * bdof : (n + 1) * bdof] = wout[ints[n]]
    sums[0] = lanes(rvec, zvec)
    sums[1] = lanes(zvec, wout)


def last_kernel(ncorner, nface, ints, weights, local, wvec, mvec, sums, *rest):
    *besides, nout, totals = rest
    couple(ints, ncorner + 4 * nface, ncorner, nface, weights, local, besides, nout)
    parts = jnp.concatenate(
        [sums[0], sums[1], lanes(wvec, mvec), lanes(mvec, nout)], axis=0
    )
    totals[...] = lax.dot_general(
        jnp.ones((1, parts.shape[1]), F32),
        parts,
        (((1,), (1,)), ((), ())),
        precision=lax.Precision.HIGHEST,
        preferred_element_type=F32,
    )


def finish_kernel(shares, rvec, zvec, wvec, mvec, nvec, sol, res):
    nblk, ncol, bdof = rvec.shape
    width = shares.shape[1]
    total = jnp.sum(shares[...], axis=0, keepdims=True)
    eye = lax.broadcasted_iota(jnp.int32, (width, width), 0) == lax.broadcasted_iota(
        jnp.int32, (width, width), 1
    )
    column = jnp.sum(jnp.where(eye, total, 0.0), axis=1, keepdims=True)
    gamma, delta, mu, nu = [column[q * ncol : (q + 1) * ncol] for q in range(4)]
    alpha = gamma / delta
    gnew = gamma - 2.0 * alpha * delta + alpha * alpha * mu
    grow = 1.0 + gnew / gamma
    dnew = grow * grow * delta - 2.0 * alpha * grow * mu + alpha * alpha * nu
    anew = gnew / dnew
    both = alpha + anew * grow
    second = anew * alpha
    sol[...] = both * zvec[...] - second * mvec[...]
    res[...] = rvec[...] - both * wvec[...] + second * nvec[...]


def call(kernel, outs, scratch, smem, *args):
    vmem = pl.BlockSpec(memory_space=pltpu.VMEM)
    return pl.pallas_call(
        kernel,
        out_shape=outs,
        in_specs=[pl.BlockSpec(memory_space=pltpu.SMEM)] * smem + [vmem] * (len(args) - smem),
        out_specs=jax.tree.map(lambda _: vmem, outs),
        scratch_shapes=scratch,
        compiler_params=pltpu.CompilerParams(vmem_limit_bytes=VMEM_LIMIT),
    )(*args)


def everywhere(values):
    total = lax.axis_size("dam") * lax.axis_size("sec")
    copies = jnp.broadcast_to(values[None], (total,) + values.shape)
    return lax.all_to_all(copies, ("dam", "sec"), split_axis=0, concat_axis=0)


def partners(axis):
    even = lax.axis_index(axis) % 2 == 0
    near = jnp.where(even, 1, 0)
    return [near] if lax.axis_size(axis) == 2 else [near, 1 - near]


def exchange(sends, axis):
    size = lax.axis_size(axis)
    if size == 2:
        both = lax.all_gather(sends[0], axis)
        return [lax.dynamic_index_in_dim(both, 1 - lax.axis_index(axis), keepdims=False)]
    got = []
    for first, send in enumerate(sends):
        pairs = [(i, i + 1) for i in range(first, size - 1, 2)]
        got.append(lax.ppermute(send, axis, pairs + [(j, i) for i, j in pairs]))
    return got


def shards(
    segment_load,
    segment_mask,
    stiffness,
    block_cols,
    capillary,
    dirichlet_blocks,
    face_map,
    face_weight,
    corner_map,
    coarse_inverse,
):
    nblk, bdof = capillary.shape[2:]
    ncol = segment_load.shape[-1] // bdof
    nface = face_map.shape[3]
    ncorner = corner_map.shape[2]
    size = nblk * bdof
    weights = face_weight[0, 0]
    dam_ids = partners("dam")
    sec_ids = [i + 2 for i in partners("sec")]
    ids = dam_ids + sec_ids
    pad = jnp.zeros((8 - len(ids),), jnp.int32)
    ints = jnp.concatenate(
        [corner_map[0, 0], face_map[0, 0].reshape(-1), jnp.stack(ids).astype(jnp.int32), pad]
    )
    masked = (
        segment_load[0, 0].reshape(nblk, bdof, ncol)
        * segment_mask[0, 0].astype(F32)[:, None, :]
    )
    rvec = jnp.swapaxes(masked, 1, 2)

    field = jax.ShapeDtypeStruct((nblk, ncol, bdof), F32)
    corner = jax.ShapeDtypeStruct((ncol, ncorner * bdof), F32)
    face = jax.ShapeDtypeStruct((ncol, nface * bdof), F32)
    flat = jax.ShapeDtypeStruct((ncol, size), F32)
    dense = jax.ShapeDtypeStruct((size, size), BF16)
    group = ncorner * bdof
    tiles = pltpu.VMEM((size // group, group, group), BF16)

    def precondition(vec, corners):
        return call(
            functools.partial(precondition_kernel, ncorner, nface),
            (field,) + (face,) * len(ids),
            [tiles, tiles, pltpu.VMEM((size // group, 2 * ncol, group), BF16)],
            1,
            ints,
            vec,
            dirichlet_blocks[0, 0],
            coarse_inverse[0],
            lax.all_gather(corners, "sec"),
        )

    def swap(sends):
        dam = exchange(sends[: len(dam_ids)], "dam")
        return dam + exchange(sends[len(dam_ids) :], "sec")

    left = pltpu.VMEM((2 * ncol, size), BF16)
    corners = call(corner_kernel, corner, [], 1, corner_map[0, 0], rvec)
    zvec, *sends = precondition(rvec, corners)
    besides = swap(sends)
    local, high, low = call(
        functools.partial(build_kernel, nface),
        (flat, dense, dense),
        [left, pltpu.VMEM((nblk, 1, bdof), F32)],
        2,
        ints,
        block_cols[0, 0].reshape(-1),
        zvec,
        stiffness[0, 0],
        capillary[0, 0],
        weights,
    )
    wvec, corners, sums = call(
        functools.partial(image_kernel, ncorner, nface),
        (field, corner, jax.ShapeDtypeStruct((2, ncol, bdof), F32)),
        [],
        1,
        ints,
        weights,
        local,
        rvec,
        zvec,
        *besides,
    )
    mvec, *sends = precondition(wvec, corners)
    besides = swap(sends)
    local = call(local_kernel, flat, [left], 0, mvec, high, low)
    nvec, totals = call(
        functools.partial(last_kernel, ncorner, nface),
        (field, jax.ShapeDtypeStruct((1, 4 * ncol), F32)),
        [],
        1,
        ints,
        weights,
        local,
        wvec,
        mvec,
        sums,
        *besides,
    )
    shares = everywhere(totals[0])
    sol, res = call(
        finish_kernel, (field, field), [], 0, shares, rvec, zvec, wvec, mvec, nvec
    )

    def back(vec):
        return jnp.swapaxes(vec, 1, 2).reshape(1, 1, nblk, bdof * ncol)

    return back(sol), back(res)


def solution(mesh):
    placed = (
        P("dam", "sec", None, None),
        P("dam", "sec", None, None),
        P("dam", "sec", None, None, None),
        P("dam", "sec", None, None),
        P("dam", "sec", None, None),
        P("dam", "sec", None, None, None),
        P("dam", "sec", None, None),
        P("dam", "sec", None, None),
        P("dam", "sec", None),
        P("dam", "sec", None),
    )
    return jax.shard_map(
        shards,
        mesh=mesh,
        in_specs=placed,
        out_specs=(P("dam", "sec", None, None), P("dam", "sec", None, None)),
        check_vma=False,
    )
```

```python
import functools

import jax
import jax.numpy as jnp
from jax import lax
from jax.experimental import pallas as pl
from jax.experimental.pallas import tpu as pltpu
from jax.sharding import PartitionSpec as P

F32 = jnp.float32
BF16 = jnp.bfloat16
VMEM_LIMIT = 16 * 1024 * 1024


def halves(x):
    high = x.astype(BF16)
    return high, (x - high.astype(F32)).astype(BF16)


def dot_t(a, b):
    return lax.dot_general(a, b, (((1,), (1,)), ((), ())), preferred_element_type=F32)


def dot(a, b):
    return lax.dot_general(a, b, (((1,), (0,)), ((), ())), preferred_element_type=F32)


def three_pass(mul, left, high, low):
    rows = left.shape[0] // 2
    first = mul(left, high)
    return first[:rows] + first[rows:] + mul(left[:rows], low)


def near_face():
    return 1 - lax.axis_index("dam") % 2


def sec_face():
    return 3 - lax.axis_index("sec")


def pack_face(face, fmap, field, out):
    bdof = field.shape[2]
    for p in range(fmap.shape[3]):
        out[..., : field.shape[1], p * bdof : (p + 1) * bdof] = field[fmap[0, 0, face, p]]


def scatter_corners(cmap, correct, field):
    bdof = field.shape[2]
    for n in range(cmap.shape[2]):
        b = cmap[0, 0, n]
        field[b] = field[b] + correct[:, n * bdof : (n + 1) * bdof]


def begin(pair, cmap, fmap, field, blocks, rows, base, payload, tiles_high, tiles_low, left):
    nblk, ncol, bdof = field.shape
    ncorner, nface = cmap.shape[2], fmap.shape[3]
    group = tiles_high.shape[1] // bdof
    tiles_high[...] = jnp.zeros_like(tiles_high)
    tiles_low[...] = jnp.zeros_like(tiles_low)
    for b in range(nblk):
        t, j = divmod(b, group)
        here = slice(j * bdof, (j + 1) * bdof)
        tiles_high[t, here, here], tiles_low[t, here, here] = halves(blocks[b])
        left[t, :ncol, here], left[t, ncol:, here] = halves(field[b])
    for t in range(nblk // group):
        out = three_pass(dot, left[t], tiles_high[t], tiles_low[t])
        for j in range(group):
            base[t * group + j] = out[:, j * bdof : (j + 1) * bdof]
    at = nface * bdof if pair else 0
    wide = ncorner * bdof
    for n in range(ncorner):
        payload[:ncol, at + n * bdof : at + (n + 1) * bdof] = field[cmap[0, 0, n]]
    if pair:
        start = pl.multiple_of(lax.axis_index("sec") * wide, wide)
        correct = three_pass(
            dot_t, stack(payload[:ncol, at:]), *halves(rows[:, pl.ds(start, wide)])
        )
        scatter_corners(cmap, correct, base)
        pack_face(sec_face(), fmap, base, payload)
        if payload.shape[0] > ncol:
            payload[ncol:, :] = jnp.zeros_like(payload[ncol:, :])
            for n in range(ncorner):
                for p in range(nface):
                    same = cmap[0, 0, n] == fmap[0, 0, sec_face(), p]
                    payload[ncol + n : ncol + n + 1, p * bdof : (p + 1) * bdof] = jnp.full(
                        (1, bdof), jnp.where(same, 1.0, 0.0), F32
                    )


def stack(x):
    return jnp.concatenate(halves(x), axis=0)


def end_kernel(pair, cmap, fmap, base, rows, shares, marks, zout, *faces):
    nblk, ncol, bdof = base.shape
    ncorner, nface = cmap.shape[2], fmap.shape[3]
    wide = ncorner * bdof
    zout[...] = base[...]
    if pair:
        me = lax.axis_index("sec")
        at = nface * bdof
        start = pl.multiple_of((1 - me) * wide, wide)
        high, low = halves(rows[:, pl.ds(start, wide)])
        own = stack(shares[pl.ds(me, 1), :ncol, at:][0])
        other = stack(shares[pl.ds(1 - me, 1), :ncol, at:][0])
        theirs = three_pass(dot, own, high, low)
        correct = three_pass(dot_t, other, high, low)
        chunk = 2 * bdof
        twice = [
            jnp.concatenate([theirs[:, n * bdof : (n + 1) * bdof]] * 2, axis=1)
            for n in range(ncorner)
        ]
        for j in range(at // chunk):
            here = slice(j * chunk, (j + 1) * chunk)
            value = shares[pl.ds(1 - me, 1), :ncol, here][0]
            for n in range(ncorner):
                mark = marks[pl.ds(1 - me, 1), ncol + n : ncol + n + 1, here][0]
                value = value + mark * twice[n]
            faces[-1][:, here] = value
    else:
        correct = 0.0
        for s in range(shares.shape[0]):
            high, low = halves(rows[:, s * wide : (s + 1) * wide])
            correct = correct + three_pass(dot_t, stack(shares[s]), high, low)
    scatter_corners(cmap, correct, zout)
    near = near_face()
    pack_face(near, fmap, zout, faces[0])
    pack_face(1 - near, fmap, zout, faces[1])
    if not pair:
        near = 3 - lax.axis_index("sec") % 2
        pack_face(near, fmap, zout, faces[2])
        pack_face(5 - near, fmap, zout, faces[3])


def start_kernel(pair, cmap, fmap, load, mask, blocks, rows, rvec, base, payload, *scratch):
    tall, short, *tiles = scratch
    nblk, ncol, bdof = rvec.shape
    lanes_at = 128
    scale = mask[...].astype(F32)
    scale = jnp.concatenate([scale] * (lanes_at // ncol), axis=1)
    for j in range(load.shape[1] // lanes_at):
        here = slice(j * lanes_at, (j + 1) * lanes_at)
        tall[here, :] = (load[:, here] * scale).T
    for c in range(ncol):
        short[c * nblk : (c + 1) * nblk, :] = tall[pl.ds(c, bdof, stride=ncol), :].T
    for b in range(nblk):
        rvec[b] = short[pl.ds(b, ncol, stride=nblk), :]
    begin(pair, cmap, fmap, rvec, blocks, rows, base, payload, *tiles)


def local_kernel(cols, field, stiff, out, left):
    nblk, ncol, bdof = field.shape
    kept = stiff.shape[2] // bdof
    for b in range(nblk):
        left[b] = stack(field[b])
    for b in range(nblk):
        gathered = jnp.concatenate([left[cols[k, 0, b]] for k in range(kept)], axis=1)
        out[b] = three_pass(dot_t, gathered, *halves(stiff[b]))


def couple(fmap, weights, capillary, local, field, besides, out):
    nblk, ncol, bdof = field.shape
    for b in range(nblk):
        out[b] = local[b] + capillary[b : b + 1, :] * field[b]
    near = near_face()
    met = [near, 1 - near]
    if len(besides) == 3:
        met.append(sec_face())
    else:
        first = 3 - lax.axis_index("sec") % 2
        met += [first, 5 - first]
    for face, beside in zip(met, besides):
        weight = weights[pl.ds(face, 1), :]
        term = weight * beside[...]
        for p in range(fmap.shape[3]):
            here = slice(p * bdof, (p + 1) * bdof)
            b = fmap[0, 0, face, p]
            out[b] = out[b] + (weight[:, here] * field[b] - term[:, here])


def lanes(first, second):
    return jnp.sum(first[...] * second[...], axis=0)


def image_kernel(
    pair, cmap, fmap, weights, capillary, local, rvec, zvec, blocks, rows, *rest
):
    count = 3 if pair else 4
    besides, (wout, sums, base, payload, *scratch) = rest[:count], rest[count:]
    couple(fmap, weights, capillary, local, zvec, besides, wout)
    sums[0] = lanes(rvec, zvec)
    sums[1] = lanes(zvec, wout)
    begin(pair, cmap, fmap, wout, blocks, rows, base, payload, *scratch)


def last_kernel(fmap, weights, capillary, local, wvec, mvec, sums, *rest):
    *besides, nout, totals = rest
    couple(fmap, weights, capillary, local, mvec, besides, nout)
    parts = jnp.concatenate(
        [sums[0], sums[1], lanes(wvec, mvec), lanes(mvec, nout)], axis=0
    )
    sides = lax.dot_general(
        jnp.ones(totals.shape[:1] + parts.shape[1:], F32),
        parts,
        (((1,), (1,)), ((), ())),
        precision=lax.Precision.HIGHEST,
        preferred_element_type=F32,
    )
    totals[...] = jnp.concatenate([sides, jnp.zeros_like(sides)], axis=1)


def finish_kernel(shares, rvec, zvec, wvec, mvec, nvec, sol, res, short, tall):
    nblk, ncol, bdof = rvec.shape
    width = 4 * ncol
    total = jnp.sum(shares[:, 0, :], axis=0, keepdims=True)[:, :width]
    eye = lax.broadcasted_iota(jnp.int32, (width, width), 0) == lax.broadcasted_iota(
        jnp.int32, (width, width), 1
    )
    column = jnp.sum(jnp.where(eye, total, 0.0), axis=1, keepdims=True)
    gamma, delta, mu, nu = [column[q * ncol : (q + 1) * ncol] for q in range(4)]
    alpha = gamma / delta
    gnew = gamma - 2.0 * alpha * delta + alpha * alpha * mu
    grow = 1.0 + gnew / gamma
    dnew = grow * grow * delta - 2.0 * alpha * grow * mu + alpha * alpha * nu
    anew = gnew / dnew
    both = alpha + anew * grow
    second = anew * alpha
    both_at = 2 * nblk
    for b in range(nblk):
        short[pl.ds(b, ncol, stride=both_at), :] = both * zvec[b] - second * mvec[b]
        short[pl.ds(nblk + b, ncol, stride=both_at), :] = (
            rvec[b] - both * wvec[b] + second * nvec[b]
        )
    for c in range(ncol):
        tall[pl.ds(c, bdof, stride=ncol), :] = short[c * both_at : (c + 1) * both_at, :].T
    lanes_at = 128
    for j in range(sol.shape[1] // lanes_at):
        here = slice(j * lanes_at, (j + 1) * lanes_at)
        flat = tall[here, :].T
        sol[:, here] = flat[:nblk]
        res[:, here] = flat[nblk:]


def call(kernel, outs, scratch, smem, *args):
    vmem = pl.BlockSpec(memory_space=pltpu.VMEM)
    return pl.pallas_call(
        kernel,
        out_shape=outs,
        in_specs=[pl.BlockSpec(memory_space=pltpu.SMEM)] * smem + [vmem] * (len(args) - smem),
        out_specs=jax.tree.map(lambda _: vmem, outs),
        scratch_shapes=scratch,
        compiler_params=pltpu.CompilerParams(vmem_limit_bytes=VMEM_LIMIT),
    )(*args)


def everywhere(values):
    if lax.axis_size("sec") == 2:
        values = lax.all_gather(values, "sec")[:, :1].sum(axis=0)
    else:
        values = lax.psum(values[:1], "sec")
    copies = jnp.broadcast_to(values[None], (lax.axis_size("dam"),) + values.shape)
    return lax.all_to_all(copies, "dam", split_axis=0, concat_axis=0)


def exchange(sends, axis):
    size = lax.axis_size(axis)
    got = []
    for first, send in enumerate(sends):
        pairs = [(i, i + 1) for i in range(first, size - 1, 2)]
        got.append(lax.ppermute(send, axis, pairs + [(j, i) for i, j in pairs]))
    return got


def shards(
    segment_load,
    segment_mask,
    stiffness,
    block_cols,
    capillary,
    dirichlet_blocks,
    face_map,
    face_weight,
    corner_map,
    coarse_inverse,
):
    nblk, bdof = capillary.shape[2:]
    ncol = segment_load.shape[-1] // bdof
    nface = face_map.shape[3]
    ncorner = corner_map.shape[2]
    size = nblk * bdof
    pair = lax.axis_size("sec") == 2
    cols = jnp.transpose(block_cols[0], (2, 0, 1))
    tang, weights = capillary[0, 0], face_weight[0, 0]
    blocks, rows = dirichlet_blocks[0, 0], coarse_inverse[0]

    def shape(*dims):
        return jax.ShapeDtypeStruct(dims, F32)

    field = shape(nblk, ncol, bdof)
    face = shape(ncol, nface * bdof)
    group = ncorner * bdof
    tiles = pltpu.VMEM((size // group, group, group), BF16)
    splits = [tiles, tiles, pltpu.VMEM((size // group, 2 * ncol, group), BF16)]
    left = pltpu.VMEM((nblk, 2 * ncol, bdof), BF16)
    lane = group + nface * bdof if pair else group
    marked = ncol + 8 if pair else ncol

    def finish(base, shares, marks):
        vec, *faces = call(
            functools.partial(end_kernel, pair),
            (field,) + (face,) * (3 if pair else 4),
            [],
            2,
            corner_map,
            face_map,
            base,
            rows,
            shares,
            marks,
        )
        besides = exchange(faces[:2], "dam")
        besides += faces[2:] if pair else exchange(faces[2:], "sec")
        return vec, besides

    def local(vec):
        return call(local_kernel, field, [left], 1, cols, vec, stiffness[0, 0])

    rvec, base, payload = call(
        functools.partial(start_kernel, pair),
        (field, field, shape(marked, lane)),
        [pltpu.VMEM((size // nblk * ncol, nblk), F32), pltpu.VMEM((ncol * nblk, bdof), F32)]
        + splits,
        2,
        corner_map,
        face_map,
        segment_load[0, 0],
        segment_mask[0, 0],
        blocks,
        rows,
    )
    marks = lax.all_gather(payload, "sec")
    zvec, besides = finish(base, marks, marks)
    wvec, sums, base, payload = call(
        functools.partial(image_kernel, pair),
        (field, shape(2, ncol, bdof), field, shape(ncol, lane)),
        splits,
        2,
        corner_map,
        face_map,
        weights,
        tang,
        local(zvec),
        rvec,
        zvec,
        blocks,
        rows,
        *besides,
    )
    mvec, besides = finish(base, lax.all_gather(payload, "sec"), marks)
    nvec, totals = call(
        last_kernel,
        (field, shape(8, 2 * bdof)),
        [],
        1,
        face_map,
        weights,
        tang,
        local(mvec),
        wvec,
        mvec,
        sums,
        *besides,
    )
    sol, res = call(
        finish_kernel,
        (shape(nblk, bdof * ncol),) * 2,
        [pltpu.VMEM((ncol * 2 * nblk, bdof), F32), pltpu.VMEM((bdof * ncol, 2 * nblk), F32)],
        0,
        everywhere(totals),
        rvec,
        zvec,
        wvec,
        mvec,
        nvec,
    )
    return sol[None, None], res[None, None]


def solution(mesh):
    placed = (
        P("dam", "sec", None, None),
        P("dam", "sec", None, None),
        P("dam", "sec", None, None, None),
        P("dam", "sec", None, None),
        P("dam", "sec", None, None),
        P("dam", "sec", None, None, None),
        P("dam", "sec", None, None),
        P("dam", "sec", None, None),
        P("dam", "sec", None),
        P("dam", "sec", None),
    )
    return jax.shard_map(
        shards,
        mesh=mesh,
        in_specs=placed,
        out_specs=(P("dam", "sec", None, None), P("dam", "sec", None, None)),
        check_vma=False,
    )
```

```python
import functools

import jax
import jax.numpy as jnp
from jax import lax
from jax.experimental import pallas as pl
from jax.experimental.pallas import tpu as pltpu
from jax.sharding import PartitionSpec as P

F32 = jnp.float32
BF16 = jnp.bfloat16
VMEM_LIMIT = 16 * 1024 * 1024


def halves(x):
    high = x.astype(BF16)
    return high, (x - high.astype(F32)).astype(BF16)


def dot_t(a, b):
    return lax.dot_general(a, b, (((1,), (1,)), ((), ())), preferred_element_type=F32)


def dot(a, b):
    return lax.dot_general(a, b, (((1,), (0,)), ((), ())), preferred_element_type=F32)


def three_pass(mul, left, high, low):
    rows = left.shape[0] // 2
    first = mul(left, high)
    return first[:rows] + first[rows:] + mul(left[:rows], low)


def near_face():
    return 1 - lax.axis_index("dam") % 2


def sec_face():
    return 3 - lax.axis_index("sec")


def pack_face(face, fmap, field, out):
    bdof = field.shape[2]
    for p in range(fmap.shape[3]):
        out[..., : field.shape[1], p * bdof : (p + 1) * bdof] = field[fmap[0, 0, face, p]]


def scatter_corners(cmap, correct, field):
    bdof = field.shape[2]
    where = [cmap[0, 0, n] for n in range(cmap.shape[2])]
    new = [
        field[b] + correct[:, n * bdof : (n + 1) * bdof] for n, b in enumerate(where)
    ]
    for b, value in zip(where, new):
        field[b] = value


def split_blocks(blocks, tiles_high, tiles_low):
    nblk, bdof = blocks.shape[:2]
    group = tiles_high.shape[1] // bdof
    tiles_high[...] = jnp.zeros_like(tiles_high)
    tiles_low[...] = jnp.zeros_like(tiles_low)
    for b in range(nblk):
        t, j = divmod(b, group)
        here = slice(j * bdof, (j + 1) * bdof)
        tiles_high[t, here, here], tiles_low[t, here, here] = halves(blocks[b])


def apply_blocks(field, tiles_high, tiles_low, left, base):
    nblk, ncol, bdof = field.shape
    group = tiles_high.shape[1] // bdof
    for b in range(nblk):
        t, j = divmod(b, group)
        here = slice(j * bdof, (j + 1) * bdof)
        left[t, :ncol, here], left[t, ncol:, here] = halves(field[b])
    for t in range(nblk // group):
        out = three_pass(dot, left[t], tiles_high[t], tiles_low[t])
        for j in range(group):
            base[t * group + j] = out[:, j * bdof : (j + 1) * bdof]


def pack_corners(pair, cmap, fmap, field, payload):
    ncol, bdof = field.shape[1:]
    at = fmap.shape[3] * bdof if pair else 0
    for n in range(cmap.shape[2]):
        payload[:ncol, at + n * bdof : at + (n + 1) * bdof] = field[cmap[0, 0, n]]


def own_correction(cmap, fmap, rows, base, payload):
    ncol, bdof = base.shape[1:]
    wide = cmap.shape[2] * bdof
    start = pl.multiple_of(lax.axis_index("sec") * wide, wide)
    own = stack(payload[:ncol, fmap.shape[3] * bdof :])
    correct = three_pass(dot_t, own, *halves(rows[:, pl.ds(start, wide)]))
    scatter_corners(cmap, correct, base)
    pack_face(sec_face(), fmap, base, payload)


def mark_corners(cmap, fmap, ncol, bdof, payload):
    payload[ncol:, :] = jnp.zeros_like(payload[ncol:, :])
    for n in range(cmap.shape[2]):
        for p in range(fmap.shape[3]):
            same = cmap[0, 0, n] == fmap[0, 0, sec_face(), p]
            payload[ncol + n : ncol + n + 1, p * bdof : (p + 1) * bdof] = jnp.full(
                (1, bdof), jnp.where(same, 1.0, 0.0), F32
            )


def stack(x):
    return jnp.concatenate(halves(x), axis=0)


def fetch(pairs, sems):
    copies = [
        pltpu.make_async_copy(source, target, sems.at[i])
        for i, (source, target) in enumerate(pairs)
    ]
    for copy in copies:
        copy.start()
    return [copy.wait for copy in copies]


def end_kernel(pair, cmap_in, fmap_in, base, rows, shares, marks, zout, *rest):
    *faces, cmap, fmap, sems = rest
    waits = fetch([(cmap_in, cmap), (fmap_in, fmap)], sems)
    nblk, ncol, bdof = base.shape
    ncorner, nface = cmap.shape[2], fmap.shape[3]
    wide = ncorner * bdof
    zout[...] = base[...]
    if pair:
        me = lax.axis_index("sec")
        at = nface * bdof
        start = pl.multiple_of((1 - me) * wide, wide)
        high, low = halves(rows[:, pl.ds(start, wide)])
        own = stack(shares[pl.ds(me, 1), :ncol, at:][0])
        other = stack(shares[pl.ds(1 - me, 1), :ncol, at:][0])
        theirs = three_pass(dot, own, high, low)
        correct = three_pass(dot_t, other, high, low)
        chunk = 2 * bdof
        twice = [
            jnp.concatenate([theirs[:, n * bdof : (n + 1) * bdof]] * 2, axis=1)
            for n in range(ncorner)
        ]
        for j in range(at // chunk):
            here = slice(j * chunk, (j + 1) * chunk)
            value = shares[pl.ds(1 - me, 1), :ncol, here][0]
            for n in range(ncorner):
                mark = marks[pl.ds(1 - me, 1), ncol + n : ncol + n + 1, here][0]
                value = value + mark * twice[n]
            faces[-1][:, here] = value
    else:
        correct = 0.0
        for s in range(shares.shape[0]):
            high, low = halves(rows[:, s * wide : (s + 1) * wide])
            correct = correct + three_pass(dot_t, stack(shares[s]), high, low)
    for wait in waits:
        wait()
    scatter_corners(cmap, correct, zout)
    near = near_face()
    pack_face(1 - near, fmap, zout, faces[0])
    pack_face(near, fmap, zout, faces[1])
    if not pair:
        near = 3 - lax.axis_index("sec") % 2
        pack_face(5 - near, fmap, zout, faces[2])
        pack_face(near, fmap, zout, faces[3])


def start_kernel(pair, *refs):
    load_in, mask_in, cmap_in, fmap_in, blocks_in, *others = refs[:9]
    rvec, base, payload, tiles_high, tiles_low, *copied = refs[9:20]
    load, mask, blocks, cmap, fmap, tall, short, left, sems = refs[20:]
    rows = copied[2]
    waits = fetch(
        [
            (load_in, load),
            (mask_in, mask),
            (blocks_in, blocks),
            (cmap_in, cmap),
            (fmap_in, fmap),
        ]
        + list(zip([cmap_in, fmap_in] + others, copied)),
        sems,
    )
    nblk, ncol, bdof = rvec.shape
    lanes_at = 128
    waits[0]()
    waits[1]()
    scale = mask[...].astype(F32)
    scale = jnp.concatenate([scale] * (lanes_at // ncol), axis=1)
    for j in range(load.shape[1] // lanes_at):
        here = slice(j * lanes_at, (j + 1) * lanes_at)
        tall[here, :] = (load[:, here] * scale).T
    for c in range(ncol):
        short[c * nblk : (c + 1) * nblk, :] = tall[pl.ds(c, bdof, stride=ncol), :].T
    for b in range(nblk):
        rvec[b] = short[pl.ds(b, ncol, stride=nblk), :]
    waits[2]()
    split_blocks(blocks, tiles_high, tiles_low)
    apply_blocks(rvec, tiles_high, tiles_low, left, base)
    waits[3]()
    waits[4]()
    pack_corners(pair, cmap, fmap, rvec, payload)
    for wait in waits[5:]:
        wait()
    if pair:
        own_correction(cmap, fmap, rows, base, payload)
        mark_corners(cmap, fmap, ncol, bdof, payload)


def local_kernel(cols_in, fmap_in, weights, capillary, field, stiff, out, left, cols, fmap, sems):
    nblk, ncol, bdof = field.shape
    waits = fetch([(cols_in, cols), (fmap_in, fmap)], sems)
    kept = stiff.shape[2] // bdof
    for b in range(nblk):
        left[b] = stack(field[b])
    waits[0]()
    group = 4
    for t in range(0, nblk, group):
        gathered = [
            jnp.concatenate([left[cols[k, 0, t + j]] for k in range(kept)], axis=1)
            for j in range(group)
        ]
        firsts = [g[:ncol] for g in gathered]
        seconds = [g[ncol:] for g in gathered]
        rows = stiff[t : t + group].reshape(group * bdof, kept * bdof)
        prod = three_pass(dot_t, jnp.concatenate(firsts + seconds, axis=0), *halves(rows))
        for j in range(group):
            out[t + j] = (
                prod[j * ncol : (j + 1) * ncol, j * bdof : (j + 1) * bdof]
                + capillary[t + j : t + j + 1, :] * field[t + j]
            )
    waits[1]()
    for face in range(4):
        where = [fmap[0, 0, face, p] for p in range(fmap.shape[3])]
        new = [
            out[b] + weights[face : face + 1, p * bdof : (p + 1) * bdof] * field[b]
            for p, b in enumerate(where)
        ]
        for b, value in zip(where, new):
            out[b] = value


def couple(fmap, weights, local, besides, out):
    bdof = local.shape[2]
    out[...] = local[...]
    near = near_face()
    met = [1 - near, near]
    if len(besides) == 3:
        met.append(sec_face())
    else:
        first = 3 - lax.axis_index("sec") % 2
        met += [5 - first, first]
    for face, beside in zip(met, besides):
        term = weights[pl.ds(face, 1), :] * beside[...]
        where = [fmap[0, 0, face, p] for p in range(fmap.shape[3])]
        new = [out[b] - term[:, p * bdof : (p + 1) * bdof] for p, b in enumerate(where)]
        for b, value in zip(where, new):
            out[b] = value


def lanes(first, second):
    return jnp.sum(first[...] * second[...], axis=0)


def image_kernel(
    pair, cmap_in, fmap_in, weights, local, rvec, zvec, tiles_high, tiles_low, rows, *rest
):
    count = 3 if pair else 4
    besides, rest = rest[:count], rest[count:]
    wout, sums, base, payload, cmap, fmap, left, sems = rest
    waits = fetch([(fmap_in, fmap), (cmap_in, cmap)], sems)
    sums[0] = lanes(rvec, zvec)
    waits[0]()
    couple(fmap, weights, local, besides, wout)
    sums[1] = lanes(zvec, wout)
    apply_blocks(wout, tiles_high, tiles_low, left, base)
    waits[1]()
    pack_corners(pair, cmap, fmap, wout, payload)
    if pair:
        own_correction(cmap, fmap, rows, base, payload)


def last_kernel(fmap_in, weights, local, wvec, mvec, sums, *rest):
    *besides, nout, totals, fmap, sems = rest
    (wait,) = fetch([(fmap_in, fmap)], sems)
    third = lanes(wvec, mvec)
    wait()
    couple(fmap, weights, local, besides, nout)
    parts = jnp.concatenate([sums[0], sums[1], third, lanes(mvec, nout)], axis=0)
    totals[...] = lax.dot_general(
        jnp.ones((1, parts.shape[1]), F32),
        parts,
        (((1,), (1,)), ((), ())),
        precision=lax.Precision.HIGHEST,
        preferred_element_type=F32,
    )


def finish_kernel(shares, rvec, zvec, wvec, mvec, nvec, sol, res, short, tall):
    nblk, ncol, bdof = rvec.shape
    width = 4 * ncol
    total = jnp.sum(shares[...], axis=0, keepdims=True)
    eye = lax.broadcasted_iota(jnp.int32, (width, width), 0) == lax.broadcasted_iota(
        jnp.int32, (width, width), 1
    )
    column = jnp.sum(jnp.where(eye, total, 0.0), axis=1, keepdims=True)
    gamma, delta, mu, nu = [column[q * ncol : (q + 1) * ncol] for q in range(4)]
    alpha = gamma / delta
    gnew = gamma - 2.0 * alpha * delta + alpha * alpha * mu
    grow = 1.0 + gnew / gamma
    dnew = grow * grow * delta - 2.0 * alpha * grow * mu + alpha * alpha * nu
    anew = gnew / dnew
    both = alpha + anew * grow
    second = anew * alpha
    both_at = 2 * nblk
    for b in range(nblk):
        short[pl.ds(b, ncol, stride=both_at), :] = both * zvec[b] - second * mvec[b]
        short[pl.ds(nblk + b, ncol, stride=both_at), :] = (
            rvec[b] - both * wvec[b] + second * nvec[b]
        )
    for c in range(ncol):
        tall[pl.ds(c, bdof, stride=ncol), :] = short[c * both_at : (c + 1) * both_at, :].T
    lanes_at = 128
    for j in range(sol.shape[1] // lanes_at):
        here = slice(j * lanes_at, (j + 1) * lanes_at)
        flat = tall[here, :].T
        sol[:, here] = flat[:nblk]
        res[:, here] = flat[nblk:]


def call(kernel, outs, scratch, args, space=pltpu.VMEM):
    vmem = pl.BlockSpec(memory_space=pltpu.VMEM)
    if space != pltpu.VMEM:
        args = [pltpu.with_memory_space_constraint(arg, space) for arg in args]
    return pl.pallas_call(
        kernel,
        out_shape=outs,
        in_specs=[pl.BlockSpec(memory_space=space)] * len(args),
        out_specs=jax.tree.map(lambda _: vmem, outs),
        scratch_shapes=scratch,
        compiler_params=pltpu.CompilerParams(vmem_limit_bytes=VMEM_LIMIT),
    )(*args)


def everywhere(values):
    total = lax.axis_size("dam") * lax.axis_size("sec")
    copies = jnp.broadcast_to(values[None], (total,) + values.shape)
    return lax.all_to_all(copies, ("dam", "sec"), split_axis=0, concat_axis=0)


def exchange(sends, axis):
    size = lax.axis_size(axis)
    got = []
    for first, send in zip((1, 0), sends):
        pairs = [(i, i + 1) for i in range(first, size - 1, 2)]
        got.append(lax.ppermute(send, axis, pairs + [(j, i) for i, j in pairs]))
    return got


def shards(
    segment_load,
    segment_mask,
    stiffness,
    block_cols,
    capillary,
    dirichlet_blocks,
    face_map,
    face_weight,
    corner_map,
    coarse_inverse,
):
    nblk, bdof = capillary.shape[2:]
    ncol = segment_load.shape[-1] // bdof
    nface = face_map.shape[3]
    ncorner = corner_map.shape[2]
    size = nblk * bdof
    pair = lax.axis_size("sec") == 2
    cols = jnp.transpose(block_cols[0], (2, 0, 1))
    tang, weights = capillary[0, 0], face_weight[0, 0]
    blocks, rows = dirichlet_blocks[0, 0], coarse_inverse[0]

    def shape(*dims, dtype=F32):
        return jax.ShapeDtypeStruct(dims, dtype)

    def like(array):
        return shape(*array.shape, dtype=array.dtype)

    def index(array):
        return pltpu.SMEM(array.shape, array.dtype)

    def sems(count):
        return pltpu.SemaphoreType.DMA((count,))

    field = shape(nblk, ncol, bdof)
    face = shape(ncol, nface * bdof)
    group = ncorner * bdof
    tiles = shape(size // group, group, group, dtype=BF16)
    halved = pltpu.VMEM((size // group, 2 * ncol, group), BF16)
    lane = group + nface * bdof if pair else group
    marked = ncol + 8 if pair else ncol
    faces_met = 3 if pair else 4

    load, mask = segment_load[0, 0], segment_mask[0, 0]
    copied = (corner_map, face_map, rows, cols, weights, tang)
    rvec, base, payload, high, low, cmap, fmap, rows, cols, weights, tang = call(
        functools.partial(start_kernel, pair),
        (field, field, shape(marked, lane), tiles, tiles)
        + tuple(like(a) for a in copied),
        [
            pltpu.VMEM(load.shape, load.dtype),
            pltpu.VMEM(mask.shape, mask.dtype),
            pltpu.VMEM(blocks.shape, blocks.dtype),
            index(corner_map),
            index(face_map),
            pltpu.VMEM((bdof * ncol, nblk), F32),
            pltpu.VMEM((ncol * nblk, bdof), F32),
            halved,
            sems(11),
        ],
        (load, mask, corner_map, face_map, blocks) + copied[2:],
        pltpu.HBM,
    )
    maps = [index(cmap), index(fmap)]

    def finish(base, shares, marks):
        vec, *faces = call(
            functools.partial(end_kernel, pair),
            (field,) + (face,) * faces_met,
            maps + [sems(2)],
            (cmap, fmap, base, rows, shares, marks),
        )
        besides = exchange(faces[:2], "dam")
        besides += faces[2:] if pair else exchange(faces[2:], "sec")
        return vec, besides

    def local(vec):
        return call(
            local_kernel,
            field,
            [pltpu.VMEM((nblk, 2 * ncol, bdof), BF16), index(cols), index(fmap), sems(2)],
            (cols, fmap, weights, tang, vec, stiffness[0, 0]),
        )

    marks = lax.all_gather(payload, "sec")
    zvec, besides = finish(base, marks, marks)
    wvec, sums, base, payload = call(
        functools.partial(image_kernel, pair),
        (field, shape(2, ncol, bdof), field, shape(ncol, lane)),
        maps + [halved, sems(2)],
        (cmap, fmap, weights, local(zvec), rvec, zvec, high, low, rows, *besides),
    )
    mvec, besides = finish(base, lax.all_gather(payload, "sec"), marks)
    nvec, totals = call(
        last_kernel,
        (field, shape(1, 4 * ncol)),
        [index(fmap), sems(1)],
        (fmap, weights, local(mvec), wvec, mvec, sums, *besides),
    )
    sol, res = call(
        finish_kernel,
        (shape(nblk, bdof * ncol),) * 2,
        [pltpu.VMEM((ncol * 2 * nblk, bdof), F32), pltpu.VMEM((bdof * ncol, 2 * nblk), F32)],
        (everywhere(totals[0]), rvec, zvec, wvec, mvec, nvec),
    )
    return sol[None, None], res[None, None]


def solution(mesh):
    placed = (
        P("dam", "sec", None, None),
        P("dam", "sec", None, None),
        P("dam", "sec", None, None, None),
        P("dam", "sec", None, None),
        P("dam", "sec", None, None),
        P("dam", "sec", None, None, None),
        P("dam", "sec", None, None),
        P("dam", "sec", None, None),
        P("dam", "sec", None),
        P("dam", "sec", None),
    )
    return jax.shard_map(
        shards,
        mesh=mesh,
        in_specs=placed,
        out_specs=(P("dam", "sec", None, None), P("dam", "sec", None, None)),
        check_vma=False,
    )
```

```python
import functools

import jax
import jax.numpy as jnp
from jax import lax
from jax.experimental import pallas as pl
from jax.experimental.pallas import tpu as pltpu
from jax.sharding import PartitionSpec as P

F32 = jnp.float32
BF16 = jnp.bfloat16
VMEM_LIMIT = 16 * 1024 * 1024
LANES = 128


def halves(x):
    high = x.astype(BF16)
    return high, (x - high.astype(F32)).astype(BF16)


def stack(x):
    return jnp.concatenate(halves(x), axis=0)


def dot_t(a, b):
    return lax.dot_general(a, b, (((1,), (1,)), ((), ())), preferred_element_type=F32)


def dot(a, b):
    return lax.dot_general(a, b, (((1,), (0,)), ((), ())), preferred_element_type=F32)


def three_pass(mul, left, high, low):
    rows = left.shape[0] // 2
    first = mul(left, high)
    return first[:rows] + first[rows:] + mul(left[:rows], low)


def fetch(pairs, sems):
    copies = [
        pltpu.make_async_copy(source, target, sems.at[i])
        for i, (source, target) in enumerate(pairs)
    ]
    for copy in copies:
        copy.start()
    return [copy.wait for copy in copies]


def face_order(pair):
    near = 1 - lax.axis_index("dam") % 2
    across = 3 - lax.axis_index("sec") % 2
    return [1 - near, near] + ([across, 5 - across] if pair else [5 - across, across])


def listed(index):
    value = index[...]
    return [[value[i, j] for j in range(value.shape[1])] for i in range(value.shape[0])]


def pack(field, where, out, at=0):
    ncol, bdof = field.shape[1:]
    for p, b in enumerate(where):
        out[:ncol, at + p * bdof : at + (p + 1) * bdof] = field[b]


def add_pieces(field, where, piece):
    new = [field[b] + piece(p, b) for p, b in enumerate(where)]
    for b, value in zip(where, new):
        field[b] = value


def lane_piece(x, p, bdof):
    return x[:, p * bdof : (p + 1) * bdof]


def split_blocks(blocks, tiles_high, tiles_low):
    nblk, bdof = blocks.shape[:2]
    group = tiles_high.shape[1] // bdof
    for b in range(nblk):
        t, j = divmod(b, group)
        here = slice(j * bdof, (j + 1) * bdof)
        tiles_high[t, here, here], tiles_low[t, here, here] = halves(blocks[b])


def apply_blocks(field, tiles_high, tiles_low, left, base):
    nblk, ncol, bdof = field.shape
    group = tiles_high.shape[1] // bdof
    for b in range(nblk):
        t, j = divmod(b, group)
        here = slice(j * bdof, (j + 1) * bdof)
        left[t, :ncol, here], left[t, ncol:, here] = halves(field[b])
    for t in range(nblk // group):
        out = three_pass(dot, left[t], tiles_high[t], tiles_low[t])
        for j in range(group):
            base[t * group + j] = lane_piece(out, j, bdof)


def offer(pair, corners, across, field, rows, base, payload):
    bdof = field.shape[2]
    if not pair:
        pack(field, corners, payload)
        return
    wide = len(corners) * bdof
    at = payload.shape[1] - wide
    me = lax.axis_index("sec")
    own = stack(jnp.concatenate([field[b] for b in corners], axis=1))
    mine = pl.multiple_of(me * wide, wide)
    other = pl.multiple_of((1 - me) * wide, wide)
    correct = three_pass(dot_t, own, *halves(rows[:, pl.ds(mine, wide)]))
    payload[: field.shape[1], at:] = three_pass(dot, own, *halves(rows[:, pl.ds(other, wide)]))
    add_pieces(base, corners, lambda n, b: lane_piece(correct, n, bdof))
    pack(base, across, payload)


def end_kernel(pair, cmap, met, base, rows, shares, marks, zout, *faces):
    nblk, ncol, bdof = base.shape
    (corners,) = listed(cmap)
    where = listed(met)
    wide = len(corners) * bdof
    zout[...] = base[...]
    if pair:
        me = lax.axis_index("sec")
        at = len(where[0]) * bdof
        correct = shares[pl.ds(1 - me, 1), :ncol, at:][0]
        theirs = shares[pl.ds(me, 1), :ncol, at:][0]
        chunk = 2 * bdof
        twice = [
            jnp.concatenate([lane_piece(theirs, n, bdof)] * 2, axis=1)
            for n in range(len(corners))
        ]
        for j in range(at // chunk):
            here = slice(j * chunk, (j + 1) * chunk)
            value = shares[pl.ds(1 - me, 1), :ncol, here][0]
            for n in range(len(corners)):
                mark = marks[pl.ds(1 - me, 1), ncol + n : ncol + n + 1, here][0]
                value = value + mark * twice[n]
            faces[-1][:, here] = value
    else:
        correct = 0.0
        for s in range(shares.shape[0]):
            high, low = halves(rows[:, s * wide : (s + 1) * wide])
            correct = correct + three_pass(dot_t, stack(shares[s]), high, low)
    add_pieces(zout, corners, lambda n, b: lane_piece(correct, n, bdof))
    for blocks, out in zip(where, faces[: 2 if pair else 4]):
        pack(zout, blocks, out)


def start_kernel(pair, *refs):
    load_in, mask_in, cmap_in, fmap_in, blocks_in, rows_in, cols_in, weights_in, tang_in = refs[:9]
    rvec, base, payload, tiles_high, tiles_low, cmap_out, met, wmet, rows, cols, tang = refs[9:20]
    load, mask, blocks, cmap, cmap_row, fmap, fmap_rows, weights, tall, short, left, sems = refs[20:]
    waits = fetch(
        [
            (load_in, load),
            (mask_in, mask),
            (cmap_in, cmap),
            (fmap_in, fmap),
            (blocks_in, blocks),
            (rows_in, rows),
            (cmap_in, cmap_row),
            (fmap_in, fmap_rows),
            (weights_in, weights),
            (cols_in, cols),
            (tang_in, tang),
        ],
        sems,
    )
    nblk, ncol, bdof = rvec.shape
    order = face_order(pair)
    tiles_high[...] = jnp.zeros_like(tiles_high)
    tiles_low[...] = jnp.zeros_like(tiles_low)
    waits[2]()
    waits[3]()
    corners = [cmap[0, 0, n] for n in range(cmap.shape[2])]
    across = [fmap[0, 0, order[2], p] for p in range(fmap.shape[3])]
    if pair:
        payload[ncol:, :] = jnp.zeros_like(payload[ncol:, :])
        for n, corner in enumerate(corners):
            for p, b in enumerate(across):
                payload[ncol + n : ncol + n + 1, p * bdof : (p + 1) * bdof] = jnp.full(
                    (1, bdof), jnp.where(corner == b, 1.0, 0.0), F32
                )
    waits[0]()
    waits[1]()
    scale = mask[...].astype(F32)
    scale = jnp.concatenate([scale] * (LANES // ncol), axis=1)
    for j in range(load.shape[1] // LANES):
        here = slice(j * LANES, (j + 1) * LANES)
        tall[here, :] = (load[:, here] * scale).T
    for c in range(ncol):
        short[c * nblk : (c + 1) * nblk, :] = tall[pl.ds(c, bdof, stride=ncol), :].T
    for b in range(nblk):
        rvec[b] = short[pl.ds(b, ncol, stride=nblk), :]
    waits[4]()
    split_blocks(blocks, tiles_high, tiles_low)
    apply_blocks(rvec, tiles_high, tiles_low, left, base)
    for wait in waits[5:]:
        wait()
    offer(pair, corners, across, rvec, rows, base, payload)
    cmap_out[...] = cmap_row[0]
    for i, face in enumerate(order):
        met[i : i + 1, :] = fmap_rows[0, 0, pl.ds(face, 1), :]
        wmet[i : i + 1, :] = weights[pl.ds(face, 1), :]


def flatten(block, nblk, ncol, bdof, short, tall, out):
    for b in range(nblk):
        short[pl.ds(b, ncol, stride=nblk), :] = block(b)
    for c in range(ncol):
        tall[pl.ds(c, bdof, stride=ncol), :] = short[c * nblk : (c + 1) * nblk, :].T
    for j in range(out.shape[1] // LANES):
        here = slice(j * LANES, (j + 1) * LANES)
        out[:, here] = tall[here, :].T


def local_kernel(cols_in, met, weights, capillary, field, stiff, out, flat, *scratch):
    left, short, tall, cols, sems = scratch
    nblk, ncol, bdof = field.shape
    (wait,) = fetch([(cols_in, cols)], sems)
    where = listed(met)
    flatten(lambda b: field[b], nblk, ncol, bdof, short, tall, flat)
    kept = stiff.shape[2] // bdof
    for b in range(nblk):
        left[b] = stack(field[b])
    wait()
    group = 4
    for t in range(0, nblk, group):
        gathered = [
            jnp.concatenate([left[cols[k, 0, t + j]] for k in range(kept)], axis=1)
            for j in range(group)
        ]
        firsts = [g[:ncol] for g in gathered]
        seconds = [g[ncol:] for g in gathered]
        rows = stiff[t : t + group].reshape(group * bdof, kept * bdof)
        prod = three_pass(dot_t, jnp.concatenate(firsts + seconds, axis=0), *halves(rows))
        for j in range(group):
            out[t + j] = (
                lane_piece(prod[j * ncol : (j + 1) * ncol], j, bdof)
                + capillary[t + j : t + j + 1, :] * field[t + j]
            )
    for i, blocks in enumerate(where):
        row = weights[i : i + 1, :]
        add_pieces(out, blocks, lambda p, b: lane_piece(row, p, bdof) * field[b])


def couple(met, weights, local, besides, out):
    bdof = local.shape[2]
    where = listed(met)
    out[...] = local[...]
    for i, beside in enumerate(besides):
        term = weights[i : i + 1, :] * beside[...]
        add_pieces(out, where[i], lambda p, b: -lane_piece(term, p, bdof))
    return where


def lanes(first, second):
    return jnp.sum(first[...] * second[...], axis=0)


def image_kernel(
    pair, cmap, met, weights, local, rvec, zvec, tiles_high, tiles_low, rows, *rest
):
    count = 3 if pair else 4
    besides, (wout, sums, base, payload, left) = rest[:count], rest[count:]
    (corners,) = listed(cmap)
    where = couple(met, weights, local, besides, wout)
    apply_blocks(wout, tiles_high, tiles_low, left, base)
    offer(pair, corners, where[2], wout, rows, base, payload)
    sums[0] = lanes(rvec, zvec)
    sums[1] = lanes(zvec, wout)


def last_kernel(met, weights, local, wvec, mvec, sums, *rest):
    *besides, nout, totals = rest
    couple(met, weights, local, besides, nout)
    parts = jnp.concatenate(
        [sums[0], sums[1], lanes(wvec, mvec), lanes(mvec, nout)], axis=0
    )
    totals[...] = lax.dot_general(
        jnp.ones((1, parts.shape[1]), F32),
        parts,
        (((1,), (1,)), ((), ())),
        precision=lax.Precision.HIGHEST,
        preferred_element_type=F32,
    )


def finish_kernel(shares, rvec, wvec, nvec, zflat, mflat, sol, res, short, tall):
    nblk, ncol, bdof = rvec.shape
    total = jnp.sum(shares[...], axis=0, keepdims=True)
    gamma, delta, mu, nu = [total[:, q * ncol : (q + 1) * ncol] for q in range(4)]
    alpha = gamma / delta
    gnew = gamma - 2.0 * alpha * delta + alpha * alpha * mu
    grow = 1.0 + gnew / gamma
    dnew = grow * grow * delta - 2.0 * alpha * grow * mu + alpha * alpha * nu
    anew = gnew / dnew
    both = alpha + anew * grow
    second = anew * alpha
    eye = lax.broadcasted_iota(jnp.int32, (ncol, ncol), 0) == lax.broadcasted_iota(
        jnp.int32, (ncol, ncol), 1
    )
    down = [
        jnp.sum(jnp.where(eye, x, 0.0), axis=1, keepdims=True) for x in (both, second)
    ]
    flatten(
        lambda b: rvec[b] - down[0] * wvec[b] + down[1] * nvec[b],
        nblk,
        ncol,
        bdof,
        short,
        tall,
        res,
    )
    along = [jnp.concatenate([x] * (LANES // ncol), axis=1) for x in (both, second)]
    for j in range(sol.shape[1] // LANES):
        here = slice(j * LANES, (j + 1) * LANES)
        sol[:, here] = along[0] * zflat[:, here] - along[1] * mflat[:, here]


def call(kernel, outs, scratch, args, space=pltpu.VMEM):
    vmem = pl.BlockSpec(memory_space=pltpu.VMEM)
    if space != pltpu.VMEM:
        args = [pltpu.with_memory_space_constraint(arg, space) for arg in args]
    return pl.pallas_call(
        kernel,
        out_shape=outs,
        in_specs=[pl.BlockSpec(memory_space=space)] * len(args),
        out_specs=jax.tree.map(lambda _: vmem, outs),
        scratch_shapes=scratch,
        compiler_params=pltpu.CompilerParams(vmem_limit_bytes=VMEM_LIMIT),
    )(*args)


def everywhere(values):
    total = lax.axis_size("dam") * lax.axis_size("sec")
    copies = jnp.broadcast_to(values[None], (total,) + values.shape)
    return lax.all_to_all(copies, ("dam", "sec"), split_axis=0, concat_axis=0)


def exchange(sends, axis):
    size = lax.axis_size(axis)
    got = []
    for first, send in zip((1, 0), sends):
        pairs = [(i, i + 1) for i in range(first, size - 1, 2)]
        got.append(lax.ppermute(send, axis, pairs + [(j, i) for i, j in pairs]))
    return got


def shards(
    segment_load,
    segment_mask,
    stiffness,
    block_cols,
    capillary,
    dirichlet_blocks,
    face_map,
    face_weight,
    corner_map,
    coarse_inverse,
):
    nblk, bdof = capillary.shape[2:]
    ncol = segment_load.shape[-1] // bdof
    nface = face_map.shape[3]
    ncorner = corner_map.shape[2]
    size = nblk * bdof
    pair = lax.axis_size("sec") == 2
    load, mask = segment_load[0, 0], segment_mask[0, 0]
    cols = jnp.transpose(block_cols[0], (2, 0, 1))
    tang, weights = capillary[0, 0], face_weight[0, 0]
    blocks, rows = dirichlet_blocks[0, 0], coarse_inverse[0]

    def shape(*dims, dtype=F32):
        return jax.ShapeDtypeStruct(dims, dtype)

    def like(array):
        return shape(*array.shape, dtype=array.dtype)

    def hold(array):
        return pltpu.VMEM(array.shape, array.dtype)

    def index(array):
        return pltpu.SMEM(array.shape, array.dtype)

    def sems(count):
        return pltpu.SemaphoreType.DMA((count,))

    field = shape(nblk, ncol, bdof)
    flat = shape(nblk, bdof * ncol)
    face = shape(ncol, nface * bdof)
    group = ncorner * bdof
    tiles = shape(size // group, group, group, dtype=BF16)
    halved = pltpu.VMEM((size // group, 2 * ncol, group), BF16)
    relayout = [pltpu.VMEM((ncol * nblk, bdof), F32), pltpu.VMEM((bdof * ncol, nblk), F32)]
    lane = group + nface * bdof if pair else group
    marked = ncol + 8 if pair else ncol

    rvec, base, payload, high, low, cmap, met, weights, rows, cols, tang = call(
        functools.partial(start_kernel, pair),
        (field, field, shape(marked, lane), tiles, tiles)
        + (shape(1, ncorner, dtype=jnp.int32), shape(4, nface, dtype=jnp.int32))
        + tuple(like(a) for a in (weights, rows, cols, tang)),
        [
            hold(load),
            hold(mask),
            hold(blocks),
            index(corner_map),
            hold(corner_map),
            index(face_map),
            hold(face_map),
            hold(weights),
            relayout[1],
            relayout[0],
            halved,
            sems(11),
        ],
        (load, mask, corner_map, face_map, blocks, rows, cols, weights, tang),
        pltpu.HBM,
    )

    def finish(base, shares, marks):
        vec, *faces = call(
            functools.partial(end_kernel, pair),
            (field,) + (face,) * (3 if pair else 4),
            [],
            (cmap, met, base, rows, shares, marks),
        )
        besides = exchange(faces[:2], "dam")
        besides += faces[2:] if pair else exchange(faces[2:], "sec")
        return vec, besides

    def local(vec):
        return call(
            local_kernel,
            (field, flat),
            [pltpu.VMEM((nblk, 2 * ncol, bdof), BF16)] + relayout + [index(cols), sems(1)],
            (cols, met, weights, tang, vec, stiffness[0, 0]),
        )

    marks = lax.all_gather(payload, "sec")
    zvec, besides = finish(base, marks, marks)
    part, zflat = local(zvec)
    wvec, sums, base, payload = call(
        functools.partial(image_kernel, pair),
        (field, shape(2, ncol, bdof), field, shape(ncol, lane)),
        [halved],
        (cmap, met, weights, part, rvec, zvec, high, low, rows, *besides),
    )
    mvec, besides = finish(base, lax.all_gather(payload, "sec"), marks)
    part, mflat = local(mvec)
    nvec, totals = call(
        last_kernel,
        (field, shape(1, 4 * ncol)),
        [],
        (met, weights, part, wvec, mvec, sums, *besides),
    )
    sol, res = call(
        finish_kernel,
        (flat, flat),
        relayout,
        (everywhere(totals[0]), rvec, wvec, nvec, zflat, mflat),
    )
    return sol[None, None], res[None, None]


def solution(mesh):
    placed = (
        P("dam", "sec", None, None),
        P("dam", "sec", None, None),
        P("dam", "sec", None, None, None),
        P("dam", "sec", None, None),
        P("dam", "sec", None, None),
        P("dam", "sec", None, None, None),
        P("dam", "sec", None, None),
        P("dam", "sec", None, None),
        P("dam", "sec", None),
        P("dam", "sec", None),
    )
    return jax.shard_map(
        shards,
        mesh=mesh,
        in_specs=placed,
        out_specs=(P("dam", "sec", None, None), P("dam", "sec", None, None)),
        check_vma=False,
    )
```

```python
import functools

import jax
import jax.numpy as jnp
from jax import lax
from jax.experimental import pallas as pl
from jax.experimental.pallas import tpu as pltpu
from jax.sharding import PartitionSpec as P

F32 = jnp.float32
BF16 = jnp.bfloat16
VMEM_LIMIT = 16 * 1024 * 1024
LANES = 128


def halves(x):
    high = x.astype(BF16)
    return high, (x - high.astype(F32)).astype(BF16)


def stack(x):
    return jnp.concatenate(halves(x), axis=0)


def dot_t(a, b):
    return lax.dot_general(a, b, (((1,), (1,)), ((), ())), preferred_element_type=F32)


def dot(a, b):
    return lax.dot_general(a, b, (((1,), (0,)), ((), ())), preferred_element_type=F32)


def three_pass(mul, left, high, low):
    rows = left.shape[0] // 2
    first = mul(left, high)
    return first[:rows] + first[rows:] + mul(left[:rows], low)


def fetch(pairs, sems):
    copies = [
        pltpu.make_async_copy(source, target, sems.at[i])
        for i, (source, target) in enumerate(pairs)
    ]
    for copy in copies:
        copy.start()
    return [copy.wait for copy in copies]


def face_order(pair):
    near = 1 - lax.axis_index("dam") % 2
    across = 3 - lax.axis_index("sec") % 2
    return [1 - near, near] + ([across, 5 - across] if pair else [5 - across, across])


def listed(index):
    value = index[...]
    return [[value[i, j] for j in range(value.shape[1])] for i in range(value.shape[0])]


def pack(field, where, out, at=0):
    ncol, bdof = field.shape[1:]
    for p, b in enumerate(where):
        out[:ncol, at + p * bdof : at + (p + 1) * bdof] = field[b]


def add_pieces(field, where, piece):
    new = [field[b] + piece(p, b) for p, b in enumerate(where)]
    for b, value in zip(where, new):
        field[b] = value


def lane_piece(x, p, bdof):
    return x[:, p * bdof : (p + 1) * bdof]


def split_blocks(blocks, tiles_high, tiles_low):
    nblk, bdof = blocks.shape[:2]
    group = tiles_high.shape[1] // bdof
    for b in range(nblk):
        t, j = divmod(b, group)
        here = slice(j * bdof, (j + 1) * bdof)
        tiles_high[t, here, here], tiles_low[t, here, here] = halves(blocks[b])


def apply_blocks(field, tiles_high, tiles_low, left, base):
    nblk, ncol, bdof = field.shape
    group = tiles_high.shape[1] // bdof
    for b in range(nblk):
        t, j = divmod(b, group)
        here = slice(j * bdof, (j + 1) * bdof)
        left[t, :ncol, here], left[t, ncol:, here] = halves(field[b])
    for t in range(nblk // group):
        out = three_pass(dot, left[t], tiles_high[t], tiles_low[t])
        for j in range(group):
            base[t * group + j] = lane_piece(out, j, bdof)


def offer(pair, corners, across, field, rows, base, payload):
    bdof = field.shape[2]
    if not pair:
        pack(field, corners, payload)
        return
    wide = len(corners) * bdof
    at = payload.shape[1] - wide
    me = lax.axis_index("sec")
    own = stack(jnp.concatenate([field[b] for b in corners], axis=1))
    mine = pl.multiple_of(me * wide, wide)
    other = pl.multiple_of((1 - me) * wide, wide)
    correct = three_pass(dot_t, own, *halves(rows[:, pl.ds(mine, wide)]))
    payload[: field.shape[1], at:] = three_pass(dot, own, *halves(rows[:, pl.ds(other, wide)]))
    add_pieces(base, corners, lambda n, b: lane_piece(correct, n, bdof))
    pack(base, across, payload)


def end_kernel(pair, cmap, met, base, rows, shares, marks, zout, *faces):
    nblk, ncol, bdof = base.shape
    (corners,) = listed(cmap)
    where = listed(met)
    wide = len(corners) * bdof
    zout[...] = base[...]
    if pair:
        me = lax.axis_index("sec")
        at = len(where[0]) * bdof
        correct = shares[pl.ds(1 - me, 1), :ncol, at:][0]
        theirs = shares[pl.ds(me, 1), :ncol, at:][0]
        chunk = 2 * bdof
        twice = [
            jnp.concatenate([lane_piece(theirs, n, bdof)] * 2, axis=1)
            for n in range(len(corners))
        ]
        for j in range(at // chunk):
            here = slice(j * chunk, (j + 1) * chunk)
            value = shares[pl.ds(1 - me, 1), :ncol, here][0]
            for n in range(len(corners)):
                mark = marks[pl.ds(1 - me, 1), ncol + n : ncol + n + 1, here][0]
                value = value + mark * twice[n]
            faces[-1][:, here] = value
    else:
        correct = 0.0
        for s in range(shares.shape[0]):
            high, low = halves(rows[:, s * wide : (s + 1) * wide])
            correct = correct + three_pass(dot_t, stack(shares[s]), high, low)
    add_pieces(zout, corners, lambda n, b: lane_piece(correct, n, bdof))
    for blocks, out in zip(where, faces[: 2 if pair else 4]):
        pack(zout, blocks, out)


def start_kernel(pair, *refs):
    load_in, mask_in, cmap_in, fmap_in, blocks_in, rows_in, cols_in, weights_in, tang_in = refs[:9]
    rvec, base, payload, tiles_high, tiles_low, cmap_out, met, wmet, rows, cols, tang = refs[9:20]
    load, mask, blocks, cmap, cmap_row, fmap, fmap_rows, weights, tall, short, left, sems = refs[20:]
    waits = fetch(
        [
            (load_in, load),
            (mask_in, mask),
            (cmap_in, cmap),
            (fmap_in, fmap),
            (blocks_in, blocks),
            (rows_in, rows),
            (cmap_in, cmap_row),
            (fmap_in, fmap_rows),
            (weights_in, weights),
            (cols_in, cols),
            (tang_in, tang),
        ],
        sems,
    )
    nblk, ncol, bdof = rvec.shape
    order = face_order(pair)
    tiles_high[...] = jnp.zeros_like(tiles_high)
    tiles_low[...] = jnp.zeros_like(tiles_low)
    waits[2]()
    waits[3]()
    corners = [cmap[0, 0, n] for n in range(cmap.shape[2])]
    across = [fmap[0, 0, order[2], p] for p in range(fmap.shape[3])]
    if pair:
        payload[ncol:, :] = jnp.zeros_like(payload[ncol:, :])
        for n, corner in enumerate(corners):
            for p, b in enumerate(across):
                payload[ncol + n : ncol + n + 1, p * bdof : (p + 1) * bdof] = jnp.full(
                    (1, bdof), jnp.where(corner == b, 1.0, 0.0), F32
                )
    waits[0]()
    waits[1]()
    scale = mask[...].astype(F32)
    scale = jnp.concatenate([scale] * (LANES // ncol), axis=1)
    for j in range(load.shape[1] // LANES):
        here = slice(j * LANES, (j + 1) * LANES)
        tall[here, :] = (load[:, here] * scale).T
    for c in range(ncol):
        short[c * nblk : (c + 1) * nblk, :] = tall[pl.ds(c, bdof, stride=ncol), :].T
    for b in range(nblk):
        rvec[b] = short[pl.ds(b, ncol, stride=nblk), :]
    waits[4]()
    split_blocks(blocks, tiles_high, tiles_low)
    apply_blocks(rvec, tiles_high, tiles_low, left, base)
    for wait in waits[5:]:
        wait()
    offer(pair, corners, across, rvec, rows, base, payload)
    cmap_out[...] = cmap_row[0]
    for i, face in enumerate(order):
        met[i : i + 1, :] = fmap_rows[0, 0, pl.ds(face, 1), :]
        wmet[i : i + 1, :] = weights[pl.ds(face, 1), :]


def flatten(block, nblk, ncol, bdof, out):
    both = jnp.concatenate([stack(block(b)) for b in range(nblk)], axis=0)
    rows, span = 2 * nblk * ncol, 2 * LANES

    def iota(shape, dim):
        return lax.broadcasted_iota(jnp.int32, shape, dim)

    first = iota((nblk, rows), 0) * (2 * ncol)
    offset = iota((nblk, rows), 1) - first
    gather = jnp.where((offset >= 0) & (offset < 2 * ncol), 1.0, 0.0).astype(BF16)
    column = iota((ncol, span), 1) & (ncol - 1)
    keep = column == iota((ncol, span), 0)
    keep = jnp.concatenate([keep] * (2 * nblk), axis=0)
    for j in range(out.shape[1] // span):
        here = slice(j * span, (j + 1) * span)
        offset = iota((bdof, span), 1) + j * span - iota((bdof, span), 0) * ncol
        spread = jnp.where((offset >= 0) & (offset < ncol), 1.0, 0.0).astype(BF16)
        wide = jnp.where(keep, dot(both, spread), 0.0).astype(BF16)
        out[:, here] = dot(gather, wide)


def local_kernel(first, cols_in, met, weights, capillary, field, stiff, out, flat, *scratch):
    copies = [(cols_in, scratch[-2])]
    if first:
        copies.append((stiff, scratch[0]))
        stiff = scratch[0]
    left, cols, sems = scratch[-3:]
    nblk, ncol, bdof = field.shape
    waits = fetch(copies, sems)
    where = listed(met)
    flatten(lambda b: field[b], nblk, ncol, bdof, flat)
    kept = stiff.shape[2] // bdof
    for b in range(nblk):
        left[b] = stack(field[b])
    for wait in waits:
        wait()
    group = 4
    for t in range(0, nblk, group):
        gathered = [
            jnp.concatenate([left[cols[k, 0, t + j]] for k in range(kept)], axis=1)
            for j in range(group)
        ]
        firsts = [g[:ncol] for g in gathered]
        seconds = [g[ncol:] for g in gathered]
        rows = stiff[t : t + group].reshape(group * bdof, kept * bdof)
        prod = three_pass(dot_t, jnp.concatenate(firsts + seconds, axis=0), *halves(rows))
        for j in range(group):
            out[t + j] = (
                lane_piece(prod[j * ncol : (j + 1) * ncol], j, bdof)
                + capillary[t + j : t + j + 1, :] * field[t + j]
            )
    for i, blocks in enumerate(where):
        row = weights[i : i + 1, :]
        add_pieces(out, blocks, lambda p, b: lane_piece(row, p, bdof) * field[b])


def couple(met, weights, local, besides, out):
    bdof = local.shape[2]
    where = listed(met)
    out[...] = local[...]
    for i, beside in enumerate(besides):
        term = weights[i : i + 1, :] * beside[...]
        add_pieces(out, where[i], lambda p, b: -lane_piece(term, p, bdof))
    return where


def lanes(first, second):
    return jnp.sum(first[...] * second[...], axis=0)


def image_kernel(
    pair, cmap, met, weights, local, rvec, zvec, tiles_high, tiles_low, rows, *rest
):
    count = 3 if pair else 4
    besides, (wout, sums, base, payload, left) = rest[:count], rest[count:]
    (corners,) = listed(cmap)
    where = couple(met, weights, local, besides, wout)
    apply_blocks(wout, tiles_high, tiles_low, left, base)
    offer(pair, corners, where[2], wout, rows, base, payload)
    sums[0] = lanes(rvec, zvec)
    sums[1] = lanes(zvec, wout)


def last_kernel(met, weights, local, wvec, mvec, sums, *rest):
    *besides, nout, totals = rest
    couple(met, weights, local, besides, nout)
    parts = jnp.concatenate(
        [sums[0], sums[1], lanes(wvec, mvec), lanes(mvec, nout)], axis=0
    )
    totals[...] = lax.dot_general(
        jnp.ones((1, parts.shape[1]), F32),
        parts,
        (((1,), (1,)), ((), ())),
        precision=lax.Precision.HIGHEST,
        preferred_element_type=F32,
    )


def finish_kernel(shares, rvec, wvec, nvec, zflat, mflat, sol, res):
    nblk, ncol, bdof = rvec.shape
    total = jnp.sum(shares[...], axis=0, keepdims=True)
    gamma, delta, mu, nu = [total[:, q * ncol : (q + 1) * ncol] for q in range(4)]
    alpha = gamma / delta
    gnew = gamma - 2.0 * alpha * delta + alpha * alpha * mu
    grow = 1.0 + gnew / gamma
    dnew = grow * grow * delta - 2.0 * alpha * grow * mu + alpha * alpha * nu
    anew = gnew / dnew
    both = alpha + anew * grow
    second = anew * alpha
    eye = lax.broadcasted_iota(jnp.int32, (ncol, ncol), 0) == lax.broadcasted_iota(
        jnp.int32, (ncol, ncol), 1
    )
    down = [
        jnp.sum(jnp.where(eye, x, 0.0), axis=1, keepdims=True) for x in (both, second)
    ]
    flatten(
        lambda b: rvec[b] - down[0] * wvec[b] + down[1] * nvec[b],
        nblk,
        ncol,
        bdof,
        res,
    )
    along = [jnp.concatenate([x] * (LANES // ncol), axis=1) for x in (both, second)]
    for j in range(sol.shape[1] // LANES):
        here = slice(j * LANES, (j + 1) * LANES)
        sol[:, here] = along[0] * zflat[:, here] - along[1] * mflat[:, here]


def call(kernel, outs, scratch, args, far=()):
    vmem = pl.BlockSpec(memory_space=pltpu.VMEM)
    hbm = pl.BlockSpec(memory_space=pltpu.HBM)
    far = [pltpu.with_memory_space_constraint(arg, pltpu.HBM) for arg in far]
    return pl.pallas_call(
        kernel,
        out_shape=outs,
        in_specs=[vmem] * len(args) + [hbm] * len(far),
        out_specs=jax.tree.map(lambda _: vmem, outs),
        scratch_shapes=scratch,
        compiler_params=pltpu.CompilerParams(vmem_limit_bytes=VMEM_LIMIT),
    )(*args, *far)


def everywhere(values):
    total = lax.axis_size("dam") * lax.axis_size("sec")
    copies = jnp.broadcast_to(values[None], (total,) + values.shape)
    return lax.all_to_all(copies, ("dam", "sec"), split_axis=0, concat_axis=0)


def exchange(sends, axis):
    size = lax.axis_size(axis)
    got = []
    for first, send in zip((1, 0), sends):
        pairs = [(i, i + 1) for i in range(first, size - 1, 2)]
        got.append(lax.ppermute(send, axis, pairs + [(j, i) for i, j in pairs]))
    return got


def shards(
    segment_load,
    segment_mask,
    stiffness,
    block_cols,
    capillary,
    dirichlet_blocks,
    face_map,
    face_weight,
    corner_map,
    coarse_inverse,
):
    nblk, bdof = capillary.shape[2:]
    ncol = segment_load.shape[-1] // bdof
    nface = face_map.shape[3]
    ncorner = corner_map.shape[2]
    size = nblk * bdof
    pair = lax.axis_size("sec") == 2
    load, mask = segment_load[0, 0], segment_mask[0, 0]
    cols = jnp.transpose(block_cols[0], (2, 0, 1))
    tang, weights = capillary[0, 0], face_weight[0, 0]
    blocks, rows = dirichlet_blocks[0, 0], coarse_inverse[0]

    def shape(*dims, dtype=F32):
        return jax.ShapeDtypeStruct(dims, dtype)

    def like(array):
        return shape(*array.shape, dtype=array.dtype)

    def hold(array):
        return pltpu.VMEM(array.shape, array.dtype)

    def index(array):
        return pltpu.SMEM(array.shape, array.dtype)

    def sems(count):
        return pltpu.SemaphoreType.DMA((count,))

    field = shape(nblk, ncol, bdof)
    flat = shape(nblk, bdof * ncol)
    face = shape(ncol, nface * bdof)
    group = ncorner * bdof
    tiles = shape(size // group, group, group, dtype=BF16)
    halved = pltpu.VMEM((size // group, 2 * ncol, group), BF16)
    lane = group + nface * bdof if pair else group
    marked = ncol + 8 if pair else ncol

    rvec, base, payload, high, low, cmap, met, weights, rows, cols, tang = call(
        functools.partial(start_kernel, pair),
        (field, field, shape(marked, lane), tiles, tiles)
        + (shape(1, ncorner, dtype=jnp.int32), shape(4, nface, dtype=jnp.int32))
        + tuple(like(a) for a in (weights, rows, cols, tang)),
        [
            hold(load),
            hold(mask),
            hold(blocks),
            index(corner_map),
            hold(corner_map),
            index(face_map),
            hold(face_map),
            hold(weights),
            pltpu.VMEM((bdof * ncol, nblk), F32),
            pltpu.VMEM((ncol * nblk, bdof), F32),
            halved,
            sems(11),
        ],
        (),
        (load, mask, corner_map, face_map, blocks, rows, cols, weights, tang),
    )

    def finish(base, shares, marks):
        vec, *faces = call(
            functools.partial(end_kernel, pair),
            (field,) + (face,) * (3 if pair else 4),
            [],
            (cmap, met, base, rows, shares, marks),
        )
        besides = exchange(faces[:2], "dam")
        besides += faces[2:] if pair else exchange(faces[2:], "sec")
        return vec, besides

    def local(vec, near, far):
        return call(
            functools.partial(local_kernel, bool(far)),
            (field, flat) + tuple(like(a) for a in far),
            [pltpu.VMEM((nblk, 2 * ncol, bdof), BF16), index(cols), sems(2)],
            (cols, met, weights, tang, vec) + near,
            far,
        )

    marks = lax.all_gather(payload, "sec")
    zvec, besides = finish(base, marks, marks)
    part, zflat, stiff = local(zvec, (), (stiffness[0, 0],))
    wvec, sums, base, payload = call(
        functools.partial(image_kernel, pair),
        (field, shape(2, ncol, bdof), field, shape(ncol, lane)),
        [halved],
        (cmap, met, weights, part, rvec, zvec, high, low, rows, *besides),
    )
    mvec, besides = finish(base, lax.all_gather(payload, "sec"), marks)
    part, mflat = local(mvec, (stiff,), ())
    nvec, totals = call(
        last_kernel,
        (field, shape(1, 4 * ncol)),
        [],
        (met, weights, part, wvec, mvec, sums, *besides),
    )
    sol, res = call(
        finish_kernel,
        (flat, flat),
        [],
        (everywhere(totals[0]), rvec, wvec, nvec, zflat, mflat),
    )
    return sol[None, None], res[None, None]


def solution(mesh):
    placed = (
        P("dam", "sec", None, None),
        P("dam", "sec", None, None),
        P("dam", "sec", None, None, None),
        P("dam", "sec", None, None),
        P("dam", "sec", None, None),
        P("dam", "sec", None, None, None),
        P("dam", "sec", None, None),
        P("dam", "sec", None, None),
        P("dam", "sec", None),
        P("dam", "sec", None),
    )
    return jax.shard_map(
        shards,
        mesh=mesh,
        in_specs=placed,
        out_specs=(P("dam", "sec", None, None), P("dam", "sec", None, None)),
        check_vma=False,
    )
```

```python
import functools

import jax
import jax.numpy as jnp
from jax import lax
from jax.experimental import pallas as pl
from jax.experimental.pallas import tpu as pltpu
from jax.sharding import PartitionSpec as P

F32 = jnp.float32
BF16 = jnp.bfloat16
VMEM_LIMIT = 16 * 1024 * 1024
LANES = 128


def halves(x):
    high = x.astype(BF16)
    return high, (x - high.astype(F32)).astype(BF16)


def stack(x):
    return jnp.concatenate(halves(x), axis=0)


def dot_t(a, b):
    return lax.dot_general(a, b, (((1,), (1,)), ((), ())), preferred_element_type=F32)


def dot(a, b):
    return lax.dot_general(a, b, (((1,), (0,)), ((), ())), preferred_element_type=F32)


def three_pass(mul, left, high, low):
    rows = left.shape[0] // 2
    first = mul(left, high)
    return first[:rows] + first[rows:] + mul(left[:rows], low)


def fetch(pairs, sems):
    copies = [
        pltpu.make_async_copy(source, target, sems.at[i])
        for i, (source, target) in enumerate(pairs)
    ]
    for copy in copies:
        copy.start()
    return [copy.wait for copy in copies]


def face_order(pair):
    near = 1 - lax.axis_index("dam") % 2
    across = 3 - lax.axis_index("sec") % 2
    return [1 - near, near] + ([across, 5 - across] if pair else [5 - across, across])


def listed(index):
    value = index[...]
    return [[value[i, j] for j in range(value.shape[1])] for i in range(value.shape[0])]


def pack(field, where, out, at=0):
    ncol, bdof = field.shape[1:]
    for p, b in enumerate(where):
        out[:ncol, at + p * bdof : at + (p + 1) * bdof] = field[b]


def add_pieces(field, where, piece):
    new = [field[b] + piece(p, b) for p, b in enumerate(where)]
    for b, value in zip(where, new):
        field[b] = value


def lane_piece(x, p, bdof):
    return x[:, p * bdof : (p + 1) * bdof]


def split_blocks(blocks, tiles_high, tiles_low):
    nblk, bdof = blocks.shape[:2]
    group = tiles_high.shape[1] // bdof
    for b in range(nblk):
        t, j = divmod(b, group)
        here = slice(j * bdof, (j + 1) * bdof)
        tiles_high[t, here, here], tiles_low[t, here, here] = halves(blocks[b])


def apply_blocks(field, tiles_high, tiles_low, left, base):
    nblk, ncol, bdof = field.shape
    group = tiles_high.shape[1] // bdof
    for b in range(nblk):
        t, j = divmod(b, group)
        here = slice(j * bdof, (j + 1) * bdof)
        left[t, :ncol, here], left[t, ncol:, here] = halves(field[b])
    for t in range(nblk // group):
        out = three_pass(dot, left[t], tiles_high[t], tiles_low[t])
        for j in range(group):
            base[t * group + j] = lane_piece(out, j, bdof)


def offer(pair, corners, across, field, rows, base, payload):
    bdof = field.shape[2]
    if not pair:
        pack(field, corners, payload)
        return
    wide = len(corners) * bdof
    at = payload.shape[1] - wide
    me = lax.axis_index("sec")
    own = stack(jnp.concatenate([field[b] for b in corners], axis=1))
    mine = pl.multiple_of(me * wide, wide)
    other = pl.multiple_of((1 - me) * wide, wide)
    correct = three_pass(dot_t, own, *halves(rows[:, pl.ds(mine, wide)]))
    payload[: field.shape[1], at:] = three_pass(dot, own, *halves(rows[:, pl.ds(other, wide)]))
    add_pieces(base, corners, lambda n, b: lane_piece(correct, n, bdof))
    pack(base, across, payload)


def end_kernel(pair, cmap, met, base, rows, shares, marks, zout, *faces):
    nblk, ncol, bdof = base.shape
    (corners,) = listed(cmap)
    where = listed(met)
    wide = len(corners) * bdof
    zout[...] = base[...]
    if pair:
        me = lax.axis_index("sec")
        at = len(where[0]) * bdof
        correct = shares[pl.ds(1 - me, 1), :ncol, at:][0]
        theirs = shares[pl.ds(me, 1), :ncol, at:][0]
        chunk = 2 * bdof
        twice = [
            jnp.concatenate([lane_piece(theirs, n, bdof)] * 2, axis=1)
            for n in range(len(corners))
        ]
        for j in range(at // chunk):
            here = slice(j * chunk, (j + 1) * chunk)
            value = shares[pl.ds(1 - me, 1), :ncol, here][0]
            for n in range(len(corners)):
                mark = marks[pl.ds(1 - me, 1), ncol + n : ncol + n + 1, here][0]
                value = value + mark * twice[n]
            faces[-1][:, here] = value
    else:
        correct = 0.0
        for s in range(shares.shape[0]):
            high, low = halves(rows[:, s * wide : (s + 1) * wide])
            correct = correct + three_pass(dot_t, stack(shares[s]), high, low)
    add_pieces(zout, corners, lambda n, b: lane_piece(correct, n, bdof))
    for blocks, out in zip(where, faces[: 2 if pair else 4]):
        pack(zout, blocks, out)


def swap_groups(x, ncol):
    subs, lanes_at = x.shape[1:]
    sub = lax.broadcasted_iota(jnp.int32, x.shape, 1)
    lane = lax.broadcasted_iota(jnp.int32, x.shape, 2)
    step = 1
    while step < subs:
        move = step * ncol
        low, left = (sub & step) == 0, (lane & move) == 0
        up = pltpu.roll(pltpu.roll(x, subs - step, 1), move, 2)
        down = pltpu.roll(pltpu.roll(x, step, 1), lanes_at - move, 2)
        x = jnp.where(low == left, x, jnp.where(low, up, down))
        step *= 2
    return x


def flatten(part, shape, out):
    nblk, ncol, bdof = shape
    subs = LANES // ncol
    for first in range(0, nblk, subs):
        tall = part(first, first + subs).reshape(LANES, bdof).T
        tall = swap_groups(tall.reshape(bdof // subs, subs, LANES), ncol)
        for j in range(bdof // subs):
            out[first : first + subs, j * LANES : (j + 1) * LANES] = tall[j]


def unflatten(part, shape, out):
    nblk, ncol, bdof = shape
    subs = LANES // ncol
    for first in range(0, nblk, subs):
        parts = [part(first, first + subs, j)[None] for j in range(bdof // subs)]
        tall = swap_groups(jnp.concatenate(parts, axis=0), ncol).reshape(bdof, LANES)
        out[first : first + subs] = tall.T.reshape(subs, ncol, bdof)


def start_kernel(pair, *refs):
    load_in, mask_in, cmap_in, fmap_in, blocks_in, rows_in, cols_in, weights_in, tang_in = refs[:9]
    rvec, base, payload, tiles_high, tiles_low, cmap_out, met, wmet, rows, cols, tang = refs[9:20]
    load, mask, blocks, cmap, cmap_row, fmap, fmap_rows, weights, left, sems = refs[20:]
    waits = fetch(
        [
            (load_in, load),
            (mask_in, mask),
            (cmap_in, cmap),
            (fmap_in, fmap),
            (blocks_in, blocks),
            (rows_in, rows),
            (cmap_in, cmap_row),
            (fmap_in, fmap_rows),
            (weights_in, weights),
            (cols_in, cols),
            (tang_in, tang),
        ],
        sems,
    )
    nblk, ncol, bdof = rvec.shape
    order = face_order(pair)
    tiles_high[...] = jnp.zeros_like(tiles_high)
    tiles_low[...] = jnp.zeros_like(tiles_low)
    waits[2]()
    waits[3]()
    corners = [cmap[0, 0, n] for n in range(cmap.shape[2])]
    across = [fmap[0, 0, order[2], p] for p in range(fmap.shape[3])]
    if pair:
        payload[ncol:, :] = jnp.zeros_like(payload[ncol:, :])
        for n, corner in enumerate(corners):
            for p, b in enumerate(across):
                payload[ncol + n : ncol + n + 1, p * bdof : (p + 1) * bdof] = jnp.full(
                    (1, bdof), jnp.where(corner == b, 1.0, 0.0), F32
                )
    waits[0]()
    waits[1]()
    scale = mask[...].astype(F32)
    scale = jnp.concatenate([scale] * (LANES // ncol), axis=1)
    unflatten(
        lambda first, last, j: load[first:last, j * LANES : (j + 1) * LANES]
        * scale[first:last],
        rvec.shape,
        rvec,
    )
    waits[4]()
    split_blocks(blocks, tiles_high, tiles_low)
    apply_blocks(rvec, tiles_high, tiles_low, left, base)
    for wait in waits[5:]:
        wait()
    offer(pair, corners, across, rvec, rows, base, payload)
    cmap_out[...] = cmap_row[0]
    for i, face in enumerate(order):
        met[i : i + 1, :] = fmap_rows[0, 0, pl.ds(face, 1), :]
        wmet[i : i + 1, :] = weights[pl.ds(face, 1), :]


def local_kernel(cols_in, met, weights, capillary, field, stiff, out, flat, *scratch):
    left, cols, sems = scratch
    nblk, ncol, bdof = field.shape
    (wait,) = fetch([(cols_in, cols)], sems)
    where = listed(met)
    flatten(lambda first, last: field[first:last], field.shape, flat)
    kept = stiff.shape[2] // bdof
    for b in range(nblk):
        left[b] = stack(field[b])
    wait()
    group = 4
    for t in range(0, nblk, group):
        gathered = [
            jnp.concatenate([left[cols[k, 0, t + j]] for k in range(kept)], axis=1)
            for j in range(group)
        ]
        firsts = [g[:ncol] for g in gathered]
        seconds = [g[ncol:] for g in gathered]
        rows = stiff[t : t + group].reshape(group * bdof, kept * bdof)
        prod = three_pass(dot_t, jnp.concatenate(firsts + seconds, axis=0), *halves(rows))
        for j in range(group):
            out[t + j] = (
                lane_piece(prod[j * ncol : (j + 1) * ncol], j, bdof)
                + capillary[t + j : t + j + 1, :] * field[t + j]
            )
    for i, blocks in enumerate(where):
        row = weights[i : i + 1, :]
        add_pieces(out, blocks, lambda p, b: lane_piece(row, p, bdof) * field[b])


def couple(met, weights, local, besides, out):
    bdof = local.shape[2]
    where = listed(met)
    out[...] = local[...]
    for i, beside in enumerate(besides):
        term = weights[i : i + 1, :] * beside[...]
        add_pieces(out, where[i], lambda p, b: -lane_piece(term, p, bdof))
    return where


def lanes(first, second):
    return jnp.sum(first[...] * second[...], axis=0)


def image_kernel(
    pair, cmap, met, weights, local, rvec, zvec, tiles_high, tiles_low, rows, *rest
):
    count = 3 if pair else 4
    besides, (wout, sums, base, payload, left) = rest[:count], rest[count:]
    (corners,) = listed(cmap)
    where = couple(met, weights, local, besides, wout)
    apply_blocks(wout, tiles_high, tiles_low, left, base)
    offer(pair, corners, where[2], wout, rows, base, payload)
    sums[0] = lanes(rvec, zvec)
    sums[1] = lanes(zvec, wout)


def last_kernel(met, weights, local, wvec, mvec, sums, *rest):
    *besides, nout, totals = rest
    couple(met, weights, local, besides, nout)
    parts = jnp.concatenate(
        [sums[0], sums[1], lanes(wvec, mvec), lanes(mvec, nout)], axis=0
    )
    totals[...] = lax.dot_general(
        jnp.ones((1, parts.shape[1]), F32),
        parts,
        (((1,), (1,)), ((), ())),
        precision=lax.Precision.HIGHEST,
        preferred_element_type=F32,
    )


def finish_kernel(shares, rvec, wvec, nvec, zflat, mflat, sol, res):
    nblk, ncol, bdof = rvec.shape
    total = jnp.sum(shares[...], axis=0, keepdims=True)
    gamma, delta, mu, nu = [total[:, q * ncol : (q + 1) * ncol] for q in range(4)]
    alpha = gamma / delta
    gnew = gamma - 2.0 * alpha * delta + alpha * alpha * mu
    grow = 1.0 + gnew / gamma
    dnew = grow * grow * delta - 2.0 * alpha * grow * mu + alpha * alpha * nu
    anew = gnew / dnew
    both = alpha + anew * grow
    second = anew * alpha
    eye = lax.broadcasted_iota(jnp.int32, (ncol, ncol), 0) == lax.broadcasted_iota(
        jnp.int32, (ncol, ncol), 1
    )
    down = [
        jnp.sum(jnp.where(eye, x, 0.0), axis=1, keepdims=True) for x in (both, second)
    ]
    flatten(
        lambda first, last: rvec[first:last]
        - down[0] * wvec[first:last]
        + down[1] * nvec[first:last],
        rvec.shape,
        res,
    )
    along = [jnp.concatenate([x] * (LANES // ncol), axis=1) for x in (both, second)]
    for j in range(sol.shape[1] // LANES):
        here = slice(j * LANES, (j + 1) * LANES)
        sol[:, here] = along[0] * zflat[:, here] - along[1] * mflat[:, here]


def call(kernel, outs, scratch, args, space=pltpu.VMEM):
    vmem = pl.BlockSpec(memory_space=pltpu.VMEM)
    if space != pltpu.VMEM:
        args = [pltpu.with_memory_space_constraint(arg, space) for arg in args]
    return pl.pallas_call(
        kernel,
        out_shape=outs,
        in_specs=[pl.BlockSpec(memory_space=space)] * len(args),
        out_specs=jax.tree.map(lambda _: vmem, outs),
        scratch_shapes=scratch,
        compiler_params=pltpu.CompilerParams(vmem_limit_bytes=VMEM_LIMIT),
    )(*args)


def everywhere(values):
    total = lax.axis_size("dam") * lax.axis_size("sec")
    copies = jnp.broadcast_to(values[None], (total,) + values.shape)
    return lax.all_to_all(copies, ("dam", "sec"), split_axis=0, concat_axis=0)


def exchange(sends, axis):
    size = lax.axis_size(axis)
    got = []
    for first, send in zip((1, 0), sends):
        pairs = [(i, i + 1) for i in range(first, size - 1, 2)]
        got.append(lax.ppermute(send, axis, pairs + [(j, i) for i, j in pairs]))
    return got


def shards(
    segment_load,
    segment_mask,
    stiffness,
    block_cols,
    capillary,
    dirichlet_blocks,
    face_map,
    face_weight,
    corner_map,
    coarse_inverse,
):
    nblk, bdof = capillary.shape[2:]
    ncol = segment_load.shape[-1] // bdof
    nface = face_map.shape[3]
    ncorner = corner_map.shape[2]
    size = nblk * bdof
    pair = lax.axis_size("sec") == 2
    load, mask = segment_load[0, 0], segment_mask[0, 0]
    cols = jnp.transpose(block_cols[0], (2, 0, 1))
    tang, weights = capillary[0, 0], face_weight[0, 0]
    blocks, rows = dirichlet_blocks[0, 0], coarse_inverse[0]

    def shape(*dims, dtype=F32):
        return jax.ShapeDtypeStruct(dims, dtype)

    def like(array):
        return shape(*array.shape, dtype=array.dtype)

    def hold(array):
        return pltpu.VMEM(array.shape, array.dtype)

    def index(array):
        return pltpu.SMEM(array.shape, array.dtype)

    def sems(count):
        return pltpu.SemaphoreType.DMA((count,))

    field = shape(nblk, ncol, bdof)
    flat = shape(nblk, bdof * ncol)
    face = shape(ncol, nface * bdof)
    group = ncorner * bdof
    tiles = shape(size // group, group, group, dtype=BF16)
    halved = pltpu.VMEM((size // group, 2 * ncol, group), BF16)
    lane = group + nface * bdof if pair else group
    marked = ncol + 8 if pair else ncol

    rvec, base, payload, high, low, cmap, met, weights, rows, cols, tang = call(
        functools.partial(start_kernel, pair),
        (field, field, shape(marked, lane), tiles, tiles)
        + (shape(1, ncorner, dtype=jnp.int32), shape(4, nface, dtype=jnp.int32))
        + tuple(like(a) for a in (weights, rows, cols, tang)),
        [
            hold(load),
            hold(mask),
            hold(blocks),
            index(corner_map),
            hold(corner_map),
            index(face_map),
            hold(face_map),
            hold(weights),
            halved,
            sems(11),
        ],
        (load, mask, corner_map, face_map, blocks, rows, cols, weights, tang),
        pltpu.HBM,
    )

    def finish(base, shares, marks):
        vec, *faces = call(
            functools.partial(end_kernel, pair),
            (field,) + (face,) * (3 if pair else 4),
            [],
            (cmap, met, base, rows, shares, marks),
        )
        besides = exchange(faces[:2], "dam")
        besides += faces[2:] if pair else exchange(faces[2:], "sec")
        return vec, besides

    def local(vec):
        return call(
            local_kernel,
            (field, flat),
            [pltpu.VMEM((nblk, 2 * ncol, bdof), BF16), index(cols), sems(1)],
            (cols, met, weights, tang, vec, stiffness[0, 0]),
        )

    marks = lax.all_gather(payload, "sec")
    zvec, besides = finish(base, marks, marks)
    part, zflat = local(zvec)
    wvec, sums, base, payload = call(
        functools.partial(image_kernel, pair),
        (field, shape(2, ncol, bdof), field, shape(ncol, lane)),
        [halved],
        (cmap, met, weights, part, rvec, zvec, high, low, rows, *besides),
    )
    mvec, besides = finish(base, lax.all_gather(payload, "sec"), marks)
    part, mflat = local(mvec)
    nvec, totals = call(
        last_kernel,
        (field, shape(1, 4 * ncol)),
        [],
        (met, weights, part, wvec, mvec, sums, *besides),
    )
    sol, res = call(
        finish_kernel,
        (flat, flat),
        [],
        (everywhere(totals[0]), rvec, wvec, nvec, zflat, mflat),
    )
    return sol[None, None], res[None, None]


def solution(mesh):
    placed = (
        P("dam", "sec", None, None),
        P("dam", "sec", None, None),
        P("dam", "sec", None, None, None),
        P("dam", "sec", None, None),
        P("dam", "sec", None, None),
        P("dam", "sec", None, None, None),
        P("dam", "sec", None, None),
        P("dam", "sec", None, None),
        P("dam", "sec", None),
        P("dam", "sec", None),
    )
    return jax.shard_map(
        shards,
        mesh=mesh,
        in_specs=placed,
        out_specs=(P("dam", "sec", None, None), P("dam", "sec", None, None)),
        check_vma=False,
    )
```

```python
import functools

import jax
import jax.numpy as jnp
from jax import lax
from jax.experimental import pallas as pl
from jax.experimental.pallas import tpu as pltpu
from jax.sharding import PartitionSpec as P

F32 = jnp.float32
BF16 = jnp.bfloat16
VMEM_LIMIT = 16 * 1024 * 1024
LANES = 128


def halves(x):
    high = x.astype(BF16)
    return high, (x - high.astype(F32)).astype(BF16)


def stack(x):
    return jnp.concatenate(halves(x), axis=0)


def dot_t(a, b):
    return lax.dot_general(a, b, (((1,), (1,)), ((), ())), preferred_element_type=F32)


def dot(a, b):
    return lax.dot_general(a, b, (((1,), (0,)), ((), ())), preferred_element_type=F32)


def three_pass(mul, left, high, low):
    rows = left.shape[0] // 2
    first = mul(left, high)
    return first[:rows] + first[rows:] + mul(left[:rows], low)


def fetch(pairs, sems):
    copies = [
        pltpu.make_async_copy(source, target, sems.at[i])
        for i, (source, target) in enumerate(pairs)
    ]
    for copy in copies:
        copy.start()
    return [copy.wait for copy in copies]


def face_order(pair):
    near = 1 - lax.axis_index("dam") % 2
    across = 3 - lax.axis_index("sec") % 2
    return [1 - near, near] + ([across, 5 - across] if pair else [5 - across, across])


def listed(index):
    value = index[...]
    return [[value[i, j] for j in range(value.shape[1])] for i in range(value.shape[0])]


def pack(field, where, out, at=0):
    ncol, bdof = field.shape[1:]
    for p, b in enumerate(where):
        out[:ncol, at + p * bdof : at + (p + 1) * bdof] = field[b]


def add_pieces(field, where, piece):
    new = [field[b] + piece(p, b) for p, b in enumerate(where)]
    for b, value in zip(where, new):
        field[b] = value


def lane_piece(x, p, bdof):
    return x[:, p * bdof : (p + 1) * bdof]


def split_blocks(blocks, tiles_high, tiles_low):
    nblk, bdof = blocks.shape[:2]
    group = tiles_high.shape[1] // bdof
    for b in range(nblk):
        t, j = divmod(b, group)
        here = slice(j * bdof, (j + 1) * bdof)
        tiles_high[t, here, here], tiles_low[t, here, here] = halves(blocks[b])


def apply_blocks(field, tiles_high, tiles_low, left, base):
    nblk, ncol, bdof = field.shape
    group = tiles_high.shape[1] // bdof
    for b in range(nblk):
        t, j = divmod(b, group)
        here = slice(j * bdof, (j + 1) * bdof)
        left[t, :ncol, here], left[t, ncol:, here] = halves(field[b])
    for t in range(nblk // group):
        out = three_pass(dot, left[t], tiles_high[t], tiles_low[t])
        for j in range(group):
            base[t * group + j] = lane_piece(out, j, bdof)


def offer(pair, corners, across, field, rows, base, payload):
    bdof = field.shape[2]
    if not pair:
        pack(field, corners, payload)
        return
    wide = len(corners) * bdof
    at = payload.shape[1] - wide
    me = lax.axis_index("sec")
    own = stack(jnp.concatenate([field[b] for b in corners], axis=1))
    mine = pl.multiple_of(me * wide, wide)
    other = pl.multiple_of((1 - me) * wide, wide)
    correct = three_pass(dot_t, own, *halves(rows[:, pl.ds(mine, wide)]))
    payload[: field.shape[1], at:] = three_pass(dot, own, *halves(rows[:, pl.ds(other, wide)]))
    add_pieces(base, corners, lambda n, b: lane_piece(correct, n, bdof))
    pack(base, across, payload)


def end_kernel(pair, cmap, met, base, rows, shares, marks, zout, *faces):
    nblk, ncol, bdof = base.shape
    (corners,) = listed(cmap)
    where = listed(met)
    wide = len(corners) * bdof
    zout[...] = base[...]
    if pair:
        me = lax.axis_index("sec")
        at = len(where[0]) * bdof
        correct = shares[pl.ds(1 - me, 1), :ncol, at:][0]
        theirs = shares[pl.ds(me, 1), :ncol, at:][0]
        chunk = 2 * bdof
        twice = [
            jnp.concatenate([lane_piece(theirs, n, bdof)] * 2, axis=1)
            for n in range(len(corners))
        ]
        for j in range(at // chunk):
            here = slice(j * chunk, (j + 1) * chunk)
            value = shares[pl.ds(1 - me, 1), :ncol, here][0]
            for n in range(len(corners)):
                mark = marks[pl.ds(1 - me, 1), ncol + n : ncol + n + 1, here][0]
                value = value + mark * twice[n]
            faces[-1][:, here] = value
    else:
        correct = 0.0
        for s in range(shares.shape[0]):
            high, low = halves(rows[:, s * wide : (s + 1) * wide])
            correct = correct + three_pass(dot_t, stack(shares[s]), high, low)
    add_pieces(zout, corners, lambda n, b: lane_piece(correct, n, bdof))
    for blocks, out in zip(where, faces[: 2 if pair else 4]):
        pack(zout, blocks, out)


def swap_groups(x, ncol):
    subs, lanes_at = x.shape[1:]
    sub = lax.broadcasted_iota(jnp.int32, x.shape, 1)
    lane = lax.broadcasted_iota(jnp.int32, x.shape, 2)
    step = 1
    while step < subs:
        move = step * ncol
        low, left = (sub & step) == 0, (lane & move) == 0
        up = pltpu.roll(pltpu.roll(x, subs - step, 1), move, 2)
        down = pltpu.roll(pltpu.roll(x, step, 1), lanes_at - move, 2)
        x = jnp.where(low == left, x, jnp.where(low, up, down))
        step *= 2
    return x


def flatten(part, shape, out):
    nblk, ncol, bdof = shape
    subs = LANES // ncol
    for first in range(0, nblk, subs):
        tall = part(first, first + subs).reshape(LANES, bdof).T
        tall = swap_groups(tall.reshape(bdof // subs, subs, LANES), ncol)
        for j in range(bdof // subs):
            out[first : first + subs, j * LANES : (j + 1) * LANES] = tall[j]


def unflatten(part, shape, out):
    nblk, ncol, bdof = shape
    subs = LANES // ncol
    for first in range(0, nblk, subs):
        parts = [part(first, first + subs, j)[None] for j in range(bdof // subs)]
        tall = swap_groups(jnp.concatenate(parts, axis=0), ncol).reshape(bdof, LANES)
        out[first : first + subs] = tall.T.reshape(subs, ncol, bdof)


def start_kernel(pair, *refs):
    load_in, mask_in, cmap_in, fmap_in, blocks_in, rows_in, cols_in, weights_in, tang_in = refs[:9]
    rvec, base, payload, tiles_high, tiles_low, cmap_out, met, wmet, rows, cols, tang = refs[9:20]
    load, mask, blocks, cmap, cmap_row, fmap, fmap_rows, weights, left, sems = refs[20:]
    waits = fetch(
        [
            (load_in, load),
            (mask_in, mask),
            (cmap_in, cmap),
            (fmap_in, fmap),
            (blocks_in, blocks),
            (rows_in, rows),
            (cmap_in, cmap_row),
            (fmap_in, fmap_rows),
            (weights_in, weights),
            (cols_in, cols),
            (tang_in, tang),
        ],
        sems,
    )
    nblk, ncol, bdof = rvec.shape
    order = face_order(pair)
    tiles_high[...] = jnp.zeros_like(tiles_high)
    tiles_low[...] = jnp.zeros_like(tiles_low)
    waits[2]()
    waits[3]()
    corners = [cmap[0, 0, n] for n in range(cmap.shape[2])]
    across = [fmap[0, 0, order[2], p] for p in range(fmap.shape[3])]
    if pair:
        payload[ncol:, :] = jnp.zeros_like(payload[ncol:, :])
        for n, corner in enumerate(corners):
            for p, b in enumerate(across):
                payload[ncol + n : ncol + n + 1, p * bdof : (p + 1) * bdof] = jnp.full(
                    (1, bdof), jnp.where(corner == b, 1.0, 0.0), F32
                )
    waits[0]()
    waits[1]()
    scale = mask[...].astype(F32)
    scale = jnp.concatenate([scale] * (LANES // ncol), axis=1)
    unflatten(
        lambda first, last, j: load[first:last, j * LANES : (j + 1) * LANES]
        * scale[first:last],
        rvec.shape,
        rvec,
    )
    waits[4]()
    split_blocks(blocks, tiles_high, tiles_low)
    apply_blocks(rvec, tiles_high, tiles_low, left, base)
    for wait in waits[5:]:
        wait()
    offer(pair, corners, across, rvec, rows, base, payload)
    cmap_out[...] = cmap_row[0]
    for i, face in enumerate(order):
        met[i : i + 1, :] = fmap_rows[0, 0, pl.ds(face, 1), :]
        wmet[i : i + 1, :] = weights[pl.ds(face, 1), :]


def local_kernel(
    cols_in, met, weights, capillary, field, other, stiff, out, flat, other_flat, *scratch
):
    left, cols, sems = scratch
    nblk, ncol, bdof = field.shape
    (wait,) = fetch([(cols_in, cols)], sems)
    where = listed(met)
    flatten(lambda first, last: field[first:last], field.shape, flat)
    flatten(lambda first, last: other[first:last], field.shape, other_flat)
    kept = stiff.shape[2] // bdof
    for b in range(nblk):
        left[b] = stack(field[b])
    wait()
    group = 4
    for t in range(0, nblk, group):
        gathered = [
            jnp.concatenate([left[cols[k, 0, t + j]] for k in range(kept)], axis=1)
            for j in range(group)
        ]
        firsts = [g[:ncol] for g in gathered]
        seconds = [g[ncol:] for g in gathered]
        rows = stiff[t : t + group].reshape(group * bdof, kept * bdof)
        prod = three_pass(dot_t, jnp.concatenate(firsts + seconds, axis=0), *halves(rows))
        for j in range(group):
            out[t + j] = (
                lane_piece(prod[j * ncol : (j + 1) * ncol], j, bdof)
                + capillary[t + j : t + j + 1, :] * field[t + j]
            )
    for i, blocks in enumerate(where):
        row = weights[i : i + 1, :]
        add_pieces(out, blocks, lambda p, b: lane_piece(row, p, bdof) * field[b])


def couple(met, weights, local, besides, out):
    bdof = local.shape[2]
    where = listed(met)
    out[...] = local[...]
    for i, beside in enumerate(besides):
        term = weights[i : i + 1, :] * beside[...]
        add_pieces(out, where[i], lambda p, b: -lane_piece(term, p, bdof))
    return where


def lanes(first, second):
    return jnp.sum(first[...] * second[...], axis=0)


def image_kernel(
    pair, cmap, met, weights, local, rvec, zvec, tiles_high, tiles_low, rows, *rest
):
    count = 3 if pair else 4
    besides, (wout, sums, base, payload, left) = rest[:count], rest[count:]
    (corners,) = listed(cmap)
    where = couple(met, weights, local, besides, wout)
    apply_blocks(wout, tiles_high, tiles_low, left, base)
    offer(pair, corners, where[2], wout, rows, base, payload)
    sums[0] = lanes(rvec, zvec)
    sums[1] = lanes(zvec, wout)


def last_kernel(met, weights, local, wvec, mvec, sums, *rest):
    *besides, nout, totals = rest
    couple(met, weights, local, besides, nout)
    parts = jnp.concatenate(
        [sums[0], sums[1], lanes(wvec, mvec), lanes(mvec, nout)], axis=0
    )
    sides = lax.dot_general(
        jnp.ones((totals.shape[0], parts.shape[1]), F32),
        parts,
        (((1,), (1,)), ((), ())),
        precision=lax.Precision.HIGHEST,
        preferred_element_type=F32,
    )
    rest = totals.shape[1] - sides.shape[1]
    totals[...] = jnp.concatenate([sides, jnp.zeros((sides.shape[0], rest), F32)], axis=1)


def finish_kernel(shares, nvec, rflat, zflat, wflat, mflat, sol, res):
    nblk, ncol, bdof = nvec.shape
    flatten(lambda first, last: nvec[first:last], nvec.shape, res)
    total = jnp.sum(shares[...], axis=0)[:1]
    gamma, delta, mu, nu = [total[:, q * ncol : (q + 1) * ncol] for q in range(4)]
    alpha = gamma / delta
    gnew = gamma - 2.0 * alpha * delta + alpha * alpha * mu
    grow = 1.0 + gnew / gamma
    dnew = grow * grow * delta - 2.0 * alpha * grow * mu + alpha * alpha * nu
    anew = gnew / dnew
    both, second = [
        jnp.concatenate([x] * (LANES // ncol), axis=1)
        for x in (alpha + anew * grow, anew * alpha)
    ]
    for j in range(sol.shape[1] // LANES):
        here = slice(j * LANES, (j + 1) * LANES)
        sol[:, here] = both * zflat[:, here] - second * mflat[:, here]
        res[:, here] = rflat[:, here] - both * wflat[:, here] + second * res[:, here]


def call(kernel, outs, scratch, args, space=pltpu.VMEM):
    vmem = pl.BlockSpec(memory_space=pltpu.VMEM)
    if space != pltpu.VMEM:
        args = [pltpu.with_memory_space_constraint(arg, space) for arg in args]
    return pl.pallas_call(
        kernel,
        out_shape=outs,
        in_specs=[pl.BlockSpec(memory_space=space)] * len(args),
        out_specs=jax.tree.map(lambda _: vmem, outs),
        scratch_shapes=scratch,
        compiler_params=pltpu.CompilerParams(vmem_limit_bytes=VMEM_LIMIT),
    )(*args)


def everywhere(values):
    return lax.all_gather(values, ("dam", "sec"))


def exchange(sends, axis):
    size = lax.axis_size(axis)
    got = []
    for first, send in zip((1, 0), sends):
        pairs = [(i, i + 1) for i in range(first, size - 1, 2)]
        got.append(lax.ppermute(send, axis, pairs + [(j, i) for i, j in pairs]))
    return got


def shards(
    segment_load,
    segment_mask,
    stiffness,
    block_cols,
    capillary,
    dirichlet_blocks,
    face_map,
    face_weight,
    corner_map,
    coarse_inverse,
):
    nblk, bdof = capillary.shape[2:]
    ncol = segment_load.shape[-1] // bdof
    nface = face_map.shape[3]
    ncorner = corner_map.shape[2]
    size = nblk * bdof
    pair = lax.axis_size("sec") == 2
    load, mask = segment_load[0, 0], segment_mask[0, 0]
    cols = jnp.transpose(block_cols[0], (2, 0, 1))
    tang, weights = capillary[0, 0], face_weight[0, 0]
    blocks, rows = dirichlet_blocks[0, 0], coarse_inverse[0]

    def shape(*dims, dtype=F32):
        return jax.ShapeDtypeStruct(dims, dtype)

    def like(array):
        return shape(*array.shape, dtype=array.dtype)

    def hold(array):
        return pltpu.VMEM(array.shape, array.dtype)

    def index(array):
        return pltpu.SMEM(array.shape, array.dtype)

    def sems(count):
        return pltpu.SemaphoreType.DMA((count,))

    field = shape(nblk, ncol, bdof)
    flat = shape(nblk, bdof * ncol)
    face = shape(ncol, nface * bdof)
    group = ncorner * bdof
    tiles = shape(size // group, group, group, dtype=BF16)
    halved = pltpu.VMEM((size // group, 2 * ncol, group), BF16)
    lane = group + nface * bdof if pair else group
    marked = ncol + 8 if pair else ncol

    rvec, base, payload, high, low, cmap, met, weights, rows, cols, tang = call(
        functools.partial(start_kernel, pair),
        (field, field, shape(marked, lane), tiles, tiles)
        + (shape(1, ncorner, dtype=jnp.int32), shape(4, nface, dtype=jnp.int32))
        + tuple(like(a) for a in (weights, rows, cols, tang)),
        [
            hold(load),
            hold(mask),
            hold(blocks),
            index(corner_map),
            hold(corner_map),
            index(face_map),
            hold(face_map),
            hold(weights),
            halved,
            sems(11),
        ],
        (load, mask, corner_map, face_map, blocks, rows, cols, weights, tang),
        pltpu.HBM,
    )

    def finish(base, shares, marks):
        vec, *faces = call(
            functools.partial(end_kernel, pair),
            (field,) + (face,) * (3 if pair else 4),
            [],
            (cmap, met, base, rows, shares, marks),
        )
        besides = exchange(faces[:2], "dam")
        besides += faces[2:] if pair else exchange(faces[2:], "sec")
        return vec, besides

    def local(vec, other):
        return call(
            local_kernel,
            (field, flat, flat),
            [pltpu.VMEM((nblk, 2 * ncol, bdof), BF16), index(cols), sems(1)],
            (cols, met, weights, tang, vec, other, stiffness[0, 0]),
        )

    marks = lax.all_gather(payload, "sec")
    zvec, besides = finish(base, marks, marks)
    part, zflat, rflat = local(zvec, rvec)
    wvec, sums, base, payload = call(
        functools.partial(image_kernel, pair),
        (field, shape(2, ncol, bdof), field, shape(ncol, lane)),
        [halved],
        (cmap, met, weights, part, rvec, zvec, high, low, rows, *besides),
    )
    mvec, besides = finish(base, lax.all_gather(payload, "sec"), marks)
    part, mflat, wflat = local(mvec, wvec)
    nvec, totals = call(
        last_kernel,
        (field, shape(8, LANES)),
        [],
        (met, weights, part, wvec, mvec, sums, *besides),
    )
    sol, res = call(
        finish_kernel,
        (flat, flat),
        [],
        (everywhere(totals), nvec, rflat, zflat, wflat, mflat),
    )
    return sol[None, None], res[None, None]


def solution(mesh):
    placed = (
        P("dam", "sec", None, None),
        P("dam", "sec", None, None),
        P("dam", "sec", None, None, None),
        P("dam", "sec", None, None),
        P("dam", "sec", None, None),
        P("dam", "sec", None, None, None),
        P("dam", "sec", None, None),
        P("dam", "sec", None, None),
        P("dam", "sec", None),
        P("dam", "sec", None),
    )
    return jax.shard_map(
        shards,
        mesh=mesh,
        in_specs=placed,
        out_specs=(P("dam", "sec", None, None), P("dam", "sec", None, None)),
        check_vma=False,
    )
```

```python
import functools

import jax
import jax.numpy as jnp
from jax import lax
from jax.experimental import pallas as pl
from jax.experimental.pallas import tpu as pltpu
from jax.sharding import PartitionSpec as P

F32 = jnp.float32
BF16 = jnp.bfloat16
VMEM_LIMIT = 16 * 1024 * 1024
LANES = 128


def halves(x):
    high = x.astype(BF16)
    return high, (x - high.astype(F32)).astype(BF16)


def stack(x):
    return jnp.concatenate(halves(x), axis=0)


def dot_t(a, b):
    return lax.dot_general(a, b, (((1,), (1,)), ((), ())), preferred_element_type=F32)


def dot(a, b):
    return lax.dot_general(a, b, (((1,), (0,)), ((), ())), preferred_element_type=F32)


def three_pass(mul, left, high, low):
    rows = left.shape[0] // 2
    first = mul(left, high)
    return first[:rows] + first[rows:] + mul(left[:rows], low)


def fetch(pairs, sems):
    copies = [
        pltpu.make_async_copy(source, target, sems.at[i])
        for i, (source, target) in enumerate(pairs)
    ]
    for copy in copies:
        copy.start()
    return [copy.wait for copy in copies]


def face_order(pair):
    near = 1 - lax.axis_index("dam") % 2
    across = 3 - lax.axis_index("sec") % 2
    return [1 - near, near] + ([across, 5 - across] if pair else [5 - across, across])


def listed(index):
    value = index[...]
    return [[value[i, j] for j in range(value.shape[1])] for i in range(value.shape[0])]


def pack(field, where, out, at=0):
    ncol, bdof = field.shape[1:]
    for p, b in enumerate(where):
        out[:ncol, at + p * bdof : at + (p + 1) * bdof] = field[b]


def add_pieces(field, where, piece):
    new = [field[b] + piece(p, b) for p, b in enumerate(where)]
    for b, value in zip(where, new):
        field[b] = value


def lane_piece(x, p, bdof):
    return x[:, p * bdof : (p + 1) * bdof]


def split_blocks(blocks, tiles_high, tiles_low):
    nblk, bdof = blocks.shape[:2]
    group = tiles_high.shape[1] // bdof
    for b in range(nblk):
        t, j = divmod(b, group)
        here = slice(j * bdof, (j + 1) * bdof)
        tiles_high[t, here, here], tiles_low[t, here, here] = halves(blocks[b])


def apply_blocks(field, tiles_high, tiles_low, left, base):
    nblk, ncol, bdof = field.shape
    group = tiles_high.shape[1] // bdof
    for b in range(nblk):
        t, j = divmod(b, group)
        here = slice(j * bdof, (j + 1) * bdof)
        left[t, :ncol, here], left[t, ncol:, here] = halves(field[b])
    for t in range(nblk // group):
        out = three_pass(dot, left[t], tiles_high[t], tiles_low[t])
        for j in range(group):
            base[t * group + j] = lane_piece(out, j, bdof)


def offer(pair, corners, across, field, rows, base, payload):
    bdof = field.shape[2]
    if not pair:
        pack(field, corners, payload)
        return
    wide = len(corners) * bdof
    at = payload.shape[1] - wide
    me = lax.axis_index("sec")
    own = stack(jnp.concatenate([field[b] for b in corners], axis=1))
    mine = pl.multiple_of(me * wide, wide)
    other = pl.multiple_of((1 - me) * wide, wide)
    correct = three_pass(dot_t, own, *halves(rows[:, pl.ds(mine, wide)]))
    payload[: field.shape[1], at:] = three_pass(dot, own, *halves(rows[:, pl.ds(other, wide)]))
    add_pieces(base, corners, lambda n, b: lane_piece(correct, n, bdof))
    pack(base, across, payload)


def end_kernel(pair, cmap, met, base, rows, shares, marks, zout, *faces):
    nblk, ncol, bdof = base.shape
    (corners,) = listed(cmap)
    where = listed(met)
    wide = len(corners) * bdof
    zout[...] = base[...]
    if pair:
        me = lax.axis_index("sec")
        at = len(where[0]) * bdof
        correct = shares[pl.ds(1 - me, 1), :ncol, at:][0]
        theirs = shares[pl.ds(me, 1), :ncol, at:][0]
        chunk = 2 * bdof
        twice = [
            jnp.concatenate([lane_piece(theirs, n, bdof)] * 2, axis=1)
            for n in range(len(corners))
        ]
        for j in range(at // chunk):
            here = slice(j * chunk, (j + 1) * chunk)
            value = shares[pl.ds(1 - me, 1), :ncol, here][0]
            for n in range(len(corners)):
                mark = marks[pl.ds(1 - me, 1), ncol + n : ncol + n + 1, here][0]
                value = value + mark * twice[n]
            faces[-1][:, here] = value
    else:
        correct = 0.0
        for s in range(shares.shape[0]):
            high, low = halves(rows[:, s * wide : (s + 1) * wide])
            correct = correct + three_pass(dot_t, stack(shares[s]), high, low)
    add_pieces(zout, corners, lambda n, b: lane_piece(correct, n, bdof))
    for blocks, out in zip(where, faces[: 2 if pair else 4]):
        pack(zout, blocks, out)


def swap_groups(x, ncol):
    subs, lanes_at = x.shape[1:]
    sub = lax.broadcasted_iota(jnp.int32, x.shape, 1)
    lane = lax.broadcasted_iota(jnp.int32, x.shape, 2)
    step = 1
    while step < subs:
        move = step * ncol
        low, left = (sub & step) == 0, (lane & move) == 0
        up = pltpu.roll(pltpu.roll(x, subs - step, 1), move, 2)
        down = pltpu.roll(pltpu.roll(x, step, 1), lanes_at - move, 2)
        x = jnp.where(low == left, x, jnp.where(low, up, down))
        step *= 2
    return x


def flatten(part, shape, out):
    nblk, ncol, bdof = shape
    subs = LANES // ncol
    for first in range(0, nblk, subs):
        tall = part(first, first + subs).reshape(LANES, bdof).T
        tall = swap_groups(tall.reshape(bdof // subs, subs, LANES), ncol)
        for j in range(bdof // subs):
            out[first : first + subs, j * LANES : (j + 1) * LANES] = tall[j]


def unflatten(part, shape, out):
    nblk, ncol, bdof = shape
    subs = LANES // ncol
    for first in range(0, nblk, subs):
        parts = [part(first, first + subs, j)[None] for j in range(bdof // subs)]
        tall = swap_groups(jnp.concatenate(parts, axis=0), ncol).reshape(bdof, LANES)
        out[first : first + subs] = tall.T.reshape(subs, ncol, bdof)


def start_kernel(pair, *refs):
    load_in, mask_in, cmap_in, fmap_in, blocks_in, rows_in, cols_in, weights_in, tang_in = refs[:9]
    rvec, base, payload, tiles_high, tiles_low, cmap_out, met, wmet, rows, cols, tang = refs[9:20]
    load, mask, blocks, cmap, cmap_row, fmap, fmap_rows, weights, left, sems = refs[20:]
    waits = fetch(
        [
            (load_in, load),
            (mask_in, mask),
            (cmap_in, cmap),
            (fmap_in, fmap),
            (blocks_in, blocks),
            (rows_in, rows),
            (cmap_in, cmap_row),
            (fmap_in, fmap_rows),
            (weights_in, weights),
            (cols_in, cols),
            (tang_in, tang),
        ],
        sems,
    )
    nblk, ncol, bdof = rvec.shape
    order = face_order(pair)
    tiles_high[...] = jnp.zeros_like(tiles_high)
    tiles_low[...] = jnp.zeros_like(tiles_low)
    waits[2]()
    waits[3]()
    corners = [cmap[0, 0, n] for n in range(cmap.shape[2])]
    across = [fmap[0, 0, order[2], p] for p in range(fmap.shape[3])]
    if pair:
        payload[ncol:, :] = jnp.zeros_like(payload[ncol:, :])
        for n, corner in enumerate(corners):
            for p, b in enumerate(across):
                payload[ncol + n : ncol + n + 1, p * bdof : (p + 1) * bdof] = jnp.full(
                    (1, bdof), jnp.where(corner == b, 1.0, 0.0), F32
                )
    for wait in waits[:2] + waits[4:]:
        wait()
    scale = mask[...].astype(F32)
    scale = jnp.concatenate([scale] * (LANES // ncol), axis=1)
    unflatten(
        lambda first, last, j: load[first:last, j * LANES : (j + 1) * LANES]
        * scale[first:last],
        rvec.shape,
        rvec,
    )
    split_blocks(blocks, tiles_high, tiles_low)
    apply_blocks(rvec, tiles_high, tiles_low, left, base)
    offer(pair, corners, across, rvec, rows, base, payload)
    cmap_out[...] = cmap_row[0]
    for i, face in enumerate(order):
        met[i : i + 1, :] = fmap_rows[0, 0, pl.ds(face, 1), :]
        wmet[i : i + 1, :] = weights[pl.ds(face, 1), :]


def local_kernel(
    cols_in, met, weights, capillary, field, other, stiff, out, flat, other_flat, *scratch
):
    left, cols, sems = scratch
    nblk, ncol, bdof = field.shape
    (wait,) = fetch([(cols_in, cols)], sems)
    where = listed(met)
    flatten(lambda first, last: field[first:last], field.shape, flat)
    flatten(lambda first, last: other[first:last], field.shape, other_flat)
    kept = stiff.shape[2] // bdof
    for b in range(nblk):
        left[b] = stack(field[b])
    wait()
    group = 4
    for t in range(0, nblk, group):
        gathered = [
            jnp.concatenate([left[cols[k, 0, t + j]] for k in range(kept)], axis=1)
            for j in range(group)
        ]
        firsts = [g[:ncol] for g in gathered]
        seconds = [g[ncol:] for g in gathered]
        rows = stiff[t : t + group].reshape(group * bdof, kept * bdof)
        prod = three_pass(dot_t, jnp.concatenate(firsts + seconds, axis=0), *halves(rows))
        for j in range(group):
            out[t + j] = (
                lane_piece(prod[j * ncol : (j + 1) * ncol], j, bdof)
                + capillary[t + j : t + j + 1, :] * field[t + j]
            )
    for i, blocks in enumerate(where):
        row = weights[i : i + 1, :]
        add_pieces(out, blocks, lambda p, b: lane_piece(row, p, bdof) * field[b])


def couple(met, weights, local, besides, out):
    bdof = local.shape[2]
    where = listed(met)
    out[...] = local[...]
    for i, beside in enumerate(besides):
        term = weights[i : i + 1, :] * beside[...]
        add_pieces(out, where[i], lambda p, b: -lane_piece(term, p, bdof))
    return where


def lanes(first, second):
    return jnp.sum(first[...] * second[...], axis=0)


def image_kernel(
    pair, cmap, met, weights, local, rvec, zvec, tiles_high, tiles_low, rows, *rest
):
    count = 3 if pair else 4
    besides, (wout, sums, base, payload, left) = rest[:count], rest[count:]
    (corners,) = listed(cmap)
    where = couple(met, weights, local, besides, wout)
    apply_blocks(wout, tiles_high, tiles_low, left, base)
    offer(pair, corners, where[2], wout, rows, base, payload)
    sums[0] = lanes(rvec, zvec)
    sums[1] = lanes(zvec, wout)


def last_kernel(met, weights, local, wvec, mvec, sums, *rest):
    *besides, nout, totals = rest
    couple(met, weights, local, besides, nout)
    parts = jnp.concatenate(
        [sums[0], sums[1], lanes(wvec, mvec), lanes(mvec, nout)], axis=0
    )
    totals[...] = lax.dot_general(
        jnp.ones((1, parts.shape[1]), F32),
        parts,
        (((1,), (1,)), ((), ())),
        precision=lax.Precision.HIGHEST,
        preferred_element_type=F32,
    )


def finish_kernel(shares, nvec, rflat, zflat, wflat, mflat, sol, res):
    nblk, ncol, bdof = nvec.shape
    flatten(lambda first, last: nvec[first:last], nvec.shape, res)
    total = jnp.sum(shares[...], axis=0, keepdims=True)
    gamma, delta, mu, nu = [total[:, q * ncol : (q + 1) * ncol] for q in range(4)]
    alpha = gamma / delta
    gnew = gamma - 2.0 * alpha * delta + alpha * alpha * mu
    grow = 1.0 + gnew / gamma
    dnew = grow * grow * delta - 2.0 * alpha * grow * mu + alpha * alpha * nu
    anew = gnew / dnew
    both, second = [
        jnp.concatenate([x] * (LANES // ncol), axis=1)
        for x in (alpha + anew * grow, anew * alpha)
    ]
    for j in range(sol.shape[1] // LANES):
        here = slice(j * LANES, (j + 1) * LANES)
        sol[:, here] = both * zflat[:, here] - second * mflat[:, here]
        res[:, here] = rflat[:, here] - both * wflat[:, here] + second * res[:, here]


def call(kernel, outs, scratch, args, space=pltpu.VMEM):
    vmem = pl.BlockSpec(memory_space=pltpu.VMEM)
    if space != pltpu.VMEM:
        args = [pltpu.with_memory_space_constraint(arg, space) for arg in args]
    return pl.pallas_call(
        kernel,
        out_shape=outs,
        in_specs=[pl.BlockSpec(memory_space=space)] * len(args),
        out_specs=jax.tree.map(lambda _: vmem, outs),
        scratch_shapes=scratch,
        compiler_params=pltpu.CompilerParams(vmem_limit_bytes=VMEM_LIMIT),
    )(*args)


def everywhere(values):
    total = lax.axis_size("dam") * lax.axis_size("sec")
    copies = jnp.broadcast_to(values[None], (total,) + values.shape)
    return lax.all_to_all(copies, ("dam", "sec"), split_axis=0, concat_axis=0)


def exchange(sends, axis):
    size = lax.axis_size(axis)
    got = []
    for first, send in zip((1, 0), sends):
        pairs = [(i, i + 1) for i in range(first, size - 1, 2)]
        got.append(lax.ppermute(send, axis, pairs + [(j, i) for i, j in pairs]))
    return got


def shards(
    segment_load,
    segment_mask,
    stiffness,
    block_cols,
    capillary,
    dirichlet_blocks,
    face_map,
    face_weight,
    corner_map,
    coarse_inverse,
):
    nblk, bdof = capillary.shape[2:]
    ncol = segment_load.shape[-1] // bdof
    nface = face_map.shape[3]
    ncorner = corner_map.shape[2]
    size = nblk * bdof
    pair = lax.axis_size("sec") == 2
    load, mask = segment_load[0, 0], segment_mask[0, 0]
    cols = jnp.transpose(block_cols[0], (2, 0, 1))
    tang, weights = capillary[0, 0], face_weight[0, 0]
    blocks, rows = dirichlet_blocks[0, 0], coarse_inverse[0]

    def shape(*dims, dtype=F32):
        return jax.ShapeDtypeStruct(dims, dtype)

    def like(array):
        return shape(*array.shape, dtype=array.dtype)

    def hold(array):
        return pltpu.VMEM(array.shape, array.dtype)

    def index(array):
        return pltpu.SMEM(array.shape, array.dtype)

    def sems(count):
        return pltpu.SemaphoreType.DMA((count,))

    field = shape(nblk, ncol, bdof)
    flat = shape(nblk, bdof * ncol)
    face = shape(ncol, nface * bdof)
    group = ncorner * bdof
    tiles = shape(size // group, group, group, dtype=BF16)
    halved = pltpu.VMEM((size // group, 2 * ncol, group), BF16)
    lane = group + nface * bdof if pair else group
    marked = ncol + 8 if pair else ncol

    rvec, base, payload, high, low, cmap, met, weights, rows, cols, tang = call(
        functools.partial(start_kernel, pair),
        (field, field, shape(marked, lane), tiles, tiles)
        + (shape(1, ncorner, dtype=jnp.int32), shape(4, nface, dtype=jnp.int32))
        + tuple(like(a) for a in (weights, rows, cols, tang)),
        [
            hold(load),
            hold(mask),
            hold(blocks),
            index(corner_map),
            hold(corner_map),
            index(face_map),
            hold(face_map),
            hold(weights),
            halved,
            sems(11),
        ],
        (load, mask, corner_map, face_map, blocks, rows, cols, weights, tang),
        pltpu.HBM,
    )

    def finish(base, shares, marks):
        vec, *faces = call(
            functools.partial(end_kernel, pair),
            (field,) + (face,) * (3 if pair else 4),
            [],
            (cmap, met, base, rows, shares, marks),
        )
        besides = exchange(faces[:2], "dam")
        besides += faces[2:] if pair else exchange(faces[2:], "sec")
        return vec, besides

    def local(vec, other):
        return call(
            local_kernel,
            (field, flat, flat),
            [pltpu.VMEM((nblk, 2 * ncol, bdof), BF16), index(cols), sems(1)],
            (cols, met, weights, tang, vec, other, stiffness[0, 0]),
        )

    marks = lax.all_gather(payload, "sec")
    zvec, besides = finish(base, marks, marks)
    part, zflat, rflat = local(zvec, rvec)
    wvec, sums, base, payload = call(
        functools.partial(image_kernel, pair),
        (field, shape(2, ncol, bdof), field, shape(ncol, lane)),
        [halved],
        (cmap, met, weights, part, rvec, zvec, high, low, rows, *besides),
    )
    mvec, besides = finish(base, lax.all_gather(payload, "sec"), marks)
    part, mflat, wflat = local(mvec, wvec)
    nvec, totals = call(
        last_kernel,
        (field, shape(1, 4 * ncol)),
        [],
        (met, weights, part, wvec, mvec, sums, *besides),
    )
    sol, res = call(
        finish_kernel,
        (flat, flat),
        [],
        (everywhere(totals[0]), nvec, rflat, zflat, wflat, mflat),
    )
    return sol[None, None], res[None, None]


def solution(mesh):
    placed = (
        P("dam", "sec", None, None),
        P("dam", "sec", None, None),
        P("dam", "sec", None, None, None),
        P("dam", "sec", None, None),
        P("dam", "sec", None, None),
        P("dam", "sec", None, None, None),
        P("dam", "sec", None, None),
        P("dam", "sec", None, None),
        P("dam", "sec", None),
        P("dam", "sec", None),
    )
    return jax.shard_map(
        shards,
        mesh=mesh,
        in_specs=placed,
        out_specs=(P("dam", "sec", None, None), P("dam", "sec", None, None)),
        check_vma=False,
    )
```

```python
import functools

import jax
import jax.numpy as jnp
from jax import lax
from jax.experimental import pallas as pl
from jax.experimental.pallas import tpu as pltpu
from jax.sharding import PartitionSpec as P

F32 = jnp.float32
BF16 = jnp.bfloat16
VMEM_LIMIT = 16 * 1024 * 1024
LANES = 128
PIECES = 4


def halves(x):
    high = x.astype(BF16)
    return high, (x - high.astype(F32)).astype(BF16)


def stack(x):
    return jnp.concatenate(halves(x), axis=0)


def dot_t(a, b):
    return lax.dot_general(a, b, (((1,), (1,)), ((), ())), preferred_element_type=F32)


def dot(a, b):
    return lax.dot_general(a, b, (((1,), (0,)), ((), ())), preferred_element_type=F32)


def three_pass(mul, left, high, low):
    rows = left.shape[0] // 2
    first = mul(left, high)
    return first[:rows] + first[rows:] + mul(left[:rows], low)


def fetch(pairs, sems):
    copies = [
        pltpu.make_async_copy(source, target, sems.at[i])
        for i, (source, target) in enumerate(pairs)
    ]
    for copy in copies:
        copy.start()
    return [copy.wait for copy in copies]


def pieces(source, target, count):
    step = source.shape[0] // count
    return [
        (source.at[i * step : (i + 1) * step], target.at[i * step : (i + 1) * step])
        for i in range(count)
    ]


def face_order(pair):
    near = 1 - lax.axis_index("dam") % 2
    across = 3 - lax.axis_index("sec") % 2
    return [1 - near, near] + ([across, 5 - across] if pair else [5 - across, across])


def listed(index):
    value = index[...]
    return [[value[i, j] for j in range(value.shape[1])] for i in range(value.shape[0])]


def pack(field, where, out, at=0):
    ncol, bdof = field.shape[1:]
    for p, b in enumerate(where):
        out[:ncol, at + p * bdof : at + (p + 1) * bdof] = field[b]


def add_pieces(field, where, piece):
    new = [field[b] + piece(p, b) for p, b in enumerate(where)]
    for b, value in zip(where, new):
        field[b] = value


def lane_piece(x, p, bdof):
    return x[:, p * bdof : (p + 1) * bdof]


def split_blocks(blocks, tiles_high, tiles_low):
    nblk, bdof = blocks.shape[:2]
    group = tiles_high.shape[1] // bdof
    for b in range(nblk):
        t, j = divmod(b, group)
        here = slice(j * bdof, (j + 1) * bdof)
        tiles_high[t, here, here], tiles_low[t, here, here] = halves(blocks[b])


def apply_blocks(field, tiles_high, tiles_low, left, base):
    nblk, ncol, bdof = field.shape
    group = tiles_high.shape[1] // bdof
    for b in range(nblk):
        t, j = divmod(b, group)
        here = slice(j * bdof, (j + 1) * bdof)
        left[t, :ncol, here], left[t, ncol:, here] = halves(field[b])
    for t in range(nblk // group):
        out = three_pass(dot, left[t], tiles_high[t], tiles_low[t])
        for j in range(group):
            base[t * group + j] = lane_piece(out, j, bdof)


def offer(pair, corners, across, field, rows, base, payload):
    bdof = field.shape[2]
    if not pair:
        pack(field, corners, payload)
        return
    wide = len(corners) * bdof
    at = payload.shape[1] - wide
    me = lax.axis_index("sec")
    own = stack(jnp.concatenate([field[b] for b in corners], axis=1))
    mine = pl.multiple_of(me * wide, wide)
    other = pl.multiple_of((1 - me) * wide, wide)
    correct = three_pass(dot_t, own, *halves(rows[:, pl.ds(mine, wide)]))
    payload[: field.shape[1], at:] = three_pass(dot, own, *halves(rows[:, pl.ds(other, wide)]))
    add_pieces(base, corners, lambda n, b: lane_piece(correct, n, bdof))
    pack(base, across, payload)


def end_kernel(pair, cmap, met, base, rows, shares, marks, zout, *faces):
    nblk, ncol, bdof = base.shape
    (corners,) = listed(cmap)
    where = listed(met)
    wide = len(corners) * bdof
    zout[...] = base[...]
    if pair:
        me = lax.axis_index("sec")
        at = len(where[0]) * bdof
        correct = shares[pl.ds(1 - me, 1), :ncol, at:][0]
        theirs = shares[pl.ds(me, 1), :ncol, at:][0]
        chunk = 2 * bdof
        twice = [
            jnp.concatenate([lane_piece(theirs, n, bdof)] * 2, axis=1)
            for n in range(len(corners))
        ]
        for j in range(at // chunk):
            here = slice(j * chunk, (j + 1) * chunk)
            value = shares[pl.ds(1 - me, 1), :ncol, here][0]
            for n in range(len(corners)):
                mark = marks[pl.ds(1 - me, 1), ncol + n : ncol + n + 1, here][0]
                value = value + mark * twice[n]
            faces[-1][:, here] = value
    else:
        correct = 0.0
        for s in range(shares.shape[0]):
            high, low = halves(rows[:, s * wide : (s + 1) * wide])
            correct = correct + three_pass(dot_t, stack(shares[s]), high, low)
    add_pieces(zout, corners, lambda n, b: lane_piece(correct, n, bdof))
    for blocks, out in zip(where, faces[: 2 if pair else 4]):
        pack(zout, blocks, out)


def swap_groups(x, ncol):
    subs, lanes_at = x.shape[1:]
    sub = lax.broadcasted_iota(jnp.int32, x.shape, 1)
    lane = lax.broadcasted_iota(jnp.int32, x.shape, 2)
    step = 1
    while step < subs:
        move = step * ncol
        low, left = (sub & step) == 0, (lane & move) == 0
        up = pltpu.roll(pltpu.roll(x, subs - step, 1), move, 2)
        down = pltpu.roll(pltpu.roll(x, step, 1), lanes_at - move, 2)
        x = jnp.where(low == left, x, jnp.where(low, up, down))
        step *= 2
    return x


def flatten(part, shape, out):
    nblk, ncol, bdof = shape
    subs = LANES // ncol
    for first in range(0, nblk, subs):
        tall = part(first, first + subs).reshape(LANES, bdof).T
        tall = swap_groups(tall.reshape(bdof // subs, subs, LANES), ncol)
        for j in range(bdof // subs):
            out[first : first + subs, j * LANES : (j + 1) * LANES] = tall[j]


def unflatten(part, shape, out):
    nblk, ncol, bdof = shape
    subs = LANES // ncol
    for first in range(0, nblk, subs):
        parts = [part(first, first + subs, j)[None] for j in range(bdof // subs)]
        tall = swap_groups(jnp.concatenate(parts, axis=0), ncol).reshape(bdof, LANES)
        out[first : first + subs] = tall.T.reshape(subs, ncol, bdof)


def start_kernel(pair, *refs):
    load_in, mask_in, cmap_in, fmap_in, blocks_in, rows_in, cols_in, weights_in, tang_in = refs[:9]
    rvec, base, payload, tiles_high, tiles_low, cmap_out, met, wmet, rows, cols, tang = refs[9:20]
    load, mask, blocks, cmap, cmap_row, fmap, fmap_rows, weights, left, sems = refs[20:]
    waits = fetch(
        [
            (load_in, load),
            (mask_in, mask),
            (cmap_in, cmap),
            (fmap_in, fmap),
            (cmap_in, cmap_row),
            (fmap_in, fmap_rows),
            (weights_in, weights),
            (cols_in, cols),
            (tang_in, tang),
        ]
        + pieces(blocks_in, blocks, PIECES)
        + pieces(rows_in, rows, PIECES),
        sems,
    )
    nblk, ncol, bdof = rvec.shape
    order = face_order(pair)
    tiles_high[...] = jnp.zeros_like(tiles_high)
    tiles_low[...] = jnp.zeros_like(tiles_low)
    waits[2]()
    waits[3]()
    corners = [cmap[0, 0, n] for n in range(cmap.shape[2])]
    across = [fmap[0, 0, order[2], p] for p in range(fmap.shape[3])]
    if pair:
        payload[ncol:, :] = jnp.zeros_like(payload[ncol:, :])
        for n, corner in enumerate(corners):
            for p, b in enumerate(across):
                payload[ncol + n : ncol + n + 1, p * bdof : (p + 1) * bdof] = jnp.full(
                    (1, bdof), jnp.where(corner == b, 1.0, 0.0), F32
                )
    for wait in waits[:2]:
        wait()
    scale = mask[...].astype(F32)
    scale = jnp.concatenate([scale] * (LANES // ncol), axis=1)
    unflatten(
        lambda first, last, j: load[first:last, j * LANES : (j + 1) * LANES]
        * scale[first:last],
        rvec.shape,
        rvec,
    )
    for wait in waits[9 : 9 + PIECES]:
        wait()
    split_blocks(blocks, tiles_high, tiles_low)
    apply_blocks(rvec, tiles_high, tiles_low, left, base)
    for wait in waits[9 + PIECES :] + waits[4:9]:
        wait()
    offer(pair, corners, across, rvec, rows, base, payload)
    cmap_out[...] = cmap_row[0]
    for i, face in enumerate(order):
        met[i : i + 1, :] = fmap_rows[0, 0, pl.ds(face, 1), :]
        wmet[i : i + 1, :] = weights[pl.ds(face, 1), :]


def local_kernel(
    first, cols_in, met, weights, capillary, field, other, stiff, out, flat, other_flat, *scratch
):
    left, cols, sems = scratch[-3:]
    copies = [(cols_in, cols)]
    if first:
        copies += pieces(stiff, scratch[0], 2 * PIECES)
        stiff = scratch[0]
    nblk, ncol, bdof = field.shape
    waits = fetch(copies, sems)
    where = listed(met)
    flatten(lambda first, last: field[first:last], field.shape, flat)
    flatten(lambda first, last: other[first:last], field.shape, other_flat)
    kept = stiff.shape[2] // bdof
    for b in range(nblk):
        left[b] = stack(field[b])
    waits.pop(0)()
    group = nblk // PIECES
    for t in range(0, nblk, group):
        for wait in waits[:2]:
            wait()
        waits = waits[2:]
        gathered = [
            jnp.concatenate([left[cols[k, 0, t + j]] for k in range(kept)], axis=1)
            for j in range(group)
        ]
        firsts = [g[:ncol] for g in gathered]
        seconds = [g[ncol:] for g in gathered]
        rows = stiff[t : t + group].reshape(group * bdof, kept * bdof)
        prod = three_pass(dot_t, jnp.concatenate(firsts + seconds, axis=0), *halves(rows))
        for j in range(group):
            out[t + j] = (
                lane_piece(prod[j * ncol : (j + 1) * ncol], j, bdof)
                + capillary[t + j : t + j + 1, :] * field[t + j]
            )
    for i, blocks in enumerate(where):
        row = weights[i : i + 1, :]
        add_pieces(out, blocks, lambda p, b: lane_piece(row, p, bdof) * field[b])


def couple(met, weights, local, besides, out):
    bdof = local.shape[2]
    where = listed(met)
    out[...] = local[...]
    for i, beside in enumerate(besides):
        term = weights[i : i + 1, :] * beside[...]
        add_pieces(out, where[i], lambda p, b: -lane_piece(term, p, bdof))
    return where


def lanes(first, second):
    return jnp.sum(first[...] * second[...], axis=0)


def image_kernel(
    pair, cmap, met, weights, local, rvec, zvec, tiles_high, tiles_low, rows, *rest
):
    count = 3 if pair else 4
    besides, (wout, sums, base, payload, left) = rest[:count], rest[count:]
    (corners,) = listed(cmap)
    where = couple(met, weights, local, besides, wout)
    apply_blocks(wout, tiles_high, tiles_low, left, base)
    offer(pair, corners, where[2], wout, rows, base, payload)
    sums[0] = lanes(rvec, zvec)
    sums[1] = lanes(zvec, wout)


def last_kernel(met, weights, local, wvec, mvec, sums, *rest):
    *besides, nout, totals = rest
    couple(met, weights, local, besides, nout)
    parts = jnp.concatenate(
        [sums[0], sums[1], lanes(wvec, mvec), lanes(mvec, nout)], axis=0
    )
    totals[...] = lax.dot_general(
        jnp.ones((1, parts.shape[1]), F32),
        parts,
        (((1,), (1,)), ((), ())),
        precision=lax.Precision.HIGHEST,
        preferred_element_type=F32,
    )


def finish_kernel(shares, nvec, rflat, zflat, wflat, mflat, sol, res):
    nblk, ncol, bdof = nvec.shape
    flatten(lambda first, last: nvec[first:last], nvec.shape, res)
    total = jnp.sum(shares[...], axis=0, keepdims=True)
    gamma, delta, mu, nu = [total[:, q * ncol : (q + 1) * ncol] for q in range(4)]
    alpha = gamma / delta
    gnew = gamma - 2.0 * alpha * delta + alpha * alpha * mu
    grow = 1.0 + gnew / gamma
    dnew = grow * grow * delta - 2.0 * alpha * grow * mu + alpha * alpha * nu
    anew = gnew / dnew
    both, second = [
        jnp.concatenate([x] * (LANES // ncol), axis=1)
        for x in (alpha + anew * grow, anew * alpha)
    ]
    for j in range(sol.shape[1] // LANES):
        here = slice(j * LANES, (j + 1) * LANES)
        sol[:, here] = both * zflat[:, here] - second * mflat[:, here]
        res[:, here] = rflat[:, here] - both * wflat[:, here] + second * res[:, here]


def call(kernel, outs, scratch, args, far=()):
    vmem = pl.BlockSpec(memory_space=pltpu.VMEM)
    hbm = pl.BlockSpec(memory_space=pltpu.HBM)
    far = [pltpu.with_memory_space_constraint(arg, pltpu.HBM) for arg in far]
    return pl.pallas_call(
        kernel,
        out_shape=outs,
        in_specs=[vmem] * len(args) + [hbm] * len(far),
        out_specs=jax.tree.map(lambda _: vmem, outs),
        scratch_shapes=scratch,
        compiler_params=pltpu.CompilerParams(vmem_limit_bytes=VMEM_LIMIT),
    )(*args, *far)


def everywhere(values):
    total = lax.axis_size("dam") * lax.axis_size("sec")
    copies = jnp.broadcast_to(values[None], (total,) + values.shape)
    return lax.all_to_all(copies, ("dam", "sec"), split_axis=0, concat_axis=0)


def exchange(sends, axis):
    size = lax.axis_size(axis)
    got = []
    for first, send in zip((1, 0), sends):
        pairs = [(i, i + 1) for i in range(first, size - 1, 2)]
        got.append(lax.ppermute(send, axis, pairs + [(j, i) for i, j in pairs]))
    return got


def shards(
    segment_load,
    segment_mask,
    stiffness,
    block_cols,
    capillary,
    dirichlet_blocks,
    face_map,
    face_weight,
    corner_map,
    coarse_inverse,
):
    nblk, bdof = capillary.shape[2:]
    ncol = segment_load.shape[-1] // bdof
    nface = face_map.shape[3]
    ncorner = corner_map.shape[2]
    size = nblk * bdof
    pair = lax.axis_size("sec") == 2
    load, mask = segment_load[0, 0], segment_mask[0, 0]
    cols = jnp.transpose(block_cols[0], (2, 0, 1))
    tang, weights = capillary[0, 0], face_weight[0, 0]
    blocks, rows = dirichlet_blocks[0, 0], coarse_inverse[0]

    def shape(*dims, dtype=F32):
        return jax.ShapeDtypeStruct(dims, dtype)

    def like(array):
        return shape(*array.shape, dtype=array.dtype)

    def hold(array):
        return pltpu.VMEM(array.shape, array.dtype)

    def index(array):
        return pltpu.SMEM(array.shape, array.dtype)

    def sems(count):
        return pltpu.SemaphoreType.DMA((count,))

    field = shape(nblk, ncol, bdof)
    flat = shape(nblk, bdof * ncol)
    face = shape(ncol, nface * bdof)
    group = ncorner * bdof
    tiles = shape(size // group, group, group, dtype=BF16)
    halved = pltpu.VMEM((size // group, 2 * ncol, group), BF16)
    lane = group + nface * bdof if pair else group
    marked = ncol + 8 if pair else ncol

    rvec, base, payload, high, low, cmap, met, weights, rows, cols, tang = call(
        functools.partial(start_kernel, pair),
        (field, field, shape(marked, lane), tiles, tiles)
        + (shape(1, ncorner, dtype=jnp.int32), shape(4, nface, dtype=jnp.int32))
        + tuple(like(a) for a in (weights, rows, cols, tang)),
        [
            hold(load),
            hold(mask),
            hold(blocks),
            index(corner_map),
            hold(corner_map),
            index(face_map),
            hold(face_map),
            hold(weights),
            halved,
            sems(9 + 2 * PIECES),
        ],
        (),
        (load, mask, corner_map, face_map, blocks, rows, cols, weights, tang),
    )

    def finish(base, shares, marks):
        vec, *faces = call(
            functools.partial(end_kernel, pair),
            (field,) + (face,) * (3 if pair else 4),
            [],
            (cmap, met, base, rows, shares, marks),
        )
        besides = exchange(faces[:2], "dam")
        besides += faces[2:] if pair else exchange(faces[2:], "sec")
        return vec, besides

    def local(vec, other, near, far):
        return call(
            functools.partial(local_kernel, bool(far)),
            (field, flat, flat) + tuple(like(a) for a in far),
            [pltpu.VMEM((nblk, 2 * ncol, bdof), BF16), index(cols), sems(1 + 2 * PIECES)],
            (cols, met, weights, tang, vec, other) + near,
            far,
        )

    marks = lax.all_gather(payload, "sec")
    zvec, besides = finish(base, marks, marks)
    part, zflat, rflat, stiff = local(zvec, rvec, (), (stiffness[0, 0],))
    wvec, sums, base, payload = call(
        functools.partial(image_kernel, pair),
        (field, shape(2, ncol, bdof), field, shape(ncol, lane)),
        [halved],
        (cmap, met, weights, part, rvec, zvec, high, low, rows, *besides),
    )
    mvec, besides = finish(base, lax.all_gather(payload, "sec"), marks)
    part, mflat, wflat = local(mvec, wvec, (stiff,), ())
    nvec, totals = call(
        last_kernel,
        (field, shape(1, 4 * ncol)),
        [],
        (met, weights, part, wvec, mvec, sums, *besides),
    )
    sol, res = call(
        finish_kernel,
        (flat, flat),
        [],
        (everywhere(totals[0]), nvec, rflat, zflat, wflat, mflat),
    )
    return sol[None, None], res[None, None]


def solution(mesh):
    placed = (
        P("dam", "sec", None, None),
        P("dam", "sec", None, None),
        P("dam", "sec", None, None, None),
        P("dam", "sec", None, None),
        P("dam", "sec", None, None),
        P("dam", "sec", None, None, None),
        P("dam", "sec", None, None),
        P("dam", "sec", None, None),
        P("dam", "sec", None),
        P("dam", "sec", None),
    )
    return jax.shard_map(
        shards,
        mesh=mesh,
        in_specs=placed,
        out_specs=(P("dam", "sec", None, None), P("dam", "sec", None, None)),
        check_vma=False,
    )
```

```python
import functools

import jax
import jax.numpy as jnp
from jax import lax
from jax.experimental import pallas as pl
from jax.experimental.pallas import tpu as pltpu
from jax.sharding import PartitionSpec as P

F32 = jnp.float32
BF16 = jnp.bfloat16
VMEM_LIMIT = 16 * 1024 * 1024
LANES = 128
PIECES = 4


def halves(x):
    high = x.astype(BF16)
    return high, (x - high.astype(F32)).astype(BF16)


def stack(x):
    return jnp.concatenate(halves(x), axis=0)


def dot_t(a, b):
    return lax.dot_general(a, b, (((1,), (1,)), ((), ())), preferred_element_type=F32)


def dot(a, b):
    return lax.dot_general(a, b, (((1,), (0,)), ((), ())), preferred_element_type=F32)


def three_pass(mul, left, high, low):
    rows = left.shape[0] // 2
    first = mul(left, high)
    return first[:rows] + first[rows:] + mul(left[:rows], low)


def fetch(pairs, sems):
    copies = [
        pltpu.make_async_copy(source, target, sems.at[i])
        for i, (source, target) in enumerate(pairs)
    ]
    for copy in copies:
        copy.start()
    return [copy.wait for copy in copies]


def pieces(source, target, count):
    step = source.shape[0] // count
    return [
        (source.at[i * step : (i + 1) * step], target.at[i * step : (i + 1) * step])
        for i in range(count)
    ]


def face_order(pair):
    near = 1 - lax.axis_index("dam") % 2
    across = 3 - lax.axis_index("sec") % 2
    return [1 - near, near] + ([across, 5 - across] if pair else [5 - across, across])


def listed(index):
    value = index[...]
    return [[value[i, j] for j in range(value.shape[1])] for i in range(value.shape[0])]


def pack(field, where, out, at=0):
    ncol, bdof = field.shape[1:]
    for p, b in enumerate(where):
        out[:ncol, at + p * bdof : at + (p + 1) * bdof] = field[b]


def add_pieces(field, where, piece):
    new = [field[b] + piece(p, b) for p, b in enumerate(where)]
    for b, value in zip(where, new):
        field[b] = value


def lane_piece(x, p, bdof):
    return x[:, p * bdof : (p + 1) * bdof]


def split_blocks(blocks, tiles_high, tiles_low):
    nblk, bdof = blocks.shape[:2]
    group = tiles_high.shape[1] // bdof
    for b in range(nblk):
        t, j = divmod(b, group)
        here = slice(j * bdof, (j + 1) * bdof)
        tiles_high[t, here, here], tiles_low[t, here, here] = halves(blocks[b])


def apply_blocks(field, tiles_high, tiles_low, left, base):
    nblk, ncol, bdof = field.shape
    group = tiles_high.shape[1] // bdof
    for b in range(nblk):
        t, j = divmod(b, group)
        here = slice(j * bdof, (j + 1) * bdof)
        left[t, :ncol, here], left[t, ncol:, here] = halves(field[b])
    for t in range(nblk // group):
        out = three_pass(dot, left[t], tiles_high[t], tiles_low[t])
        for j in range(group):
            base[t * group + j] = lane_piece(out, j, bdof)


def offer(pair, corners, across, field, rows, base, payload):
    bdof = field.shape[2]
    if not pair:
        pack(field, corners, payload)
        return
    wide = len(corners) * bdof
    at = payload.shape[1] - wide
    me = lax.axis_index("sec")
    own = stack(jnp.concatenate([field[b] for b in corners], axis=1))
    mine = pl.multiple_of(me * wide, wide)
    other = pl.multiple_of((1 - me) * wide, wide)
    correct = three_pass(dot_t, own, *halves(rows[:, pl.ds(mine, wide)]))
    payload[: field.shape[1], at:] = three_pass(dot, own, *halves(rows[:, pl.ds(other, wide)]))
    add_pieces(base, corners, lambda n, b: lane_piece(correct, n, bdof))
    pack(base, across, payload)


def end_kernel(pair, cmap, met, base, rows, shares, zout, *faces):
    nblk, ncol, bdof = base.shape
    (corners,) = listed(cmap)
    where = listed(met)
    wide = len(corners) * bdof
    zout[...] = base[...]
    if pair:
        at = len(where[0]) * bdof
        correct = shares[pl.ds(1 - lax.axis_index("sec"), 1), :ncol, at:][0]
    else:
        correct = 0.0
        for s in range(shares.shape[0]):
            high, low = halves(rows[:, s * wide : (s + 1) * wide])
            correct = correct + three_pass(dot_t, stack(shares[s]), high, low)
    add_pieces(zout, corners, lambda n, b: lane_piece(correct, n, bdof))
    for blocks, out in zip(where, faces):
        pack(zout, blocks, out)


def face_across(shares, labels, nface, shape, out):
    nblk, ncol, bdof = shape
    at = nface * bdof
    me = lax.axis_index("sec")
    names = labels[pl.ds(1 - me, 1), ncol : ncol + 2, : LANES][0]
    for p in range(nface):
        value = shares[pl.ds(1 - me, 1), :ncol, p * bdof : (p + 1) * bdof][0]
        for n in range((shares.shape[2] - at) // bdof):
            here = slice(at + n * bdof, at + (n + 1) * bdof)
            same = jnp.where(names[0, n] == names[1, p], 1.0, 0.0)
            value = value + same * shares[pl.ds(me, 1), :ncol, here][0]
        out[:, p * bdof : (p + 1) * bdof] = value


def swap_groups(x, ncol):
    subs, lanes_at = x.shape[1:]
    sub = lax.broadcasted_iota(jnp.int32, x.shape, 1)
    lane = lax.broadcasted_iota(jnp.int32, x.shape, 2)
    step = 1
    while step < subs:
        move = step * ncol
        low, left = (sub & step) == 0, (lane & move) == 0
        up = pltpu.roll(pltpu.roll(x, subs - step, 1), move, 2)
        down = pltpu.roll(pltpu.roll(x, step, 1), lanes_at - move, 2)
        x = jnp.where(low == left, x, jnp.where(low, up, down))
        step *= 2
    return x


def flatten(part, shape, out):
    nblk, ncol, bdof = shape
    subs = LANES // ncol
    for first in range(0, nblk, subs):
        tall = part(first, first + subs).reshape(LANES, bdof).T
        tall = swap_groups(tall.reshape(bdof // subs, subs, LANES), ncol)
        for j in range(bdof // subs):
            out[first : first + subs, j * LANES : (j + 1) * LANES] = tall[j]


def unflatten(part, shape, out):
    nblk, ncol, bdof = shape
    subs = LANES // ncol
    for first in range(0, nblk, subs):
        parts = [part(first, first + subs, j)[None] for j in range(bdof // subs)]
        tall = swap_groups(jnp.concatenate(parts, axis=0), ncol).reshape(bdof, LANES)
        out[first : first + subs] = tall.T.reshape(subs, ncol, bdof)


def start_kernel(pair, *refs):
    load_in, mask_in, cmap_in, fmap_in, blocks_in, rows_in, cols_in, weights_in, tang_in = refs[:9]
    rvec, base, payload, tiles_high, tiles_low, cmap_out, met, wmet, rows, cols, tang = refs[9:20]
    load, mask, blocks, cmap, cmap_row, fmap, fmap_rows, weights, left, sems = refs[20:]
    waits = fetch(
        [
            (load_in, load),
            (mask_in, mask),
            (cmap_in, cmap),
            (fmap_in, fmap),
            (cmap_in, cmap_row),
            (fmap_in, fmap_rows),
            (weights_in, weights),
            (cols_in, cols),
            (tang_in, tang),
        ]
        + pieces(blocks_in, blocks, PIECES)
        + pieces(rows_in, rows, PIECES),
        sems,
    )
    nblk, ncol, bdof = rvec.shape
    order = face_order(pair)
    tiles_high[...] = jnp.zeros_like(tiles_high)
    tiles_low[...] = jnp.zeros_like(tiles_low)
    waits[2]()
    waits[3]()
    corners = [cmap[0, 0, n] for n in range(cmap.shape[2])]
    across = [fmap[0, 0, order[2], p] for p in range(fmap.shape[3])]
    for wait in waits[:2]:
        wait()
    scale = mask[...].astype(F32)
    scale = jnp.concatenate([scale] * (LANES // ncol), axis=1)
    unflatten(
        lambda first, last, j: load[first:last, j * LANES : (j + 1) * LANES]
        * scale[first:last],
        rvec.shape,
        rvec,
    )
    for wait in waits[9 : 9 + PIECES]:
        wait()
    split_blocks(blocks, tiles_high, tiles_low)
    apply_blocks(rvec, tiles_high, tiles_low, left, base)
    for wait in waits[9 + PIECES :] + waits[4:9]:
        wait()
    offer(pair, corners, across, rvec, rows, base, payload)
    cmap_out[...] = cmap_row[0]
    if pair:
        payload[ncol:, :] = jnp.zeros_like(payload[ncol:, :])
        payload[ncol : ncol + 1, : len(corners)] = cmap_row[0].astype(F32)
        payload[ncol + 1 : ncol + 2, : len(across)] = fmap_rows[
            0, 0, pl.ds(order[2], 1), :
        ].astype(F32)
    for i, face in enumerate(order):
        met[i : i + 1, :] = fmap_rows[0, 0, pl.ds(face, 1), :]
        wmet[i : i + 1, :] = weights[pl.ds(face, 1), :]


def local_kernel(
    pair, cols_in, met, weights, capillary, field, other, stiff, shares, labels, *rest
):
    out, sums, flat, other_flat, *across, left, cols, sems = rest
    nblk, ncol, bdof = field.shape
    (wait,) = fetch([(cols_in, cols)], sems)
    where = listed(met)
    if pair:
        face_across(shares, labels, len(where[2]), field.shape, across[0])
    sums[...] = lanes(field, other)
    flatten(lambda first, last: field[first:last], field.shape, flat)
    flatten(lambda first, last: other[first:last], field.shape, other_flat)
    kept = stiff.shape[2] // bdof
    for b in range(nblk):
        left[b] = stack(field[b])
    wait()
    group = 4
    for t in range(0, nblk, group):
        gathered = [
            jnp.concatenate([left[cols[k, 0, t + j]] for k in range(kept)], axis=1)
            for j in range(group)
        ]
        firsts = [g[:ncol] for g in gathered]
        seconds = [g[ncol:] for g in gathered]
        rows = stiff[t : t + group].reshape(group * bdof, kept * bdof)
        prod = three_pass(dot_t, jnp.concatenate(firsts + seconds, axis=0), *halves(rows))
        for j in range(group):
            out[t + j] = (
                lane_piece(prod[j * ncol : (j + 1) * ncol], j, bdof)
                + capillary[t + j : t + j + 1, :] * field[t + j]
            )
    for i, blocks in enumerate(where):
        row = weights[i : i + 1, :]
        add_pieces(out, blocks, lambda p, b: lane_piece(row, p, bdof) * field[b])


def couple(met, weights, local, besides, out):
    bdof = local.shape[2]
    where = listed(met)
    out[...] = local[...]
    for i, beside in enumerate(besides):
        term = weights[i : i + 1, :] * beside[...]
        add_pieces(out, where[i], lambda p, b: -lane_piece(term, p, bdof))
    return where


def lanes(first, second):
    return jnp.sum(first[...] * second[...], axis=0)


def image_kernel(
    pair, cmap, met, weights, local, zvec, tiles_high, tiles_low, rows, *rest
):
    count = 3 if pair else 4
    besides, (wout, sums, base, payload, left) = rest[:count], rest[count:]
    (corners,) = listed(cmap)
    where = couple(met, weights, local, besides, wout)
    apply_blocks(wout, tiles_high, tiles_low, left, base)
    offer(pair, corners, where[2], wout, rows, base, payload)
    sums[...] = lanes(zvec, wout)


def last_kernel(met, weights, local, rvec, zvec, mvec, gamma, delta, mu, *rest):
    *besides, nout, totals = rest
    rm = lanes(rvec, mvec)
    couple(met, weights, local, besides, nout)
    parts = [gamma[...], delta[...], mu[...], rm, lanes(mvec, nout), lanes(zvec, nout)]
    parts = jnp.concatenate(parts, axis=0)
    totals[...] = lax.dot_general(
        jnp.ones((1, parts.shape[1]), F32),
        parts,
        (((1,), (1,)), ((), ())),
        precision=lax.Precision.HIGHEST,
        preferred_element_type=F32,
    )


def finish_kernel(shares, nvec, rflat, zflat, wflat, mflat, sol, res):
    nblk, ncol, bdof = nvec.shape
    flatten(lambda first, last: nvec[first:last], nvec.shape, res)
    total = jnp.sum(shares[...], axis=0, keepdims=True)
    gamma, delta, mu, rm, nu, zn = [total[:, q * ncol : (q + 1) * ncol] for q in range(6)]
    alpha = gamma / delta
    gnew = gamma - alpha * (delta + rm) + alpha * alpha * mu
    grow = 1.0 + gnew / gamma
    dnew = grow * grow * delta - alpha * grow * (mu + zn) + alpha * alpha * nu
    anew = gnew / dnew
    both, second = [
        jnp.concatenate([x] * (LANES // ncol), axis=1)
        for x in (alpha + anew * grow, anew * alpha)
    ]
    for j in range(sol.shape[1] // LANES):
        here = slice(j * LANES, (j + 1) * LANES)
        sol[:, here] = both * zflat[:, here] - second * mflat[:, here]
        res[:, here] = rflat[:, here] - both * wflat[:, here] + second * res[:, here]


def call(kernel, outs, scratch, args, far=()):
    vmem = pl.BlockSpec(memory_space=pltpu.VMEM)
    hbm = pl.BlockSpec(memory_space=pltpu.HBM)
    far = [pltpu.with_memory_space_constraint(arg, pltpu.HBM) for arg in far]
    return pl.pallas_call(
        kernel,
        out_shape=outs,
        in_specs=[vmem] * len(args) + [hbm] * len(far),
        out_specs=jax.tree.map(lambda _: vmem, outs),
        scratch_shapes=scratch,
        compiler_params=pltpu.CompilerParams(vmem_limit_bytes=VMEM_LIMIT),
    )(*args, *far)


def everywhere(values):
    total = lax.axis_size("dam") * lax.axis_size("sec")
    copies = jnp.broadcast_to(values[None], (total,) + values.shape)
    return lax.all_to_all(copies, ("dam", "sec"), split_axis=0, concat_axis=0)


def exchange(sends, axis):
    size = lax.axis_size(axis)
    got = []
    for first, send in zip((1, 0), sends):
        pairs = [(i, i + 1) for i in range(first, size - 1, 2)]
        got.append(lax.ppermute(send, axis, pairs + [(j, i) for i, j in pairs]))
    return got


def shards(
    segment_load,
    segment_mask,
    stiffness,
    block_cols,
    capillary,
    dirichlet_blocks,
    face_map,
    face_weight,
    corner_map,
    coarse_inverse,
):
    nblk, bdof = capillary.shape[2:]
    ncol = segment_load.shape[-1] // bdof
    nface = face_map.shape[3]
    ncorner = corner_map.shape[2]
    size = nblk * bdof
    pair = lax.axis_size("sec") == 2
    load, mask = segment_load[0, 0], segment_mask[0, 0]
    cols = jnp.transpose(block_cols[0], (2, 0, 1))
    tang, weights = capillary[0, 0], face_weight[0, 0]
    blocks, rows = dirichlet_blocks[0, 0], coarse_inverse[0]

    def shape(*dims, dtype=F32):
        return jax.ShapeDtypeStruct(dims, dtype)

    def like(array):
        return shape(*array.shape, dtype=array.dtype)

    def hold(array):
        return pltpu.VMEM(array.shape, array.dtype)

    def index(array):
        return pltpu.SMEM(array.shape, array.dtype)

    def sems(count):
        return pltpu.SemaphoreType.DMA((count,))

    field = shape(nblk, ncol, bdof)
    flat = shape(nblk, bdof * ncol)
    face = shape(ncol, nface * bdof)
    group = ncorner * bdof
    tiles = shape(size // group, group, group, dtype=BF16)
    halved = pltpu.VMEM((size // group, 2 * ncol, group), BF16)
    lane = group + nface * bdof if pair else group
    marked = ncol + 8 if pair else ncol

    rvec, base, payload, high, low, cmap, met, weights, rows, cols, tang = call(
        functools.partial(start_kernel, pair),
        (field, field, shape(marked, lane), tiles, tiles)
        + (shape(1, ncorner, dtype=jnp.int32), shape(4, nface, dtype=jnp.int32))
        + tuple(like(a) for a in (weights, rows, cols, tang)),
        [
            hold(load),
            hold(mask),
            hold(blocks),
            index(corner_map),
            hold(corner_map),
            index(face_map),
            hold(face_map),
            hold(weights),
            halved,
            sems(9 + 2 * PIECES),
        ],
        (),
        (load, mask, corner_map, face_map, blocks, rows, cols, weights, tang),
    )

    def finish(base, shares):
        vec, *faces = call(
            functools.partial(end_kernel, pair),
            (field,) + (face,) * (2 if pair else 4),
            [],
            (cmap, met, base, rows, shares),
        )
        return vec, exchange(faces[:2], "dam"), exchange(faces[2:], "sec")

    def local(vec, other, shares, labels):
        part, sums, *rest = call(
            functools.partial(local_kernel, pair),
            (field, shape(ncol, bdof), flat, flat) + ((face,) if pair else ()),
            [pltpu.VMEM((nblk, 2 * ncol, bdof), BF16), index(cols), sems(1)],
            (cols, met, weights, tang, vec, other, stiffness[0, 0], shares, labels),
        )
        return part, sums, *rest[:2], rest[2:]

    shares = labels = lax.all_gather(payload, "sec")
    zvec, besides, beyond = finish(base, shares)
    part, gamma, zflat, rflat, across = local(zvec, rvec, shares, labels)
    wvec, delta, base, payload = call(
        functools.partial(image_kernel, pair),
        (field, shape(ncol, bdof), field, shape(ncol, lane)),
        [halved],
        (cmap, met, weights, part, zvec, high, low, rows, *besides, *beyond, *across),
    )
    shares = lax.all_gather(payload, "sec")
    mvec, besides, beyond = finish(base, shares)
    part, mu, mflat, wflat, across = local(mvec, wvec, shares, labels)
    nvec, totals = call(
        last_kernel,
        (field, shape(1, 6 * ncol)),
        [],
        (met, weights, part, rvec, zvec, mvec, gamma, delta, mu, *besides, *beyond, *across),
    )
    sol, res = call(
        finish_kernel,
        (flat, flat),
        [],
        (everywhere(totals[0]), nvec, rflat, zflat, wflat, mflat),
    )
    return sol[None, None], res[None, None]


def solution(mesh):
    placed = (
        P("dam", "sec", None, None),
        P("dam", "sec", None, None),
        P("dam", "sec", None, None, None),
        P("dam", "sec", None, None),
        P("dam", "sec", None, None),
        P("dam", "sec", None, None, None),
        P("dam", "sec", None, None),
        P("dam", "sec", None, None),
        P("dam", "sec", None),
        P("dam", "sec", None),
    )
    return jax.shard_map(
        shards,
        mesh=mesh,
        in_specs=placed,
        out_specs=(P("dam", "sec", None, None), P("dam", "sec", None, None)),
        check_vma=False,
    )
```

```python
import functools

import jax
import jax.numpy as jnp
from jax import lax
from jax.experimental import pallas as pl
from jax.experimental.pallas import tpu as pltpu
from jax.sharding import PartitionSpec as P

F32 = jnp.float32
BF16 = jnp.bfloat16
VMEM_LIMIT = 16 * 1024 * 1024
LANES = 128
PIECES = 4


def halves(x):
    high = x.astype(BF16)
    return high, (x - high.astype(F32)).astype(BF16)


def stack(x):
    return jnp.concatenate(halves(x), axis=0)


def dot_t(a, b):
    return lax.dot_general(a, b, (((1,), (1,)), ((), ())), preferred_element_type=F32)


def dot(a, b):
    return lax.dot_general(a, b, (((1,), (0,)), ((), ())), preferred_element_type=F32)


def three_pass(mul, left, high, low):
    rows = left.shape[0] // 2
    first = mul(left, high)
    return first[:rows] + first[rows:] + mul(left[:rows], low)


def fetch(pairs, sems):
    copies = [
        pltpu.make_async_copy(source, target, sems.at[i])
        for i, (source, target) in enumerate(pairs)
    ]
    for copy in copies:
        copy.start()
    return [copy.wait for copy in copies]


def pieces(source, target, count):
    step = source.shape[0] // count
    return [
        (source.at[i * step : (i + 1) * step], target.at[i * step : (i + 1) * step])
        for i in range(count)
    ]


def face_order(pair):
    near = 1 - lax.axis_index("dam") % 2
    across = 3 - lax.axis_index("sec") % 2
    return [1 - near, near] + ([across, 5 - across] if pair else [5 - across, across])


def listed(index):
    value = index[...]
    return [[value[i, j] for j in range(value.shape[1])] for i in range(value.shape[0])]


def pack(field, where, out, at=0):
    ncol, bdof = field.shape[1:]
    for p, b in enumerate(where):
        out[:ncol, at + p * bdof : at + (p + 1) * bdof] = field[b]


def add_pieces(field, where, piece):
    new = [field[b] + piece(p, b) for p, b in enumerate(where)]
    for b, value in zip(where, new):
        field[b] = value


def lane_piece(x, p, bdof):
    return x[:, p * bdof : (p + 1) * bdof]


def split_blocks(blocks, tiles_high, tiles_low):
    nblk, bdof = blocks.shape[:2]
    group = tiles_high.shape[1] // bdof
    for b in range(nblk):
        t, j = divmod(b, group)
        here = slice(j * bdof, (j + 1) * bdof)
        tiles_high[t, here, here], tiles_low[t, here, here] = halves(blocks[b])


def apply_blocks(field, tiles_high, tiles_low, left, base):
    nblk, ncol, bdof = field.shape
    group = tiles_high.shape[1] // bdof
    for b in range(nblk):
        t, j = divmod(b, group)
        here = slice(j * bdof, (j + 1) * bdof)
        left[t, :ncol, here], left[t, ncol:, here] = halves(field[b])
    for t in range(nblk // group):
        out = three_pass(dot, left[t], tiles_high[t], tiles_low[t])
        for j in range(group):
            base[t * group + j] = lane_piece(out, j, bdof)


def offer(pair, corners, across, field, rows, tiles, left, base, payload):
    bdof = field.shape[2]
    if not pair:
        pack(field, corners, payload)
        apply_blocks(field, *tiles, left, base)
        return
    wide = len(corners) * bdof
    at = payload.shape[1] - wide
    me = lax.axis_index("sec")
    own = stack(jnp.concatenate([field[b] for b in corners], axis=1))
    mine = pl.multiple_of(me * wide, wide)
    other = pl.multiple_of((1 - me) * wide, wide)
    correct = three_pass(dot_t, own, *halves(rows[:, pl.ds(mine, wide)]))
    payload[: field.shape[1], at:] = three_pass(dot, own, *halves(rows[:, pl.ds(other, wide)]))
    apply_blocks(field, *tiles, left, base)
    add_pieces(base, corners, lambda n, b: lane_piece(correct, n, bdof))
    pack(base, across, payload)


def end_kernel(pair, cmap, met, base, rows, shares, zout, *faces):
    nblk, ncol, bdof = base.shape
    (corners,) = listed(cmap)
    where = listed(met)
    wide = len(corners) * bdof
    zout[...] = base[...]
    if pair:
        at = len(where[0]) * bdof
        correct = shares[pl.ds(1 - lax.axis_index("sec"), 1), :ncol, at:][0]
    else:
        correct = 0.0
        for s in range(shares.shape[0]):
            high, low = halves(rows[:, s * wide : (s + 1) * wide])
            correct = correct + three_pass(dot_t, stack(shares[s]), high, low)
    add_pieces(zout, corners, lambda n, b: lane_piece(correct, n, bdof))
    for blocks, out in zip(where, faces):
        pack(zout, blocks, out)


def face_across(shares, labels, nface, shape, out):
    nblk, ncol, bdof = shape
    at = nface * bdof
    me = lax.axis_index("sec")
    names = labels[pl.ds(1 - me, 1), ncol : ncol + 2, : LANES][0]
    for p in range(nface):
        value = shares[pl.ds(1 - me, 1), :ncol, p * bdof : (p + 1) * bdof][0]
        for n in range((shares.shape[2] - at) // bdof):
            here = slice(at + n * bdof, at + (n + 1) * bdof)
            same = jnp.where(names[0, n] == names[1, p], 1.0, 0.0)
            value = value + same * shares[pl.ds(me, 1), :ncol, here][0]
        out[:, p * bdof : (p + 1) * bdof] = value


def swap_groups(x, ncol):
    subs, lanes_at = x.shape[1:]
    sub = lax.broadcasted_iota(jnp.int32, x.shape, 1)
    lane = lax.broadcasted_iota(jnp.int32, x.shape, 2)
    step = 1
    while step < subs:
        move = step * ncol
        low, left = (sub & step) == 0, (lane & move) == 0
        up = pltpu.roll(pltpu.roll(x, subs - step, 1), move, 2)
        down = pltpu.roll(pltpu.roll(x, step, 1), lanes_at - move, 2)
        x = jnp.where(low == left, x, jnp.where(low, up, down))
        step *= 2
    return x


def flatten(part, shape, out):
    nblk, ncol, bdof = shape
    subs = LANES // ncol
    for first in range(0, nblk, subs):
        tall = part(first, first + subs).reshape(LANES, bdof).T
        tall = swap_groups(tall.reshape(bdof // subs, subs, LANES), ncol)
        for j in range(bdof // subs):
            out[first : first + subs, j * LANES : (j + 1) * LANES] = tall[j]


def unflatten(part, shape, out):
    nblk, ncol, bdof = shape
    subs = LANES // ncol
    for first in range(0, nblk, subs):
        parts = [part(first, first + subs, j)[None] for j in range(bdof // subs)]
        tall = swap_groups(jnp.concatenate(parts, axis=0), ncol).reshape(bdof, LANES)
        out[first : first + subs] = tall.T.reshape(subs, ncol, bdof)


def start_kernel(pair, *refs):
    load_in, mask_in, cmap_in, fmap_in, blocks_in, rows_in, cols_in, weights_in, tang_in = refs[:9]
    rvec, base, payload, tiles_high, tiles_low, cmap_out, met, wmet, rows, cols, tang = refs[9:20]
    load, mask, blocks, cmap, cmap_row, fmap, fmap_rows, weights, left, sems = refs[20:]
    waits = fetch(
        [
            (load_in, load),
            (mask_in, mask),
            (cmap_in, cmap),
            (fmap_in, fmap),
            (cmap_in, cmap_row),
            (fmap_in, fmap_rows),
            (weights_in, weights),
            (cols_in, cols),
            (tang_in, tang),
        ]
        + pieces(blocks_in, blocks, PIECES)
        + pieces(rows_in, rows, PIECES),
        sems,
    )
    nblk, ncol, bdof = rvec.shape
    order = face_order(pair)
    tiles_high[...] = jnp.zeros_like(tiles_high)
    tiles_low[...] = jnp.zeros_like(tiles_low)
    waits[2]()
    waits[3]()
    corners = [cmap[0, 0, n] for n in range(cmap.shape[2])]
    across = [fmap[0, 0, order[2], p] for p in range(fmap.shape[3])]
    for wait in waits[:2]:
        wait()
    scale = mask[...].astype(F32)
    scale = jnp.concatenate([scale] * (LANES // ncol), axis=1)
    unflatten(
        lambda first, last, j: load[first:last, j * LANES : (j + 1) * LANES]
        * scale[first:last],
        rvec.shape,
        rvec,
    )
    for wait in waits[9 : 9 + PIECES]:
        wait()
    split_blocks(blocks, tiles_high, tiles_low)
    for wait in waits[9 + PIECES :] + waits[4:9]:
        wait()
    tiles = (tiles_high, tiles_low)
    offer(pair, corners, across, rvec, rows, tiles, left, base, payload)
    cmap_out[...] = cmap_row[0]
    if pair:
        payload[ncol:, :] = jnp.zeros_like(payload[ncol:, :])
        payload[ncol : ncol + 1, : len(corners)] = cmap_row[0].astype(F32)
        payload[ncol + 1 : ncol + 2, : len(across)] = fmap_rows[
            0, 0, pl.ds(order[2], 1), :
        ].astype(F32)
    for i, face in enumerate(order):
        met[i : i + 1, :] = fmap_rows[0, 0, pl.ds(face, 1), :]
        wmet[i : i + 1, :] = weights[pl.ds(face, 1), :]


def local_kernel(
    pair, cols_in, met, weights, capillary, field, other, stiff, shares, labels, *rest
):
    out, sums, flat, other_flat, *across, left, cols, sems = rest
    nblk, ncol, bdof = field.shape
    (wait,) = fetch([(cols_in, cols)], sems)
    where = listed(met)
    if pair:
        face_across(shares, labels, len(where[2]), field.shape, across[0])
    sums[...] = lanes(field, other)
    flatten(lambda first, last: field[first:last], field.shape, flat)
    flatten(lambda first, last: other[first:last], field.shape, other_flat)
    kept = stiff.shape[2] // bdof
    for b in range(nblk):
        left[b] = stack(field[b])
    wait()
    group = 4
    for t in range(0, nblk, group):
        gathered = [
            jnp.concatenate([left[cols[k, 0, t + j]] for k in range(kept)], axis=1)
            for j in range(group)
        ]
        firsts = [g[:ncol] for g in gathered]
        seconds = [g[ncol:] for g in gathered]
        rows = stiff[t : t + group].reshape(group * bdof, kept * bdof)
        prod = three_pass(dot_t, jnp.concatenate(firsts + seconds, axis=0), *halves(rows))
        for j in range(group):
            out[t + j] = (
                lane_piece(prod[j * ncol : (j + 1) * ncol], j, bdof)
                + capillary[t + j : t + j + 1, :] * field[t + j]
            )
    for i, blocks in enumerate(where):
        row = weights[i : i + 1, :]
        add_pieces(out, blocks, lambda p, b: lane_piece(row, p, bdof) * field[b])


def couple(met, weights, local, besides, out):
    bdof = local.shape[2]
    where = listed(met)
    out[...] = local[...]
    for i, beside in enumerate(besides):
        term = weights[i : i + 1, :] * beside[...]
        add_pieces(out, where[i], lambda p, b: -lane_piece(term, p, bdof))
    return where


def lanes(first, second):
    return jnp.sum(first[...] * second[...], axis=0)


def image_kernel(
    pair, cmap, met, weights, local, zvec, tiles_high, tiles_low, rows, *rest
):
    count = 3 if pair else 4
    besides, (wout, sums, base, payload, left) = rest[:count], rest[count:]
    (corners,) = listed(cmap)
    where = couple(met, weights, local, besides, wout)
    tiles = (tiles_high, tiles_low)
    offer(pair, corners, where[2], wout, rows, tiles, left, base, payload)
    sums[...] = lanes(zvec, wout)


def last_kernel(met, weights, local, rvec, zvec, mvec, gamma, delta, mu, *rest):
    *besides, nout, totals = rest
    rm = lanes(rvec, mvec)
    couple(met, weights, local, besides, nout)
    parts = [gamma[...], delta[...], mu[...], rm, lanes(mvec, nout), lanes(zvec, nout)]
    parts = jnp.concatenate(parts, axis=0)
    totals[...] = lax.dot_general(
        jnp.ones((1, parts.shape[1]), F32),
        parts,
        (((1,), (1,)), ((), ())),
        precision=lax.Precision.HIGHEST,
        preferred_element_type=F32,
    )


def finish_kernel(shares, nvec, rflat, zflat, wflat, mflat, sol, res):
    nblk, ncol, bdof = nvec.shape
    flatten(lambda first, last: nvec[first:last], nvec.shape, res)
    total = jnp.sum(shares[...], axis=0, keepdims=True)
    gamma, delta, mu, rm, nu, zn = [total[:, q * ncol : (q + 1) * ncol] for q in range(6)]
    alpha = gamma / delta
    gnew = gamma - alpha * (delta + rm) + alpha * alpha * mu
    grow = 1.0 + gnew / gamma
    dnew = grow * grow * delta - alpha * grow * (mu + zn) + alpha * alpha * nu
    anew = gnew / dnew
    both, second = [
        jnp.concatenate([x] * (LANES // ncol), axis=1)
        for x in (alpha + anew * grow, anew * alpha)
    ]
    for j in range(sol.shape[1] // LANES):
        here = slice(j * LANES, (j + 1) * LANES)
        sol[:, here] = both * zflat[:, here] - second * mflat[:, here]
        res[:, here] = rflat[:, here] - both * wflat[:, here] + second * res[:, here]


def call(kernel, outs, scratch, args, far=()):
    vmem = pl.BlockSpec(memory_space=pltpu.VMEM)
    hbm = pl.BlockSpec(memory_space=pltpu.HBM)
    far = [pltpu.with_memory_space_constraint(arg, pltpu.HBM) for arg in far]
    return pl.pallas_call(
        kernel,
        out_shape=outs,
        in_specs=[vmem] * len(args) + [hbm] * len(far),
        out_specs=jax.tree.map(lambda _: vmem, outs),
        scratch_shapes=scratch,
        compiler_params=pltpu.CompilerParams(vmem_limit_bytes=VMEM_LIMIT),
    )(*args, *far)


def everywhere(values):
    total = lax.axis_size("dam") * lax.axis_size("sec")
    copies = jnp.broadcast_to(values[None], (total,) + values.shape)
    return lax.all_to_all(copies, ("dam", "sec"), split_axis=0, concat_axis=0)


def exchange(sends, axis):
    size = lax.axis_size(axis)
    got = []
    for first, send in zip((1, 0), sends):
        pairs = [(i, i + 1) for i in range(first, size - 1, 2)]
        got.append(lax.ppermute(send, axis, pairs + [(j, i) for i, j in pairs]))
    return got


def shards(
    segment_load,
    segment_mask,
    stiffness,
    block_cols,
    capillary,
    dirichlet_blocks,
    face_map,
    face_weight,
    corner_map,
    coarse_inverse,
):
    nblk, bdof = capillary.shape[2:]
    ncol = segment_load.shape[-1] // bdof
    nface = face_map.shape[3]
    ncorner = corner_map.shape[2]
    size = nblk * bdof
    pair = lax.axis_size("sec") == 2
    load, mask = segment_load[0, 0], segment_mask[0, 0]
    cols = jnp.transpose(block_cols[0], (2, 0, 1))
    tang, weights = capillary[0, 0], face_weight[0, 0]
    blocks, rows = dirichlet_blocks[0, 0], coarse_inverse[0]

    def shape(*dims, dtype=F32):
        return jax.ShapeDtypeStruct(dims, dtype)

    def like(array):
        return shape(*array.shape, dtype=array.dtype)

    def hold(array):
        return pltpu.VMEM(array.shape, array.dtype)

    def index(array):
        return pltpu.SMEM(array.shape, array.dtype)

    def sems(count):
        return pltpu.SemaphoreType.DMA((count,))

    field = shape(nblk, ncol, bdof)
    flat = shape(nblk, bdof * ncol)
    face = shape(ncol, nface * bdof)
    group = ncorner * bdof
    tiles = shape(size // group, group, group, dtype=BF16)
    halved = pltpu.VMEM((size // group, 2 * ncol, group), BF16)
    lane = group + nface * bdof if pair else group
    marked = ncol + 8 if pair else ncol

    rvec, base, payload, high, low, cmap, met, weights, rows, cols, tang = call(
        functools.partial(start_kernel, pair),
        (field, field, shape(marked, lane), tiles, tiles)
        + (shape(1, ncorner, dtype=jnp.int32), shape(4, nface, dtype=jnp.int32))
        + tuple(like(a) for a in (weights, rows, cols, tang)),
        [
            hold(load),
            hold(mask),
            hold(blocks),
            index(corner_map),
            hold(corner_map),
            index(face_map),
            hold(face_map),
            hold(weights),
            halved,
            sems(9 + 2 * PIECES),
        ],
        (),
        (load, mask, corner_map, face_map, blocks, rows, cols, weights, tang),
    )

    def finish(base, shares):
        vec, *faces = call(
            functools.partial(end_kernel, pair),
            (field,) + (face,) * (2 if pair else 4),
            [],
            (cmap, met, base, rows, shares),
        )
        return vec, exchange(faces[:2], "dam"), exchange(faces[2:], "sec")

    def local(vec, other, shares, labels):
        part, sums, *rest = call(
            functools.partial(local_kernel, pair),
            (field, shape(ncol, bdof), flat, flat) + ((face,) if pair else ()),
            [pltpu.VMEM((nblk, 2 * ncol, bdof), BF16), index(cols), sems(1)],
            (cols, met, weights, tang, vec, other, stiffness[0, 0], shares, labels),
        )
        return part, sums, *rest[:2], rest[2:]

    shares = labels = lax.all_gather(payload, "sec")
    zvec, besides, beyond = finish(base, shares)
    part, gamma, zflat, rflat, across = local(zvec, rvec, shares, labels)
    wvec, delta, base, payload = call(
        functools.partial(image_kernel, pair),
        (field, shape(ncol, bdof), field, shape(ncol, lane)),
        [halved],
        (cmap, met, weights, part, zvec, high, low, rows, *besides, *beyond, *across),
    )
    shares = lax.all_gather(payload, "sec")
    mvec, besides, beyond = finish(base, shares)
    part, mu, mflat, wflat, across = local(mvec, wvec, shares, labels)
    nvec, totals = call(
        last_kernel,
        (field, shape(1, 6 * ncol)),
        [],
        (met, weights, part, rvec, zvec, mvec, gamma, delta, mu, *besides, *beyond, *across),
    )
    sol, res = call(
        finish_kernel,
        (flat, flat),
        [],
        (everywhere(totals[0]), nvec, rflat, zflat, wflat, mflat),
    )
    return sol[None, None], res[None, None]


def solution(mesh):
    placed = (
        P("dam", "sec", None, None),
        P("dam", "sec", None, None),
        P("dam", "sec", None, None, None),
        P("dam", "sec", None, None),
        P("dam", "sec", None, None),
        P("dam", "sec", None, None, None),
        P("dam", "sec", None, None),
        P("dam", "sec", None, None),
        P("dam", "sec", None),
        P("dam", "sec", None),
    )
    return jax.shard_map(
        shards,
        mesh=mesh,
        in_specs=placed,
        out_specs=(P("dam", "sec", None, None), P("dam", "sec", None, None)),
        check_vma=False,
    )
```

```python
import functools

import jax
import jax.numpy as jnp
from jax import lax
from jax.experimental import pallas as pl
from jax.experimental.pallas import tpu as pltpu
from jax.sharding import PartitionSpec as P

F32 = jnp.float32
BF16 = jnp.bfloat16
VMEM_LIMIT = 16 * 1024 * 1024
LANES = 128
PIECES = 4


def halves(x):
    high = x.astype(BF16)
    return high, (x - high.astype(F32)).astype(BF16)


def stack(x):
    return jnp.concatenate(halves(x), axis=0)


def dot_t(a, b):
    return lax.dot_general(a, b, (((1,), (1,)), ((), ())), preferred_element_type=F32)


def dot(a, b):
    return lax.dot_general(a, b, (((1,), (0,)), ((), ())), preferred_element_type=F32)


def three_pass(mul, left, high, low):
    rows = left.shape[0] // 2
    first = mul(left, high)
    return first[:rows] + first[rows:] + mul(left[:rows], low)


def fetch(pairs, sems):
    copies = [
        pltpu.make_async_copy(source, target, sems.at[i])
        for i, (source, target) in enumerate(pairs)
    ]
    for copy in copies:
        copy.start()
    return [copy.wait for copy in copies]


def pieces(source, target, count):
    step = source.shape[0] // count
    return [
        (source.at[i * step : (i + 1) * step], target.at[i * step : (i + 1) * step])
        for i in range(count)
    ]


def face_order(pair):
    near = 1 - lax.axis_index("dam") % 2
    across = 3 - lax.axis_index("sec") % 2
    return [1 - near, near] + ([across, 5 - across] if pair else [5 - across, across])


def listed(index):
    value = index[...]
    return [[value[i, j] for j in range(value.shape[1])] for i in range(value.shape[0])]


def pack(field, where, out, at=0):
    ncol, bdof = field.shape[1:]
    for p, b in enumerate(where):
        out[:ncol, at + p * bdof : at + (p + 1) * bdof] = field[b]


def add_pieces(field, where, piece):
    new = [field[b] + piece(p, b) for p, b in enumerate(where)]
    for b, value in zip(where, new):
        field[b] = value


def lane_piece(x, p, bdof):
    return x[:, p * bdof : (p + 1) * bdof]


def split_blocks(blocks, tiles_high, tiles_low):
    nblk, bdof = blocks.shape[:2]
    group = tiles_high.shape[1] // bdof
    for b in range(nblk):
        t, j = divmod(b, group)
        here = slice(j * bdof, (j + 1) * bdof)
        tiles_high[t, here, here], tiles_low[t, here, here] = halves(blocks[b])


def apply_blocks(field, tiles_high, tiles_low, left, base):
    nblk, ncol, bdof = field.shape
    group = tiles_high.shape[1] // bdof
    for b in range(nblk):
        t, j = divmod(b, group)
        here = slice(j * bdof, (j + 1) * bdof)
        left[t, :ncol, here], left[t, ncol:, here] = halves(field[b])
    for t in range(nblk // group):
        out = three_pass(dot, left[t], tiles_high[t], tiles_low[t])
        for j in range(group):
            base[t * group + j] = lane_piece(out, j, bdof)


def offer(pair, corners, across, field, rows, tiles, left, base, payload):
    bdof = field.shape[2]
    if not pair:
        pack(field, corners, payload)
        apply_blocks(field, *tiles, left, base)
        return
    wide = len(corners) * bdof
    at = payload.shape[1] - wide
    me = lax.axis_index("sec")
    own = stack(jnp.concatenate([field[b] for b in corners], axis=1))
    mine = pl.multiple_of(me * wide, wide)
    other = pl.multiple_of((1 - me) * wide, wide)
    correct = three_pass(dot_t, own, *halves(rows[:, pl.ds(mine, wide)]))
    payload[: field.shape[1], at:] = three_pass(dot, own, *halves(rows[:, pl.ds(other, wide)]))
    apply_blocks(field, *tiles, left, base)
    add_pieces(base, corners, lambda n, b: lane_piece(correct, n, bdof))
    pack(base, across, payload)


def end_kernel(pair, cmap, met, base, rows, shares, zout, *faces):
    nblk, ncol, bdof = base.shape
    (corners,) = listed(cmap)
    where = listed(met)
    wide = len(corners) * bdof
    zout[...] = base[...]
    if pair:
        at = len(where[0]) * bdof
        correct = shares[pl.ds(1 - lax.axis_index("sec"), 1), :ncol, at:][0]
    else:
        correct = 0.0
        for s in range(shares.shape[0]):
            high, low = halves(rows[:, s * wide : (s + 1) * wide])
            correct = correct + three_pass(dot_t, stack(shares[s]), high, low)
    add_pieces(zout, corners, lambda n, b: lane_piece(correct, n, bdof))
    for blocks, out in zip(where, faces):
        pack(zout, blocks, out)


def face_across(shares, labels, nface, shape, out):
    nblk, ncol, bdof = shape
    at = nface * bdof
    me = lax.axis_index("sec")
    names = labels[pl.ds(1 - me, 1), ncol : ncol + 2, : LANES][0]
    for p in range(nface):
        value = shares[pl.ds(1 - me, 1), :ncol, p * bdof : (p + 1) * bdof][0]
        for n in range((shares.shape[2] - at) // bdof):
            here = slice(at + n * bdof, at + (n + 1) * bdof)
            same = jnp.where(names[0, n] == names[1, p], 1.0, 0.0)
            value = value + same * shares[pl.ds(me, 1), :ncol, here][0]
        out[:, p * bdof : (p + 1) * bdof] = value


def swap_groups(x, ncol):
    subs, lanes_at = x.shape[1:]
    sub = lax.broadcasted_iota(jnp.int32, x.shape, 1)
    lane = lax.broadcasted_iota(jnp.int32, x.shape, 2)
    step = 1
    while step < subs:
        move = step * ncol
        low, left = (sub & step) == 0, (lane & move) == 0
        up = pltpu.roll(pltpu.roll(x, subs - step, 1), move, 2)
        down = pltpu.roll(pltpu.roll(x, step, 1), lanes_at - move, 2)
        x = jnp.where(low == left, x, jnp.where(low, up, down))
        step *= 2
    return x


def flatten(part, shape, out):
    nblk, ncol, bdof = shape
    subs = LANES // ncol
    for first in range(0, nblk, subs):
        tall = part(first, first + subs).reshape(LANES, bdof).T
        tall = swap_groups(tall.reshape(bdof // subs, subs, LANES), ncol)
        for j in range(bdof // subs):
            out[first : first + subs, j * LANES : (j + 1) * LANES] = tall[j]


def unflatten(part, shape, out):
    nblk, ncol, bdof = shape
    subs = LANES // ncol
    for first in range(0, nblk, subs):
        parts = [part(first, first + subs, j)[None] for j in range(bdof // subs)]
        tall = swap_groups(jnp.concatenate(parts, axis=0), ncol).reshape(bdof, LANES)
        out[first : first + subs] = tall.T.reshape(subs, ncol, bdof)


def start_kernel(pair, *refs):
    load_in, mask_in, cmap_in, fmap_in, blocks_in, rows_in, cols_in, weights_in, tang_in = refs[:9]
    rvec, base, payload, tiles_high, tiles_low, cmap_out, met, wmet, rows, cols, tang = refs[9:20]
    load, mask, blocks, cmap, cmap_row, fmap, fmap_rows, weights, left, sems = refs[20:]
    waits = fetch(
        [
            (mask_in, mask),
            *pieces(load_in, load, load.shape[0] // (LANES // rvec.shape[1])),
            *pieces(blocks_in, blocks, PIECES),
            (cmap_in, cmap),
            (fmap_in, fmap),
            *pieces(rows_in, rows, PIECES),
            (cmap_in, cmap_row),
            (fmap_in, fmap_rows),
            (weights_in, weights),
            (cols_in, cols),
            (tang_in, tang),
        ],
        sems,
    )
    loads = waits[: load.shape[0] // (LANES // rvec.shape[1]) + 1]
    waits = waits[len(loads) :]
    nblk, ncol, bdof = rvec.shape
    order = face_order(pair)
    tiles_high[...] = jnp.zeros_like(tiles_high)
    tiles_low[...] = jnp.zeros_like(tiles_low)
    for wait in loads:
        wait()
    scale = mask[...].astype(F32)
    scale = jnp.concatenate([scale] * (LANES // ncol), axis=1)
    unflatten(
        lambda first, last, j: load[first:last, j * LANES : (j + 1) * LANES]
        * scale[first:last],
        rvec.shape,
        rvec,
    )
    for wait in waits[:PIECES]:
        wait()
    split_blocks(blocks, tiles_high, tiles_low)
    for wait in waits[PIECES:]:
        wait()
    corners = [cmap[0, 0, n] for n in range(cmap.shape[2])]
    across = [fmap[0, 0, order[2], p] for p in range(fmap.shape[3])]
    tiles = (tiles_high, tiles_low)
    offer(pair, corners, across, rvec, rows, tiles, left, base, payload)
    cmap_out[...] = cmap_row[0]
    if pair:
        payload[ncol:, :] = jnp.zeros_like(payload[ncol:, :])
        payload[ncol : ncol + 1, : len(corners)] = cmap_row[0].astype(F32)
        payload[ncol + 1 : ncol + 2, : len(across)] = fmap_rows[
            0, 0, pl.ds(order[2], 1), :
        ].astype(F32)
    for i, face in enumerate(order):
        met[i : i + 1, :] = fmap_rows[0, 0, pl.ds(face, 1), :]
        wmet[i : i + 1, :] = weights[pl.ds(face, 1), :]


def local_kernel(
    pair, cols_in, met, weights, capillary, field, other, stiff, shares, labels, *rest
):
    out, sums, flat, other_flat, *across, left, cols, sems = rest
    nblk, ncol, bdof = field.shape
    (wait,) = fetch([(cols_in, cols)], sems)
    where = listed(met)
    if pair:
        face_across(shares, labels, len(where[2]), field.shape, across[0])
    sums[...] = lanes(field, other)
    flatten(lambda first, last: field[first:last], field.shape, flat)
    flatten(lambda first, last: other[first:last], field.shape, other_flat)
    kept = stiff.shape[2] // bdof
    for b in range(nblk):
        left[b] = stack(field[b])
    wait()
    group = 4
    for t in range(0, nblk, group):
        gathered = [
            jnp.concatenate([left[cols[k, 0, t + j]] for k in range(kept)], axis=1)
            for j in range(group)
        ]
        firsts = [g[:ncol] for g in gathered]
        seconds = [g[ncol:] for g in gathered]
        rows = stiff[t : t + group].reshape(group * bdof, kept * bdof)
        prod = three_pass(dot_t, jnp.concatenate(firsts + seconds, axis=0), *halves(rows))
        for j in range(group):
            out[t + j] = (
                lane_piece(prod[j * ncol : (j + 1) * ncol], j, bdof)
                + capillary[t + j : t + j + 1, :] * field[t + j]
            )
    for i, blocks in enumerate(where):
        row = weights[i : i + 1, :]
        add_pieces(out, blocks, lambda p, b: lane_piece(row, p, bdof) * field[b])


def couple(met, weights, local, besides, out):
    bdof = local.shape[2]
    where = listed(met)
    out[...] = local[...]
    for i, beside in enumerate(besides):
        term = weights[i : i + 1, :] * beside[...]
        add_pieces(out, where[i], lambda p, b: -lane_piece(term, p, bdof))
    return where


def lanes(first, second):
    return jnp.sum(first[...] * second[...], axis=0)


def image_kernel(
    pair, cmap, met, weights, local, zvec, tiles_high, tiles_low, rows, *rest
):
    count = 3 if pair else 4
    besides, (wout, sums, base, payload, left) = rest[:count], rest[count:]
    (corners,) = listed(cmap)
    where = couple(met, weights, local, besides, wout)
    tiles = (tiles_high, tiles_low)
    offer(pair, corners, where[2], wout, rows, tiles, left, base, payload)
    sums[...] = lanes(zvec, wout)


def last_kernel(met, weights, local, rvec, zvec, mvec, gamma, delta, mu, *rest):
    *besides, nout, totals = rest
    rm = lanes(rvec, mvec)
    couple(met, weights, local, besides, nout)
    parts = [gamma[...], delta[...], mu[...], rm, lanes(mvec, nout), lanes(zvec, nout)]
    parts = jnp.concatenate(parts, axis=0)
    sides = lax.dot_general(
        jnp.ones((1, parts.shape[1]), F32),
        parts,
        (((1,), (1,)), ((), ())),
        precision=lax.Precision.HIGHEST,
        preferred_element_type=F32,
    )
    totals[...] = jnp.broadcast_to(sides[None], totals.shape)


def finish_kernel(shares, nvec, rflat, zflat, wflat, mflat, sol, res):
    nblk, ncol, bdof = nvec.shape
    flatten(lambda first, last: nvec[first:last], nvec.shape, res)
    total = jnp.sum(shares[...], axis=0, keepdims=True)
    gamma, delta, mu, rm, nu, zn = [total[:, q * ncol : (q + 1) * ncol] for q in range(6)]
    alpha = gamma / delta
    gnew = gamma - alpha * (delta + rm) + alpha * alpha * mu
    grow = 1.0 + gnew / gamma
    dnew = grow * grow * delta - alpha * grow * (mu + zn) + alpha * alpha * nu
    anew = gnew / dnew
    both, second = [
        jnp.concatenate([x] * (LANES // ncol), axis=1)
        for x in (alpha + anew * grow, anew * alpha)
    ]
    for j in range(sol.shape[1] // LANES):
        here = slice(j * LANES, (j + 1) * LANES)
        sol[:, here] = both * zflat[:, here] - second * mflat[:, here]
        res[:, here] = rflat[:, here] - both * wflat[:, here] + second * res[:, here]


def call(kernel, outs, scratch, args, far=()):
    vmem = pl.BlockSpec(memory_space=pltpu.VMEM)
    hbm = pl.BlockSpec(memory_space=pltpu.HBM)
    far = [pltpu.with_memory_space_constraint(arg, pltpu.HBM) for arg in far]
    return pl.pallas_call(
        kernel,
        out_shape=outs,
        in_specs=[vmem] * len(args) + [hbm] * len(far),
        out_specs=jax.tree.map(lambda _: vmem, outs),
        scratch_shapes=scratch,
        compiler_params=pltpu.CompilerParams(vmem_limit_bytes=VMEM_LIMIT),
    )(*args, *far)


def everywhere(copies):
    return lax.all_to_all(copies, ("dam", "sec"), split_axis=0, concat_axis=0)


def exchange(sends, axis):
    size = lax.axis_size(axis)
    got = []
    for first, send in zip((1, 0), sends):
        pairs = [(i, i + 1) for i in range(first, size - 1, 2)]
        got.append(lax.ppermute(send, axis, pairs + [(j, i) for i, j in pairs]))
    return got


def shards(
    segment_load,
    segment_mask,
    stiffness,
    block_cols,
    capillary,
    dirichlet_blocks,
    face_map,
    face_weight,
    corner_map,
    coarse_inverse,
):
    nblk, bdof = capillary.shape[2:]
    ncol = segment_load.shape[-1] // bdof
    nface = face_map.shape[3]
    ncorner = corner_map.shape[2]
    size = nblk * bdof
    pair = lax.axis_size("sec") == 2
    load, mask = segment_load[0, 0], segment_mask[0, 0]
    cols = jnp.transpose(block_cols[0], (2, 0, 1))
    tang, weights = capillary[0, 0], face_weight[0, 0]
    blocks, rows = dirichlet_blocks[0, 0], coarse_inverse[0]

    def shape(*dims, dtype=F32):
        return jax.ShapeDtypeStruct(dims, dtype)

    def like(array):
        return shape(*array.shape, dtype=array.dtype)

    def hold(array):
        return pltpu.VMEM(array.shape, array.dtype)

    def index(array):
        return pltpu.SMEM(array.shape, array.dtype)

    def sems(count):
        return pltpu.SemaphoreType.DMA((count,))

    field = shape(nblk, ncol, bdof)
    flat = shape(nblk, bdof * ncol)
    face = shape(ncol, nface * bdof)
    group = ncorner * bdof
    tiles = shape(size // group, group, group, dtype=BF16)
    halved = pltpu.VMEM((size // group, 2 * ncol, group), BF16)
    lane = group + nface * bdof if pair else group
    marked = ncol + 8 if pair else ncol

    rvec, base, payload, high, low, cmap, met, weights, rows, cols, tang = call(
        functools.partial(start_kernel, pair),
        (field, field, shape(marked, lane), tiles, tiles)
        + (shape(1, ncorner, dtype=jnp.int32), shape(4, nface, dtype=jnp.int32))
        + tuple(like(a) for a in (weights, rows, cols, tang)),
        [
            hold(load),
            hold(mask),
            hold(blocks),
            index(corner_map),
            hold(corner_map),
            index(face_map),
            hold(face_map),
            hold(weights),
            halved,
            sems(8 + nblk * ncol // LANES + 2 * PIECES),
        ],
        (),
        (load, mask, corner_map, face_map, blocks, rows, cols, weights, tang),
    )

    def finish(base, shares):
        vec, *faces = call(
            functools.partial(end_kernel, pair),
            (field,) + (face,) * (2 if pair else 4),
            [],
            (cmap, met, base, rows, shares),
        )
        return vec, exchange(faces[:2], "dam"), exchange(faces[2:], "sec")

    def local(vec, other, shares, labels):
        part, sums, *rest = call(
            functools.partial(local_kernel, pair),
            (field, shape(ncol, bdof), flat, flat) + ((face,) if pair else ()),
            [pltpu.VMEM((nblk, 2 * ncol, bdof), BF16), index(cols), sems(1)],
            (cols, met, weights, tang, vec, other, stiffness[0, 0], shares, labels),
        )
        return part, sums, *rest[:2], rest[2:]

    shares = labels = lax.all_gather(payload, "sec")
    zvec, besides, beyond = finish(base, shares)
    part, gamma, zflat, rflat, across = local(zvec, rvec, shares, labels)
    wvec, delta, base, payload = call(
        functools.partial(image_kernel, pair),
        (field, shape(ncol, bdof), field, shape(ncol, lane)),
        [halved],
        (cmap, met, weights, part, zvec, high, low, rows, *besides, *beyond, *across),
    )
    shares = lax.all_gather(payload, "sec")
    mvec, besides, beyond = finish(base, shares)
    part, mu, mflat, wflat, across = local(mvec, wvec, shares, labels)
    nvec, totals = call(
        last_kernel,
        (field, shape(lax.axis_size("dam") * lax.axis_size("sec"), 1, 6 * ncol)),
        [],
        (met, weights, part, rvec, zvec, mvec, gamma, delta, mu, *besides, *beyond, *across),
    )
    sol, res = call(
        finish_kernel,
        (flat, flat),
        [],
        (everywhere(totals)[:, 0], nvec, rflat, zflat, wflat, mflat),
    )
    return sol[None, None], res[None, None]


def solution(mesh):
    placed = (
        P("dam", "sec", None, None),
        P("dam", "sec", None, None),
        P("dam", "sec", None, None, None),
        P("dam", "sec", None, None),
        P("dam", "sec", None, None),
        P("dam", "sec", None, None, None),
        P("dam", "sec", None, None),
        P("dam", "sec", None, None),
        P("dam", "sec", None),
        P("dam", "sec", None),
    )
    return jax.shard_map(
        shards,
        mesh=mesh,
        in_specs=placed,
        out_specs=(P("dam", "sec", None, None), P("dam", "sec", None, None)),
        check_vma=False,
    )
```

```python
import functools

import jax
import jax.numpy as jnp
from jax import lax
from jax.experimental import pallas as pl
from jax.experimental.pallas import tpu as pltpu
from jax.sharding import PartitionSpec as P

F32 = jnp.float32
BF16 = jnp.bfloat16
VMEM_LIMIT = 16 * 1024 * 1024
LANES = 128
PIECES = 4


def halves(x):
    high = x.astype(BF16)
    return high, (x - high.astype(F32)).astype(BF16)


def stack(x):
    return jnp.concatenate(halves(x), axis=0)


def dot_t(a, b):
    return lax.dot_general(a, b, (((1,), (1,)), ((), ())), preferred_element_type=F32)


def dot(a, b):
    return lax.dot_general(a, b, (((1,), (0,)), ((), ())), preferred_element_type=F32)


def three_pass(mul, left, high, low):
    rows = left.shape[0] // 2
    first = mul(left, high)
    return first[:rows] + first[rows:] + mul(left[:rows], low)


def fetch(pairs, sems):
    copies = [
        pltpu.make_async_copy(source, target, sems.at[i])
        for i, (source, target) in enumerate(pairs)
    ]
    for copy in copies:
        copy.start()
    return [copy.wait for copy in copies]


def pieces(source, target, count):
    step = source.shape[0] // count
    return [
        (source.at[i * step : (i + 1) * step], target.at[i * step : (i + 1) * step])
        for i in range(count)
    ]


def face_order(pair):
    near = 1 - lax.axis_index("dam") % 2
    across = 3 - lax.axis_index("sec") % 2
    return [1 - near, near] + ([across, 5 - across] if pair else [5 - across, across])


def listed(index):
    value = index[...]
    return [[value[i, j] for j in range(value.shape[1])] for i in range(value.shape[0])]


def pack(field, where, out, at=0):
    ncol, bdof = field.shape[1:]
    for p, b in enumerate(where):
        out[:ncol, at + p * bdof : at + (p + 1) * bdof] = field[b]


def add_pieces(field, where, piece):
    new = [field[b] + piece(p, b) for p, b in enumerate(where)]
    for b, value in zip(where, new):
        field[b] = value


def lane_piece(x, p, bdof):
    return x[:, p * bdof : (p + 1) * bdof]


def split_blocks(blocks, tiles_high, tiles_low):
    nblk, bdof = blocks.shape[:2]
    group = tiles_high.shape[1] // bdof
    for b in range(nblk):
        t, j = divmod(b, group)
        here = slice(j * bdof, (j + 1) * bdof)
        tiles_high[t, here, here], tiles_low[t, here, here] = halves(blocks[b])


def apply_blocks(field, tiles_high, tiles_low, left, base):
    nblk, ncol, bdof = field.shape
    group = tiles_high.shape[1] // bdof
    for b in range(nblk):
        t, j = divmod(b, group)
        here = slice(j * bdof, (j + 1) * bdof)
        left[t, :ncol, here], left[t, ncol:, here] = halves(field[b])
    for t in range(nblk // group):
        out = three_pass(dot, left[t], tiles_high[t], tiles_low[t])
        for j in range(group):
            base[t * group + j] = lane_piece(out, j, bdof)


def offer(pair, corners, across, field, rows, tiles, left, base, payload):
    bdof = field.shape[2]
    if not pair:
        pack(field, corners, payload)
        apply_blocks(field, *tiles, left, base)
        return
    wide = len(corners) * bdof
    at = payload.shape[1] - wide
    me = lax.axis_index("sec")
    own = stack(jnp.concatenate([field[b] for b in corners], axis=1))
    mine = pl.multiple_of(me * wide, wide)
    other = pl.multiple_of((1 - me) * wide, wide)
    correct = three_pass(dot_t, own, *halves(rows[:, pl.ds(mine, wide)]))
    payload[: field.shape[1], at:] = three_pass(dot, own, *halves(rows[:, pl.ds(other, wide)]))
    apply_blocks(field, *tiles, left, base)
    add_pieces(base, corners, lambda n, b: lane_piece(correct, n, bdof))
    pack(base, across, payload)


def end_kernel(pair, cmap, met, base, rows, shares, zout, *faces):
    nblk, ncol, bdof = base.shape
    (corners,) = listed(cmap)
    where = listed(met)
    wide = len(corners) * bdof
    zout[...] = base[...]
    if pair:
        at = len(where[0]) * bdof
        correct = shares[pl.ds(1 - lax.axis_index("sec"), 1), :ncol, at:][0]
    else:
        correct = 0.0
        for s in range(shares.shape[0]):
            high, low = halves(rows[:, s * wide : (s + 1) * wide])
            correct = correct + three_pass(dot_t, stack(shares[s]), high, low)
    add_pieces(zout, corners, lambda n, b: lane_piece(correct, n, bdof))
    for blocks, out in zip(where, faces):
        pack(zout, blocks, out)


def face_across(shares, labels, nface, shape, out):
    nblk, ncol, bdof = shape
    at = nface * bdof
    me = lax.axis_index("sec")
    names = labels[pl.ds(1 - me, 1), ncol : ncol + 2, : LANES][0]
    for p in range(nface):
        value = shares[pl.ds(1 - me, 1), :ncol, p * bdof : (p + 1) * bdof][0]
        for n in range((shares.shape[2] - at) // bdof):
            here = slice(at + n * bdof, at + (n + 1) * bdof)
            same = jnp.where(names[0, n] == names[1, p], 1.0, 0.0)
            value = value + same * shares[pl.ds(me, 1), :ncol, here][0]
        out[:, p * bdof : (p + 1) * bdof] = value


def swap_groups(x, ncol):
    subs, lanes_at = x.shape[1:]
    sub = lax.broadcasted_iota(jnp.int32, x.shape, 1)
    lane = lax.broadcasted_iota(jnp.int32, x.shape, 2)
    step = 1
    while step < subs:
        move = step * ncol
        low, left = (sub & step) == 0, (lane & move) == 0
        up = pltpu.roll(pltpu.roll(x, subs - step, 1), move, 2)
        down = pltpu.roll(pltpu.roll(x, step, 1), lanes_at - move, 2)
        x = jnp.where(low == left, x, jnp.where(low, up, down))
        step *= 2
    return x


def flatten(part, shape, out):
    nblk, ncol, bdof = shape
    subs = LANES // ncol
    for first in range(0, nblk, subs):
        tall = part(first, first + subs).reshape(LANES, bdof).T
        tall = swap_groups(tall.reshape(bdof // subs, subs, LANES), ncol)
        for j in range(bdof // subs):
            out[first : first + subs, j * LANES : (j + 1) * LANES] = tall[j]


def unflatten(part, shape, out):
    nblk, ncol, bdof = shape
    subs = LANES // ncol
    for first in range(0, nblk, subs):
        parts = [part(first, first + subs, j)[None] for j in range(bdof // subs)]
        tall = swap_groups(jnp.concatenate(parts, axis=0), ncol).reshape(bdof, LANES)
        out[first : first + subs] = tall.T.reshape(subs, ncol, bdof)


def start_kernel(pair, *refs):
    load_in, mask_in, cmap_in, fmap_in, blocks_in, rows_in, cols_in, weights_in, tang_in = refs[:9]
    rvec, base, payload, tiles_high, tiles_low, cmap_out, met, wmet, rows, cols, tang = refs[9:20]
    load, mask, blocks, cmap, cmap_row, fmap, fmap_rows, weights, left, sems = refs[20:]
    waits = fetch(
        [
            (mask_in, mask),
            *pieces(load_in, load, load.shape[0] // (LANES // rvec.shape[1])),
            *pieces(blocks_in, blocks, PIECES),
            (cmap_in, cmap),
            (fmap_in, fmap),
            *pieces(rows_in, rows, PIECES),
            (cmap_in, cmap_row),
            (fmap_in, fmap_rows),
            (weights_in, weights),
            (cols_in, cols),
            (tang_in, tang),
        ],
        sems,
    )
    loads = waits[: load.shape[0] // (LANES // rvec.shape[1]) + 1]
    waits = waits[len(loads) :]
    nblk, ncol, bdof = rvec.shape
    order = face_order(pair)
    tiles_high[...] = jnp.zeros_like(tiles_high)
    tiles_low[...] = jnp.zeros_like(tiles_low)
    for wait in loads + waits[:PIECES]:
        wait()
    split_blocks(blocks, tiles_high, tiles_low)
    scale = mask[...].astype(F32)
    scale = jnp.concatenate([scale] * (LANES // ncol), axis=1)
    unflatten(
        lambda first, last, j: load[first:last, j * LANES : (j + 1) * LANES]
        * scale[first:last],
        rvec.shape,
        rvec,
    )
    for wait in waits[PIECES:]:
        wait()
    corners = [cmap[0, 0, n] for n in range(cmap.shape[2])]
    across = [fmap[0, 0, order[2], p] for p in range(fmap.shape[3])]
    tiles = (tiles_high, tiles_low)
    offer(pair, corners, across, rvec, rows, tiles, left, base, payload)
    cmap_out[...] = cmap_row[0]
    if pair:
        payload[ncol:, :] = jnp.zeros_like(payload[ncol:, :])
        payload[ncol : ncol + 1, : len(corners)] = cmap_row[0].astype(F32)
        payload[ncol + 1 : ncol + 2, : len(across)] = fmap_rows[
            0, 0, pl.ds(order[2], 1), :
        ].astype(F32)
    for i, face in enumerate(order):
        met[i : i + 1, :] = fmap_rows[0, 0, pl.ds(face, 1), :]
        wmet[i : i + 1, :] = weights[pl.ds(face, 1), :]


def local_kernel(
    pair, cols_in, met, weights, capillary, field, other, stiff, shares, labels, *rest
):
    out, sums, flat, other_flat, *across, left, cols, sems = rest
    nblk, ncol, bdof = field.shape
    (wait,) = fetch([(cols_in, cols)], sems)
    where = listed(met)
    if pair:
        face_across(shares, labels, len(where[2]), field.shape, across[0])
    sums[...] = lanes(field, other)
    flatten(lambda first, last: field[first:last], field.shape, flat)
    flatten(lambda first, last: other[first:last], field.shape, other_flat)
    kept = stiff.shape[2] // bdof
    for b in range(nblk):
        left[b] = stack(field[b])
    wait()
    group = 4
    for t in range(0, nblk, group):
        gathered = [
            jnp.concatenate([left[cols[k, 0, t + j]] for k in range(kept)], axis=1)
            for j in range(group)
        ]
        firsts = [g[:ncol] for g in gathered]
        seconds = [g[ncol:] for g in gathered]
        rows = stiff[t : t + group].reshape(group * bdof, kept * bdof)
        prod = three_pass(dot_t, jnp.concatenate(firsts + seconds, axis=0), *halves(rows))
        for j in range(group):
            out[t + j] = (
                lane_piece(prod[j * ncol : (j + 1) * ncol], j, bdof)
                + capillary[t + j : t + j + 1, :] * field[t + j]
            )
    for i, blocks in enumerate(where):
        row = weights[i : i + 1, :]
        add_pieces(out, blocks, lambda p, b: lane_piece(row, p, bdof) * field[b])


def couple(met, weights, local, besides, out):
    bdof = local.shape[2]
    where = listed(met)
    out[...] = local[...]
    for i, beside in enumerate(besides):
        term = weights[i : i + 1, :] * beside[...]
        add_pieces(out, where[i], lambda p, b: -lane_piece(term, p, bdof))
    return where


def lanes(first, second):
    return jnp.sum(first[...] * second[...], axis=0)


def image_kernel(
    pair, cmap, met, weights, local, zvec, tiles_high, tiles_low, rows, *rest
):
    count = 3 if pair else 4
    besides, (wout, sums, base, payload, left) = rest[:count], rest[count:]
    (corners,) = listed(cmap)
    where = couple(met, weights, local, besides, wout)
    tiles = (tiles_high, tiles_low)
    offer(pair, corners, where[2], wout, rows, tiles, left, base, payload)
    sums[...] = lanes(zvec, wout)


def last_kernel(met, weights, local, rvec, zvec, mvec, gamma, delta, mu, *rest):
    *besides, nout, totals = rest
    rm = lanes(rvec, mvec)
    couple(met, weights, local, besides, nout)
    parts = [gamma[...], delta[...], mu[...], rm, lanes(mvec, nout), lanes(zvec, nout)]
    parts = jnp.concatenate(parts, axis=0)
    sides = lax.dot_general(
        jnp.ones((1, parts.shape[1]), F32),
        parts,
        (((1,), (1,)), ((), ())),
        precision=lax.Precision.HIGHEST,
        preferred_element_type=F32,
    )
    totals[...] = jnp.broadcast_to(sides[None], totals.shape)


def finish_kernel(shares, nvec, rflat, zflat, wflat, mflat, sol_out, res_out, sol, res, sems):
    nblk, ncol, bdof = nvec.shape
    flatten(lambda first, last: nvec[first:last], nvec.shape, res)
    total = jnp.sum(shares[...], axis=0, keepdims=True)
    gamma, delta, mu, rm, nu, zn = [total[:, q * ncol : (q + 1) * ncol] for q in range(6)]
    alpha = gamma / delta
    gnew = gamma - alpha * (delta + rm) + alpha * alpha * mu
    grow = 1.0 + gnew / gamma
    dnew = grow * grow * delta - alpha * grow * (mu + zn) + alpha * alpha * nu
    anew = gnew / dnew
    both, second = [
        jnp.concatenate([x] * (LANES // ncol), axis=1)
        for x in (alpha + anew * grow, anew * alpha)
    ]
    spans = [slice(j * LANES, (j + 1) * LANES) for j in range(sol.shape[1] // LANES)]
    for here in spans:
        sol[:, here] = both * zflat[:, here] - second * mflat[:, here]
    waits = fetch([(sol, sol_out)], sems.at[pl.ds(0, 1)])
    half = nblk // 2
    for i, rows in enumerate((slice(0, half), slice(half, nblk))):
        for here in spans:
            res[rows, here] = (
                rflat[rows, here] - both * wflat[rows, here] + second * res[rows, here]
            )
        waits += fetch([(res.at[rows], res_out.at[rows])], sems.at[pl.ds(i + 1, 1)])
    for wait in waits:
        wait()


def call(kernel, outs, scratch, args, far=(), near=True):
    vmem = pl.BlockSpec(memory_space=pltpu.VMEM)
    hbm = pl.BlockSpec(memory_space=pltpu.HBM)
    far = [pltpu.with_memory_space_constraint(arg, pltpu.HBM) for arg in far]
    return pl.pallas_call(
        kernel,
        out_shape=outs,
        in_specs=[vmem] * len(args) + [hbm] * len(far),
        out_specs=jax.tree.map(lambda _: vmem if near else hbm, outs),
        scratch_shapes=scratch,
        compiler_params=pltpu.CompilerParams(vmem_limit_bytes=VMEM_LIMIT),
    )(*args, *far)


def everywhere(copies):
    return lax.all_to_all(copies, ("dam", "sec"), split_axis=0, concat_axis=0)


def exchange(sends, axis):
    size = lax.axis_size(axis)
    got = []
    for first, send in zip((1, 0), sends):
        pairs = [(i, i + 1) for i in range(first, size - 1, 2)]
        got.append(lax.ppermute(send, axis, pairs + [(j, i) for i, j in pairs]))
    return got


def shards(
    segment_load,
    segment_mask,
    stiffness,
    block_cols,
    capillary,
    dirichlet_blocks,
    face_map,
    face_weight,
    corner_map,
    coarse_inverse,
):
    nblk, bdof = capillary.shape[2:]
    ncol = segment_load.shape[-1] // bdof
    nface = face_map.shape[3]
    ncorner = corner_map.shape[2]
    size = nblk * bdof
    pair = lax.axis_size("sec") == 2
    load, mask = segment_load[0, 0], segment_mask[0, 0]
    cols = jnp.transpose(block_cols[0], (2, 0, 1))
    tang, weights = capillary[0, 0], face_weight[0, 0]
    blocks, rows = dirichlet_blocks[0, 0], coarse_inverse[0]

    def shape(*dims, dtype=F32):
        return jax.ShapeDtypeStruct(dims, dtype)

    def like(array):
        return shape(*array.shape, dtype=array.dtype)

    def hold(array):
        return pltpu.VMEM(array.shape, array.dtype)

    def index(array):
        return pltpu.SMEM(array.shape, array.dtype)

    def sems(count):
        return pltpu.SemaphoreType.DMA((count,))

    field = shape(nblk, ncol, bdof)
    flat = shape(nblk, bdof * ncol)
    face = shape(ncol, nface * bdof)
    group = ncorner * bdof
    tiles = shape(size // group, group, group, dtype=BF16)
    halved = pltpu.VMEM((size // group, 2 * ncol, group), BF16)
    lane = group + nface * bdof if pair else group
    marked = ncol + 8 if pair else ncol

    rvec, base, payload, high, low, cmap, met, weights, rows, cols, tang = call(
        functools.partial(start_kernel, pair),
        (field, field, shape(marked, lane), tiles, tiles)
        + (shape(1, ncorner, dtype=jnp.int32), shape(4, nface, dtype=jnp.int32))
        + tuple(like(a) for a in (weights, rows, cols, tang)),
        [
            hold(load),
            hold(mask),
            hold(blocks),
            index(corner_map),
            hold(corner_map),
            index(face_map),
            hold(face_map),
            hold(weights),
            halved,
            sems(8 + nblk * ncol // LANES + 2 * PIECES),
        ],
        (),
        (load, mask, corner_map, face_map, blocks, rows, cols, weights, tang),
    )

    def finish(base, shares):
        vec, *faces = call(
            functools.partial(end_kernel, pair),
            (field,) + (face,) * (2 if pair else 4),
            [],
            (cmap, met, base, rows, shares),
        )
        return vec, exchange(faces[:2], "dam"), exchange(faces[2:], "sec")

    def local(vec, other, shares, labels):
        part, sums, *rest = call(
            functools.partial(local_kernel, pair),
            (field, shape(ncol, bdof), flat, flat) + ((face,) if pair else ()),
            [pltpu.VMEM((nblk, 2 * ncol, bdof), BF16), index(cols), sems(1)],
            (cols, met, weights, tang, vec, other, stiffness[0, 0], shares, labels),
        )
        return part, sums, *rest[:2], rest[2:]

    shares = labels = lax.all_gather(payload, "sec")
    zvec, besides, beyond = finish(base, shares)
    part, gamma, zflat, rflat, across = local(zvec, rvec, shares, labels)
    wvec, delta, base, payload = call(
        functools.partial(image_kernel, pair),
        (field, shape(ncol, bdof), field, shape(ncol, lane)),
        [halved],
        (cmap, met, weights, part, zvec, high, low, rows, *besides, *beyond, *across),
    )
    shares = lax.all_gather(payload, "sec")
    mvec, besides, beyond = finish(base, shares)
    part, mu, mflat, wflat, across = local(mvec, wvec, shares, labels)
    nvec, totals = call(
        last_kernel,
        (field, shape(lax.axis_size("dam") * lax.axis_size("sec"), 1, 6 * ncol)),
        [],
        (met, weights, part, rvec, zvec, mvec, gamma, delta, mu, *besides, *beyond, *across),
    )
    sol, res = call(
        finish_kernel,
        (flat, flat),
        [hold(flat), hold(flat), sems(3)],
        (everywhere(totals)[:, 0], nvec, rflat, zflat, wflat, mflat),
        (),
        False,
    )
    return sol[None, None], res[None, None]


def solution(mesh):
    placed = (
        P("dam", "sec", None, None),
        P("dam", "sec", None, None),
        P("dam", "sec", None, None, None),
        P("dam", "sec", None, None),
        P("dam", "sec", None, None),
        P("dam", "sec", None, None, None),
        P("dam", "sec", None, None),
        P("dam", "sec", None, None),
        P("dam", "sec", None),
        P("dam", "sec", None),
    )
    return jax.shard_map(
        shards,
        mesh=mesh,
        in_specs=placed,
        out_specs=(P("dam", "sec", None, None), P("dam", "sec", None, None)),
        check_vma=False,
    )
```

```python
import functools

import jax
import jax.numpy as jnp
from jax import lax
from jax.experimental import pallas as pl
from jax.experimental.pallas import tpu as pltpu
from jax.sharding import PartitionSpec as P

F32 = jnp.float32
BF16 = jnp.bfloat16
VMEM_LIMIT = 16 * 1024 * 1024
LANES = 128
PIECES = 4


def halves(x):
    high = x.astype(BF16)
    return high, (x - high.astype(F32)).astype(BF16)


def stack(x):
    return jnp.concatenate(halves(x), axis=0)


def dot_t(a, b):
    return lax.dot_general(a, b, (((1,), (1,)), ((), ())), preferred_element_type=F32)


def dot(a, b):
    return lax.dot_general(a, b, (((1,), (0,)), ((), ())), preferred_element_type=F32)


def three_pass(mul, left, high, low):
    rows = left.shape[0] // 2
    first = mul(left, high)
    return first[:rows] + first[rows:] + mul(left[:rows], low)


def fetch(pairs, sems):
    copies = [
        pltpu.make_async_copy(source, target, sems.at[i])
        for i, (source, target) in enumerate(pairs)
    ]
    for copy in copies:
        copy.start()
    return [copy.wait for copy in copies]


def pieces(source, target, count):
    step = source.shape[0] // count
    return [
        (source.at[i * step : (i + 1) * step], target.at[i * step : (i + 1) * step])
        for i in range(count)
    ]


def face_order(pair):
    near = 1 - lax.axis_index("dam") % 2
    across = 3 - lax.axis_index("sec") % 2
    return [1 - near, near] + ([across, 5 - across] if pair else [5 - across, across])


def listed(index):
    value = index[...]
    return [[value[i, j] for j in range(value.shape[1])] for i in range(value.shape[0])]


def pack(field, where, out, at=0):
    ncol, bdof = field.shape[1:]
    for p, b in enumerate(where):
        out[:ncol, at + p * bdof : at + (p + 1) * bdof] = field[b]


def add_pieces(field, where, piece):
    new = [field[b] + piece(p, b) for p, b in enumerate(where)]
    for b, value in zip(where, new):
        field[b] = value


def lane_piece(x, p, bdof):
    return x[:, p * bdof : (p + 1) * bdof]


def apply_blocks(field, high, low, base):
    nblk, ncol, bdof = field.shape
    group = 4
    for t in range(0, nblk, group):
        parts = [halves(field[t + j]) for j in range(group)]
        left = jnp.concatenate([p[0] for p in parts] + [p[1] for p in parts], axis=0)
        rows = [x[t : t + group].reshape(group * bdof, bdof) for x in (high, low)]
        prod = three_pass(dot_t, left, *rows)
        for j in range(group):
            base[t + j] = lane_piece(prod[j * ncol : (j + 1) * ncol], j, bdof)


def offer(pair, corners, across, field, rows, split, base, payload):
    bdof = field.shape[2]
    if not pair:
        pack(field, corners, payload)
        apply_blocks(field, *split, base)
        return
    wide = len(corners) * bdof
    at = payload.shape[1] - wide
    me = lax.axis_index("sec")
    own = stack(jnp.concatenate([field[b] for b in corners], axis=1))
    mine = pl.multiple_of(me * wide, wide)
    other = pl.multiple_of((1 - me) * wide, wide)
    correct = three_pass(dot_t, own, *halves(rows[:, pl.ds(mine, wide)]))
    payload[: field.shape[1], at:] = three_pass(dot, own, *halves(rows[:, pl.ds(other, wide)]))
    apply_blocks(field, *split, base)
    add_pieces(base, corners, lambda n, b: lane_piece(correct, n, bdof))
    pack(base, across, payload)


def end_kernel(pair, cmap, met, base, rows, shares, zout, *faces):
    nblk, ncol, bdof = base.shape
    (corners,) = listed(cmap)
    where = listed(met)
    wide = len(corners) * bdof
    zout[...] = base[...]
    if pair:
        at = len(where[0]) * bdof
        correct = shares[pl.ds(1 - lax.axis_index("sec"), 1), :ncol, at:][0]
    else:
        correct = 0.0
        for s in range(shares.shape[0]):
            high, low = halves(rows[:, s * wide : (s + 1) * wide])
            correct = correct + three_pass(dot_t, stack(shares[s]), high, low)
    add_pieces(zout, corners, lambda n, b: lane_piece(correct, n, bdof))
    for blocks, out in zip(where, faces):
        pack(zout, blocks, out)


def face_across(shares, labels, nface, shape, out):
    nblk, ncol, bdof = shape
    at = nface * bdof
    me = lax.axis_index("sec")
    names = labels[pl.ds(1 - me, 1), ncol : ncol + 2, : LANES][0]
    for p in range(nface):
        value = shares[pl.ds(1 - me, 1), :ncol, p * bdof : (p + 1) * bdof][0]
        for n in range((shares.shape[2] - at) // bdof):
            here = slice(at + n * bdof, at + (n + 1) * bdof)
            same = jnp.where(names[0, n] == names[1, p], 1.0, 0.0)
            value = value + same * shares[pl.ds(me, 1), :ncol, here][0]
        out[:, p * bdof : (p + 1) * bdof] = value


def swap_groups(x, ncol):
    subs, lanes_at = x.shape[1:]
    sub = lax.broadcasted_iota(jnp.int32, x.shape, 1)
    lane = lax.broadcasted_iota(jnp.int32, x.shape, 2)
    step = 1
    while step < subs:
        move = step * ncol
        low, left = (sub & step) == 0, (lane & move) == 0
        up = pltpu.roll(pltpu.roll(x, subs - step, 1), move, 2)
        down = pltpu.roll(pltpu.roll(x, step, 1), lanes_at - move, 2)
        x = jnp.where(low == left, x, jnp.where(low, up, down))
        step *= 2
    return x


def flatten(part, shape, out):
    nblk, ncol, bdof = shape
    subs = LANES // ncol
    for first in range(0, nblk, subs):
        tall = part(first, first + subs).reshape(LANES, bdof).T
        tall = swap_groups(tall.reshape(bdof // subs, subs, LANES), ncol)
        for j in range(bdof // subs):
            out[first : first + subs, j * LANES : (j + 1) * LANES] = tall[j]


def unflatten(part, shape, out):
    nblk, ncol, bdof = shape
    subs = LANES // ncol
    for first in range(0, nblk, subs):
        parts = [part(first, first + subs, j)[None] for j in range(bdof // subs)]
        tall = swap_groups(jnp.concatenate(parts, axis=0), ncol).reshape(bdof, LANES)
        out[first : first + subs] = tall.T.reshape(subs, ncol, bdof)


def start_kernel(pair, *refs):
    load_in, mask_in, cmap_in, fmap_in, blocks_in, rows_in, cols_in, weights_in, tang_in = refs[:9]
    rvec, base, payload, high, low, cmap_out, met, wmet, rows, cols, tang = refs[9:20]
    load, mask, blocks, cmap, cmap_row, fmap, fmap_rows, weights, sems = refs[20:]
    waits = fetch(
        [
            (mask_in, mask),
            *pieces(load_in, load, load.shape[0] // (LANES // rvec.shape[1])),
            *pieces(blocks_in, blocks, PIECES),
            (cmap_in, cmap),
            (fmap_in, fmap),
            *pieces(rows_in, rows, PIECES),
            (cmap_in, cmap_row),
            (fmap_in, fmap_rows),
            (weights_in, weights),
            (cols_in, cols),
            (tang_in, tang),
        ],
        sems,
    )
    loads = waits[: load.shape[0] // (LANES // rvec.shape[1]) + 1]
    waits = waits[len(loads) :]
    nblk, ncol, bdof = rvec.shape
    order = face_order(pair)
    for wait in loads:
        wait()
    scale = mask[...].astype(F32)
    scale = jnp.concatenate([scale] * (LANES // ncol), axis=1)
    unflatten(
        lambda first, last, j: load[first:last, j * LANES : (j + 1) * LANES]
        * scale[first:last],
        rvec.shape,
        rvec,
    )
    for wait in waits[:PIECES]:
        wait()
    high[...], low[...] = halves(blocks[...])
    for wait in waits[PIECES:]:
        wait()
    corners = [cmap[0, 0, n] for n in range(cmap.shape[2])]
    across = [fmap[0, 0, order[2], p] for p in range(fmap.shape[3])]
    offer(pair, corners, across, rvec, rows, (high, low), base, payload)
    cmap_out[...] = cmap_row[0]
    if pair:
        payload[ncol:, :] = jnp.zeros_like(payload[ncol:, :])
        payload[ncol : ncol + 1, : len(corners)] = cmap_row[0].astype(F32)
        payload[ncol + 1 : ncol + 2, : len(across)] = fmap_rows[
            0, 0, pl.ds(order[2], 1), :
        ].astype(F32)
    for i, face in enumerate(order):
        met[i : i + 1, :] = fmap_rows[0, 0, pl.ds(face, 1), :]
        wmet[i : i + 1, :] = weights[pl.ds(face, 1), :]


def local_kernel(
    pair, cols_in, met, weights, capillary, field, other, stiff, shares, labels, *rest
):
    out, sums, flat, other_flat, *across, left, cols, sems = rest
    nblk, ncol, bdof = field.shape
    (wait,) = fetch([(cols_in, cols)], sems)
    where = listed(met)
    if pair:
        face_across(shares, labels, len(where[2]), field.shape, across[0])
    sums[...] = lanes(field, other)
    flatten(lambda first, last: field[first:last], field.shape, flat)
    flatten(lambda first, last: other[first:last], field.shape, other_flat)
    kept = stiff.shape[2] // bdof
    for b in range(nblk):
        left[b] = stack(field[b])
    wait()
    group = 4
    for t in range(0, nblk, group):
        gathered = [
            jnp.concatenate([left[cols[k, 0, t + j]] for k in range(kept)], axis=1)
            for j in range(group)
        ]
        firsts = [g[:ncol] for g in gathered]
        seconds = [g[ncol:] for g in gathered]
        rows = stiff[t : t + group].reshape(group * bdof, kept * bdof)
        prod = three_pass(dot_t, jnp.concatenate(firsts + seconds, axis=0), *halves(rows))
        for j in range(group):
            out[t + j] = (
                lane_piece(prod[j * ncol : (j + 1) * ncol], j, bdof)
                + capillary[t + j : t + j + 1, :] * field[t + j]
            )
    for i, blocks in enumerate(where):
        row = weights[i : i + 1, :]
        add_pieces(out, blocks, lambda p, b: lane_piece(row, p, bdof) * field[b])


def couple(met, weights, local, besides, out):
    bdof = local.shape[2]
    where = listed(met)
    out[...] = local[...]
    for i, beside in enumerate(besides):
        term = weights[i : i + 1, :] * beside[...]
        add_pieces(out, where[i], lambda p, b: -lane_piece(term, p, bdof))
    return where


def lanes(first, second):
    return jnp.sum(first[...] * second[...], axis=0)


def image_kernel(
    pair, cmap, met, weights, local, zvec, high, low, rows, *rest
):
    count = 3 if pair else 4
    besides, (wout, sums, base, payload) = rest[:count], rest[count:]
    (corners,) = listed(cmap)
    where = couple(met, weights, local, besides, wout)
    offer(pair, corners, where[2], wout, rows, (high, low), base, payload)
    sums[...] = lanes(zvec, wout)


def last_kernel(met, weights, local, rvec, zvec, mvec, gamma, delta, mu, *rest):
    *besides, nout, totals = rest
    rm = lanes(rvec, mvec)
    couple(met, weights, local, besides, nout)
    parts = [gamma[...], delta[...], mu[...], rm, lanes(mvec, nout), lanes(zvec, nout)]
    parts = jnp.concatenate(parts, axis=0)
    sides = lax.dot_general(
        jnp.ones((1, parts.shape[1]), F32),
        parts,
        (((1,), (1,)), ((), ())),
        precision=lax.Precision.HIGHEST,
        preferred_element_type=F32,
    )
    totals[...] = jnp.broadcast_to(sides[None], totals.shape)


def finish_kernel(shares, nvec, rflat, zflat, wflat, mflat, sol, res):
    nblk, ncol, bdof = nvec.shape
    flatten(lambda first, last: nvec[first:last], nvec.shape, res)
    total = jnp.sum(shares[...], axis=0, keepdims=True)
    gamma, delta, mu, rm, nu, zn = [total[:, q * ncol : (q + 1) * ncol] for q in range(6)]
    alpha = gamma / delta
    gnew = gamma - alpha * (delta + rm) + alpha * alpha * mu
    grow = 1.0 + gnew / gamma
    dnew = grow * grow * delta - alpha * grow * (mu + zn) + alpha * alpha * nu
    anew = gnew / dnew
    both, second = [
        jnp.concatenate([x] * (LANES // ncol), axis=1)
        for x in (alpha + anew * grow, anew * alpha)
    ]
    for j in range(sol.shape[1] // LANES):
        here = slice(j * LANES, (j + 1) * LANES)
        sol[:, here] = both * zflat[:, here] - second * mflat[:, here]
        res[:, here] = rflat[:, here] - both * wflat[:, here] + second * res[:, here]


def call(kernel, outs, scratch, args, far=()):
    vmem = pl.BlockSpec(memory_space=pltpu.VMEM)
    hbm = pl.BlockSpec(memory_space=pltpu.HBM)
    far = [pltpu.with_memory_space_constraint(arg, pltpu.HBM) for arg in far]
    return pl.pallas_call(
        kernel,
        out_shape=outs,
        in_specs=[vmem] * len(args) + [hbm] * len(far),
        out_specs=jax.tree.map(lambda _: vmem, outs),
        scratch_shapes=scratch,
        compiler_params=pltpu.CompilerParams(vmem_limit_bytes=VMEM_LIMIT),
    )(*args, *far)


def everywhere(copies):
    return lax.all_to_all(copies, ("dam", "sec"), split_axis=0, concat_axis=0)


def exchange(sends, axis):
    size = lax.axis_size(axis)
    got = []
    for first, send in zip((1, 0), sends):
        pairs = [(i, i + 1) for i in range(first, size - 1, 2)]
        got.append(lax.ppermute(send, axis, pairs + [(j, i) for i, j in pairs]))
    return got


def shards(
    segment_load,
    segment_mask,
    stiffness,
    block_cols,
    capillary,
    dirichlet_blocks,
    face_map,
    face_weight,
    corner_map,
    coarse_inverse,
):
    nblk, bdof = capillary.shape[2:]
    ncol = segment_load.shape[-1] // bdof
    nface = face_map.shape[3]
    ncorner = corner_map.shape[2]
    pair = lax.axis_size("sec") == 2
    load, mask = segment_load[0, 0], segment_mask[0, 0]
    cols = jnp.transpose(block_cols[0], (2, 0, 1))
    tang, weights = capillary[0, 0], face_weight[0, 0]
    blocks, rows = dirichlet_blocks[0, 0], coarse_inverse[0]

    def shape(*dims, dtype=F32):
        return jax.ShapeDtypeStruct(dims, dtype)

    def like(array):
        return shape(*array.shape, dtype=array.dtype)

    def hold(array):
        return pltpu.VMEM(array.shape, array.dtype)

    def index(array):
        return pltpu.SMEM(array.shape, array.dtype)

    def sems(count):
        return pltpu.SemaphoreType.DMA((count,))

    field = shape(nblk, ncol, bdof)
    flat = shape(nblk, bdof * ncol)
    face = shape(ncol, nface * bdof)
    group = ncorner * bdof
    half = shape(nblk, bdof, bdof, dtype=BF16)
    lane = group + nface * bdof if pair else group
    marked = ncol + 8 if pair else ncol

    rvec, base, payload, high, low, cmap, met, weights, rows, cols, tang = call(
        functools.partial(start_kernel, pair),
        (field, field, shape(marked, lane), half, half)
        + (shape(1, ncorner, dtype=jnp.int32), shape(4, nface, dtype=jnp.int32))
        + tuple(like(a) for a in (weights, rows, cols, tang)),
        [
            hold(load),
            hold(mask),
            hold(blocks),
            index(corner_map),
            hold(corner_map),
            index(face_map),
            hold(face_map),
            hold(weights),
            sems(8 + nblk * ncol // LANES + 2 * PIECES),
        ],
        (),
        (load, mask, corner_map, face_map, blocks, rows, cols, weights, tang),
    )

    def finish(base, shares):
        vec, *faces = call(
            functools.partial(end_kernel, pair),
            (field,) + (face,) * (2 if pair else 4),
            [],
            (cmap, met, base, rows, shares),
        )
        return vec, exchange(faces[:2], "dam"), exchange(faces[2:], "sec")

    def local(vec, other, shares, labels):
        part, sums, *rest = call(
            functools.partial(local_kernel, pair),
            (field, shape(ncol, bdof), flat, flat) + ((face,) if pair else ()),
            [pltpu.VMEM((nblk, 2 * ncol, bdof), BF16), index(cols), sems(1)],
            (cols, met, weights, tang, vec, other, stiffness[0, 0], shares, labels),
        )
        return part, sums, *rest[:2], rest[2:]

    shares = labels = lax.all_gather(payload, "sec")
    zvec, besides, beyond = finish(base, shares)
    part, gamma, zflat, rflat, across = local(zvec, rvec, shares, labels)
    wvec, delta, base, payload = call(
        functools.partial(image_kernel, pair),
        (field, shape(ncol, bdof), field, shape(ncol, lane)),
        [],
        (cmap, met, weights, part, zvec, high, low, rows, *besides, *beyond, *across),
    )
    shares = lax.all_gather(payload, "sec")
    mvec, besides, beyond = finish(base, shares)
    part, mu, mflat, wflat, across = local(mvec, wvec, shares, labels)
    nvec, totals = call(
        last_kernel,
        (field, shape(lax.axis_size("dam") * lax.axis_size("sec"), 1, 6 * ncol)),
        [],
        (met, weights, part, rvec, zvec, mvec, gamma, delta, mu, *besides, *beyond, *across),
    )
    sol, res = call(
        finish_kernel,
        (flat, flat),
        [],
        (everywhere(totals)[:, 0], nvec, rflat, zflat, wflat, mflat),
    )
    return sol[None, None], res[None, None]


def solution(mesh):
    placed = (
        P("dam", "sec", None, None),
        P("dam", "sec", None, None),
        P("dam", "sec", None, None, None),
        P("dam", "sec", None, None),
        P("dam", "sec", None, None),
        P("dam", "sec", None, None, None),
        P("dam", "sec", None, None),
        P("dam", "sec", None, None),
        P("dam", "sec", None),
        P("dam", "sec", None),
    )
    return jax.shard_map(
        shards,
        mesh=mesh,
        in_specs=placed,
        out_specs=(P("dam", "sec", None, None), P("dam", "sec", None, None)),
        check_vma=False,
    )
```

```python
import functools

import jax
import jax.numpy as jnp
from jax import lax
from jax.experimental import pallas as pl
from jax.experimental.pallas import tpu as pltpu
from jax.sharding import PartitionSpec as P

F32 = jnp.float32
BF16 = jnp.bfloat16
VMEM_LIMIT = 16 * 1024 * 1024
LANES = 128
PIECES = 4


def halves(x):
    high = x.astype(BF16)
    return high, (x - high.astype(F32)).astype(BF16)


def stack(x):
    return jnp.concatenate(halves(x), axis=0)


def dot_t(a, b):
    return lax.dot_general(a, b, (((1,), (1,)), ((), ())), preferred_element_type=F32)


def dot(a, b):
    return lax.dot_general(a, b, (((1,), (0,)), ((), ())), preferred_element_type=F32)


def three_pass(mul, left, high, low):
    rows = left.shape[0] // 2
    first = mul(left, high)
    return first[:rows] + first[rows:] + mul(left[:rows], low)


def fetch(pairs, sems):
    copies = [
        pltpu.make_async_copy(source, target, sems.at[i])
        for i, (source, target) in enumerate(pairs)
    ]
    for copy in copies:
        copy.start()
    return [copy.wait for copy in copies]


def pieces(source, target, count):
    step = source.shape[0] // count
    return [
        (source.at[i * step : (i + 1) * step], target.at[i * step : (i + 1) * step])
        for i in range(count)
    ]


def face_order(pair):
    near = 1 - lax.axis_index("dam") % 2
    across = 3 - lax.axis_index("sec") % 2
    return [1 - near, near] + ([across, 5 - across] if pair else [5 - across, across])


def listed(index):
    value = index[...]
    return [[value[i, j] for j in range(value.shape[1])] for i in range(value.shape[0])]


def pack(field, where, out, at=0):
    ncol, bdof = field.shape[1:]
    for p, b in enumerate(where):
        out[:ncol, at + p * bdof : at + (p + 1) * bdof] = field[b]


def add_pieces(field, where, piece):
    new = [field[b] + piece(p, b) for p, b in enumerate(where)]
    for b, value in zip(where, new):
        field[b] = value


def lane_piece(x, p, bdof):
    return x[:, p * bdof : (p + 1) * bdof]


def apply_blocks(field, high, low, base):
    nblk, ncol, bdof = field.shape
    group = 4
    for t in range(0, nblk, group):
        parts = [halves(field[t + j]) for j in range(group)]
        left = jnp.concatenate([p[0] for p in parts] + [p[1] for p in parts], axis=0)
        rows = [x[t : t + group].reshape(group * bdof, bdof) for x in (high, low)]
        prod = three_pass(dot_t, left, *rows)
        for j in range(group):
            base[t + j] = lane_piece(prod[j * ncol : (j + 1) * ncol], j, bdof)


def offer(pair, corners, across, field, rows, split, base, payload):
    bdof = field.shape[2]
    if not pair:
        pack(field, corners, payload)
        apply_blocks(field, *split, base)
        return
    wide = len(corners) * bdof
    at = payload.shape[1] - wide
    me = lax.axis_index("sec")
    own = stack(jnp.concatenate([field[b] for b in corners], axis=1))
    mine = pl.multiple_of(me * wide, wide)
    other = pl.multiple_of((1 - me) * wide, wide)
    correct = three_pass(dot_t, own, *halves(rows[:, pl.ds(mine, wide)]))
    payload[: field.shape[1], at:] = three_pass(dot, own, *halves(rows[:, pl.ds(other, wide)]))
    apply_blocks(field, *split, base)
    add_pieces(base, corners, lambda n, b: lane_piece(correct, n, bdof))
    pack(base, across, payload)


def end_kernel(pair, cmap, met, base, rows, shares, zout, *faces):
    nblk, ncol, bdof = base.shape
    (corners,) = listed(cmap)
    where = listed(met)
    wide = len(corners) * bdof
    zout[...] = base[...]
    if pair:
        at = len(where[0]) * bdof
        correct = shares[pl.ds(1 - lax.axis_index("sec"), 1), :ncol, at:][0]
    else:
        correct = 0.0
        for s in range(shares.shape[0]):
            high, low = halves(rows[:, s * wide : (s + 1) * wide])
            correct = correct + three_pass(dot_t, stack(shares[s]), high, low)
    add_pieces(zout, corners, lambda n, b: lane_piece(correct, n, bdof))
    for blocks, out in zip(where, faces):
        pack(zout, blocks, out)


def face_across(shares, labels, nface, shape, out):
    nblk, ncol, bdof = shape
    at = nface * bdof
    me = lax.axis_index("sec")
    names = labels[pl.ds(1 - me, 1), ncol : ncol + 2, : LANES][0]
    for p in range(nface):
        value = shares[pl.ds(1 - me, 1), :ncol, p * bdof : (p + 1) * bdof][0]
        for n in range((shares.shape[2] - at) // bdof):
            here = slice(at + n * bdof, at + (n + 1) * bdof)
            same = jnp.where(names[0, n] == names[1, p], 1.0, 0.0)
            value = value + same * shares[pl.ds(me, 1), :ncol, here][0]
        out[:, p * bdof : (p + 1) * bdof] = value


def swap_groups(x, ncol):
    subs, lanes_at = x.shape[1:]
    sub = lax.broadcasted_iota(jnp.int32, x.shape, 1)
    lane = lax.broadcasted_iota(jnp.int32, x.shape, 2)
    step = 1
    while step < subs:
        move = step * ncol
        low, left = (sub & step) == 0, (lane & move) == 0
        up = pltpu.roll(pltpu.roll(x, subs - step, 1), move, 2)
        down = pltpu.roll(pltpu.roll(x, step, 1), lanes_at - move, 2)
        x = jnp.where(low == left, x, jnp.where(low, up, down))
        step *= 2
    return x


def flatten(part, shape, out):
    nblk, ncol, bdof = shape
    subs = LANES // ncol
    for first in range(0, nblk, subs):
        tall = part(first, first + subs).reshape(LANES, bdof).T
        tall = swap_groups(tall.reshape(bdof // subs, subs, LANES), ncol)
        for j in range(bdof // subs):
            out[first : first + subs, j * LANES : (j + 1) * LANES] = tall[j]


def unflatten(part, shape, out):
    nblk, ncol, bdof = shape
    subs = LANES // ncol
    for first in range(0, nblk, subs):
        parts = [part(first, first + subs, j)[None] for j in range(bdof // subs)]
        tall = swap_groups(jnp.concatenate(parts, axis=0), ncol).reshape(bdof, LANES)
        out[first : first + subs] = tall.T.reshape(subs, ncol, bdof)


def start_kernel(pair, *refs):
    load_in, mask_in, cmap_in, fmap_in, blocks_in, rows_in, cols_in, weights_in, tang_in = refs[:9]
    rvec, base, payload, high, low, cmap_out, met, wmet, rows, cols, tang = refs[9:20]
    load, mask, blocks, cmap, cmap_row, fmap, fmap_rows, weights, sems = refs[20:]
    waits = fetch(
        [
            (mask_in, mask),
            *pieces(load_in, load, load.shape[0] // (LANES // rvec.shape[1])),
            *pieces(blocks_in, blocks, PIECES),
            (cmap_in, cmap),
            (fmap_in, fmap),
            *pieces(rows_in, rows, PIECES),
            (cmap_in, cmap_row),
            (fmap_in, fmap_rows),
            (weights_in, weights),
            (cols_in, cols),
            (tang_in, tang),
        ],
        sems,
    )
    loads = waits[: load.shape[0] // (LANES // rvec.shape[1]) + 1]
    waits = waits[len(loads) :]
    nblk, ncol, bdof = rvec.shape
    order = face_order(pair)
    for wait in loads:
        wait()
    scale = mask[...].astype(F32)
    scale = jnp.concatenate([scale] * (LANES // ncol), axis=1)
    unflatten(
        lambda first, last, j: load[first:last, j * LANES : (j + 1) * LANES]
        * scale[first:last],
        rvec.shape,
        rvec,
    )
    for wait in waits[:PIECES]:
        wait()
    high[...], low[...] = halves(blocks[...])
    for wait in waits[PIECES:]:
        wait()
    corners = [cmap[0, 0, n] for n in range(cmap.shape[2])]
    across = [fmap[0, 0, order[2], p] for p in range(fmap.shape[3])]
    offer(pair, corners, across, rvec, rows, (high, low), base, payload)
    cmap_out[...] = cmap_row[0]
    if pair:
        payload[ncol:, :] = jnp.zeros_like(payload[ncol:, :])
        payload[ncol : ncol + 1, : len(corners)] = cmap_row[0].astype(F32)
        payload[ncol + 1 : ncol + 2, : len(across)] = fmap_rows[
            0, 0, pl.ds(order[2], 1), :
        ].astype(F32)
    for i, face in enumerate(order):
        met[i : i + 1, :] = fmap_rows[0, 0, pl.ds(face, 1), :]
        wmet[i : i + 1, :] = weights[pl.ds(face, 1), :]


def local_kernel(
    pair, cols_in, met, weights, capillary, field, other, stiff, shares, labels, *rest
):
    out, sums, flat, other_flat, *across, left, cols, sems = rest
    nblk, ncol, bdof = field.shape
    (wait,) = fetch([(cols_in, cols)], sems)
    where = listed(met)
    if pair:
        face_across(shares, labels, len(where[2]), field.shape, across[0])
    sums[...] = lanes(field, other)
    flatten(lambda first, last: field[first:last], field.shape, flat)
    flatten(lambda first, last: other[first:last], field.shape, other_flat)
    kept = stiff.shape[2] // bdof
    for b in range(nblk):
        left[b] = stack(field[b])
    wait()
    group = 4
    for t in range(0, nblk, group):
        gathered = [
            jnp.concatenate([left[cols[k, 0, t + j]] for k in range(kept)], axis=1)
            for j in range(group)
        ]
        firsts = [g[:ncol] for g in gathered]
        seconds = [g[ncol:] for g in gathered]
        rows = stiff[t : t + group].reshape(group * bdof, kept * bdof)
        prod = three_pass(dot_t, jnp.concatenate(firsts + seconds, axis=0), *halves(rows))
        for j in range(group):
            out[t + j] = (
                lane_piece(prod[j * ncol : (j + 1) * ncol], j, bdof)
                + capillary[t + j : t + j + 1, :] * field[t + j]
            )
    for i, blocks in enumerate(where):
        row = weights[i : i + 1, :]
        add_pieces(out, blocks, lambda p, b: lane_piece(row, p, bdof) * field[b])
    if pair:
        term = weights[2:3, :] * across[0][...]
        add_pieces(out, where[2], lambda p, b: -lane_piece(term, p, bdof))


def couple(met, weights, local, besides, out):
    bdof = local.shape[2]
    where = listed(met)
    out[...] = local[...]
    for i, beside in enumerate(besides):
        term = weights[i : i + 1, :] * beside[...]
        add_pieces(out, where[i], lambda p, b: -lane_piece(term, p, bdof))
    return where


def lanes(first, second):
    return jnp.sum(first[...] * second[...], axis=0)


def image_kernel(
    pair, cmap, met, weights, local, zvec, high, low, rows, *rest
):
    count = 2 if pair else 4
    besides, (wout, sums, base, payload) = rest[:count], rest[count:]
    (corners,) = listed(cmap)
    where = couple(met, weights, local, besides, wout)
    offer(pair, corners, where[2], wout, rows, (high, low), base, payload)
    sums[...] = lanes(zvec, wout)


def last_kernel(met, weights, local, rvec, zvec, mvec, gamma, delta, mu, *rest):
    *besides, nout, totals = rest
    rm = lanes(rvec, mvec)
    couple(met, weights, local, besides, nout)
    parts = [gamma[...], delta[...], mu[...], rm, lanes(mvec, nout), lanes(zvec, nout)]
    parts = jnp.concatenate(parts, axis=0)
    sides = lax.dot_general(
        jnp.ones((1, parts.shape[1]), F32),
        parts,
        (((1,), (1,)), ((), ())),
        precision=lax.Precision.HIGHEST,
        preferred_element_type=F32,
    )
    totals[...] = jnp.broadcast_to(sides[None], totals.shape)


def finish_kernel(shares, nvec, rflat, zflat, wflat, mflat, sol, res):
    nblk, ncol, bdof = nvec.shape
    flatten(lambda first, last: nvec[first:last], nvec.shape, res)
    total = jnp.sum(shares[...], axis=0, keepdims=True)
    gamma, delta, mu, rm, nu, zn = [total[:, q * ncol : (q + 1) * ncol] for q in range(6)]
    alpha = gamma / delta
    gnew = gamma - alpha * (delta + rm) + alpha * alpha * mu
    grow = 1.0 + gnew / gamma
    dnew = grow * grow * delta - alpha * grow * (mu + zn) + alpha * alpha * nu
    anew = gnew / dnew
    both, second = [
        jnp.concatenate([x] * (LANES // ncol), axis=1)
        for x in (alpha + anew * grow, anew * alpha)
    ]
    for j in range(sol.shape[1] // LANES):
        here = slice(j * LANES, (j + 1) * LANES)
        sol[:, here] = both * zflat[:, here] - second * mflat[:, here]
        res[:, here] = rflat[:, here] - both * wflat[:, here] + second * res[:, here]


def call(kernel, outs, scratch, args, far=()):
    vmem = pl.BlockSpec(memory_space=pltpu.VMEM)
    hbm = pl.BlockSpec(memory_space=pltpu.HBM)
    far = [pltpu.with_memory_space_constraint(arg, pltpu.HBM) for arg in far]
    return pl.pallas_call(
        kernel,
        out_shape=outs,
        in_specs=[vmem] * len(args) + [hbm] * len(far),
        out_specs=jax.tree.map(lambda _: vmem, outs),
        scratch_shapes=scratch,
        compiler_params=pltpu.CompilerParams(vmem_limit_bytes=VMEM_LIMIT),
    )(*args, *far)


def everywhere(copies):
    return lax.all_to_all(copies, ("dam", "sec"), split_axis=0, concat_axis=0)


def exchange(sends, axis):
    size = lax.axis_size(axis)
    got = []
    for first, send in zip((1, 0), sends):
        pairs = [(i, i + 1) for i in range(first, size - 1, 2)]
        got.append(lax.ppermute(send, axis, pairs + [(j, i) for i, j in pairs]))
    return got


def shards(
    segment_load,
    segment_mask,
    stiffness,
    block_cols,
    capillary,
    dirichlet_blocks,
    face_map,
    face_weight,
    corner_map,
    coarse_inverse,
):
    nblk, bdof = capillary.shape[2:]
    ncol = segment_load.shape[-1] // bdof
    nface = face_map.shape[3]
    ncorner = corner_map.shape[2]
    pair = lax.axis_size("sec") == 2
    load, mask = segment_load[0, 0], segment_mask[0, 0]
    cols = jnp.transpose(block_cols[0], (2, 0, 1))
    tang, weights = capillary[0, 0], face_weight[0, 0]
    blocks, rows = dirichlet_blocks[0, 0], coarse_inverse[0]

    def shape(*dims, dtype=F32):
        return jax.ShapeDtypeStruct(dims, dtype)

    def like(array):
        return shape(*array.shape, dtype=array.dtype)

    def hold(array):
        return pltpu.VMEM(array.shape, array.dtype)

    def index(array):
        return pltpu.SMEM(array.shape, array.dtype)

    def sems(count):
        return pltpu.SemaphoreType.DMA((count,))

    field = shape(nblk, ncol, bdof)
    flat = shape(nblk, bdof * ncol)
    face = shape(ncol, nface * bdof)
    group = ncorner * bdof
    half = shape(nblk, bdof, bdof, dtype=BF16)
    lane = group + nface * bdof if pair else group
    marked = ncol + 8 if pair else ncol

    rvec, base, payload, high, low, cmap, met, weights, rows, cols, tang = call(
        functools.partial(start_kernel, pair),
        (field, field, shape(marked, lane), half, half)
        + (shape(1, ncorner, dtype=jnp.int32), shape(4, nface, dtype=jnp.int32))
        + tuple(like(a) for a in (weights, rows, cols, tang)),
        [
            hold(load),
            hold(mask),
            hold(blocks),
            index(corner_map),
            hold(corner_map),
            index(face_map),
            hold(face_map),
            hold(weights),
            sems(8 + nblk * ncol // LANES + 2 * PIECES),
        ],
        (),
        (load, mask, corner_map, face_map, blocks, rows, cols, weights, tang),
    )

    def finish(base, shares):
        vec, *faces = call(
            functools.partial(end_kernel, pair),
            (field,) + (face,) * (2 if pair else 4),
            [],
            (cmap, met, base, rows, shares),
        )
        return vec, exchange(faces[:2], "dam"), exchange(faces[2:], "sec")

    def local(vec, other, shares, labels):
        return call(
            functools.partial(local_kernel, pair),
            (field, shape(ncol, bdof), flat, flat),
            ([hold(face)] if pair else [])
            + [pltpu.VMEM((nblk, 2 * ncol, bdof), BF16), index(cols), sems(1)],
            (cols, met, weights, tang, vec, other, stiffness[0, 0], shares, labels),
        )

    shares = labels = lax.all_gather(payload, "sec")
    zvec, besides, beyond = finish(base, shares)
    part, gamma, zflat, rflat = local(zvec, rvec, shares, labels)
    wvec, delta, base, payload = call(
        functools.partial(image_kernel, pair),
        (field, shape(ncol, bdof), field, shape(ncol, lane)),
        [],
        (cmap, met, weights, part, zvec, high, low, rows, *besides, *beyond),
    )
    shares = lax.all_gather(payload, "sec")
    mvec, besides, beyond = finish(base, shares)
    part, mu, mflat, wflat = local(mvec, wvec, shares, labels)
    nvec, totals = call(
        last_kernel,
        (field, shape(lax.axis_size("dam") * lax.axis_size("sec"), 1, 6 * ncol)),
        [],
        (met, weights, part, rvec, zvec, mvec, gamma, delta, mu, *besides, *beyond),
    )
    sol, res = call(
        finish_kernel,
        (flat, flat),
        [],
        (everywhere(totals)[:, 0], nvec, rflat, zflat, wflat, mflat),
    )
    return sol[None, None], res[None, None]


def solution(mesh):
    placed = (
        P("dam", "sec", None, None),
        P("dam", "sec", None, None),
        P("dam", "sec", None, None, None),
        P("dam", "sec", None, None),
        P("dam", "sec", None, None),
        P("dam", "sec", None, None, None),
        P("dam", "sec", None, None),
        P("dam", "sec", None, None),
        P("dam", "sec", None),
        P("dam", "sec", None),
    )
    return jax.shard_map(
        shards,
        mesh=mesh,
        in_specs=placed,
        out_specs=(P("dam", "sec", None, None), P("dam", "sec", None, None)),
        check_vma=False,
    )
```
